32 devices in a mesh: dp: 16 (over z, y, x), mp: 2 (over core).
Axes of the slice: x: 2, y: 2, z: 4, core: 2. Of those that a mesh axis runs over, the one named last changes fastest.
Arguments:
- layer_input: bfloat16 [16, 512, 512], P('dp'), may hold values from -6 to 6
- memory: bfloat16 [2, 16, 512, 512], P(None, 'dp'), may hold values from -6 to 6
- doc_lengths: int32 [16, 4], P('dp'), may hold values from 1 to 256, 448 in all within a row
- neighbour_owner: int32 [16, 512, 4], P('dp'), may hold values from 0 to 15, all different within a row; in each aligned block of 512 rows (0 to 511, 512 to 1023, ..., all dimensions but the last counted through in order) at most 256 rows name the same one
- neighbour_row: int32 [16, 512, 4], P('dp'), may hold values from 0 to 1023
- table: bfloat16 [16384, 512], P('dp'), may hold values from -6 to 6
- gain_attn: float32 [2, 512], replicated, may hold values from 0.5 to 1.5
- w_query: bfloat16 [2, 512, 512], P(None, None, 'mp'), may hold values from -0.25 to 0.25
- w_key: bfloat16 [2, 512, 512], P(None, None, 'mp'), may hold values from -0.25 to 0.25
- w_value: bfloat16 [2, 512, 512], P(None, None, 'mp'), may hold values from -0.25 to 0.25
- w_out: bfloat16 [2, 512, 512], P(None, 'mp'), may hold values from -1.5 to 1.5
- gain_ffn: float32 [2, 512], replicated, may hold values from 0.5 to 1.5
- w_up: bfloat16 [2, 512, 2048], P(None, None, 'mp'), may hold values from -0.25 to 0.25
- w_down: bfloat16 [2, 2048, 512], P(None, 'mp'), may hold values from -0.125 to 0.125
- w_gate: float32 [512], replicated, may hold values from -0.25 to 0.25
- cotangent: bfloat16 [16, 512, 512], P('dp'), may hold values from -6 to 6
Outputs:
- layer_output: float32 [16, 512, 512], P('dp')
- input_grad: float32 [16, 512, 512], P('dp')
- memory_grad: float32 [2, 16, 512, 512], P(None, 'dp')
- grad_gain_attn: float32 [2, 512], replicated
- grad_w_query: float32 [2, 512, 512], P(None, None, 'mp')
- grad_w_key: float32 [2, 512, 512], P(None, None, 'mp')
- grad_w_value: float32 [2, 512, 512], P(None, None, 'mp')
- grad_w_out: float32 [2, 512, 512], P(None, 'mp')
- grad_gain_ffn: float32 [2, 512], replicated
- grad_w_up: float32 [2, 512, 2048], P(None, None, 'mp')
- grad_w_down: float32 [2, 2048, 512], P(None, 'mp')
- grad_w_gate: float32 [512], replicated
The draws below stay inside these ranges and needn't reach their ends.
Inputs may be any that keep to these rules, and one draw needn't show every extreme that they name: `doc_lengths`: the 4 lengths of a row sum to 448; the longest is 256. `neighbour_owner`: A token's 4 owners differ. Among the tokens of one index of dp, no owner is named by more than 256 tokens, a bound that some block reaches.
All inputs are finite; a program needn't handle non-finite values.
Results may differ from the reference program's by a relative error of at most 0.024.
Values may be sent and summed in bfloat16 or wider, within the bound.
No kernel may reach another device: no remote copies, remote signals or barrier semaphores. Data moves between devices by JAX's collectives and lax.ppermute only.
A program may use at most 192 MiB of HBM per device.

```python
import math
import jax
import jax.numpy as jnp
import numpy as np
from jax import lax

D = 512
HEADS = 8
HD = 64
FF = 2048
K = 4
SEG = 512
MEM = 512
LAYERS = 2
DOCS = 4
ROWS_DEV = 1
TAB_DEV = 1024
ROWS = 16
TABLE = 16384
CAP = 256
FILLED = 448
MOST_DOC = 256
N_DP = 16


def plant(values, rng, smallest, top_value):
    dims = values.shape
    spot = [jax.random.randint(jax.random.fold_in(rng, axis), (), 0, dims[axis]) for axis in range(len(dims))]
    values = values.at[tuple(spot)].set(smallest)
    longest = dims.index(max(dims))
    spot[longest] = (spot[longest] + 1) % dims[longest]
    return values.at[tuple(spot)].set(top_value)


def level_of(stream_key, extent, shards, least, largest):
    loudness = 1.0
    for position, shards_of in shards:
        heights = jax.random.uniform(jax.random.fold_in(jax.random.fold_in(stream_key, 6), position), (shards_of,), jnp.float32, least / len(shards), largest / len(shards))
        loudness = loudness * jnp.repeat(jnp.exp(heights), extent[position] // shards_of).reshape((-1,) + (1,) * (len(extent) - 1 - position))
    return loudness


def profile(number_of, total, limit, lean):
    weights = [(1 << 20) // math.isqrt(standing ** lean) + 1 for standing in range(2, number_of + 1)]
    spare, holding = total - limit - (number_of - 1), [1] * (number_of - 1)
    while spare > 0:
        movable = [i for i in range(number_of - 1) if holding[i] < limit]
        whole, left = sum([weights[i] for i in movable]), spare
        for i in movable:
            extra = min(limit - holding[i], max(1, left * weights[i] // whole), spare)
            holding[i] = holding[i] + extra
            spare = spare - extra
    return np.array([limit] + holding)


def uneven_parts(key, amount, total, reach, skew):
    if amount == 2:
        one = jax.random.randint(key, (), max(1, total - reach), min(reach, total - 1) + 1)
        return jnp.stack([one, total - one])
    sizes = jnp.asarray(profile(amount, total, reach, skew), jnp.int32)
    pairs = (amount - 1) // 2
    giver, sink = sizes[1:1 + 2 * pairs:2], sizes[2:2 + 2 * pairs:2]
    slack = jnp.minimum(giver - 1, reach - sink)
    moved = jax.random.randint(jax.random.fold_in(key, 1), (pairs,), 0, 1 << 20) % (slack + 1)
    sizes = sizes.at[1:1 + 2 * pairs:2].set(giver - moved).at[2:2 + 2 * pairs:2].set(sink + moved)
    return sizes[jax.random.permutation(jax.random.fold_in(key, 2), amount)]


def shared_out(own_key, own, number, rows, amount, top, most, lean):
    sequence = jax.random.permutation(own_key, amount)
    heavy_load, common = load_shares(amount, rows * top, most, lean, True), load_shares(amount, rows * top, most, lean, False)
    places = jnp.arange(amount)

    def named(tallies, rotation):
        used = int((tallies > 0).sum())
        fixed = max(1, used // 4)
        passed = fixed + (places - fixed + rotation * (used - fixed)) % max(1, amount - fixed)
        return jnp.zeros((amount,), jnp.int32).at[sequence[jnp.where(places < fixed, places, passed)]].set(jnp.asarray(tallies, jnp.int32))

    tallies = jnp.where(number % 4 == 0, named(heavy_load, number // 4), named(common, number - number // 4 - 1))
    mixed = jax.random.permutation(jax.random.fold_in(own, 3), amount)
    source_of, receiver = mixed[0:amount // 2 * 2:2], mixed[1:amount // 2 * 2:2]
    room = jnp.minimum(tallies[source_of] - 1, most - tallies[receiver]) // 2
    room = jnp.where((source_of == sequence[0]) | (receiver == sequence[0]) | (tallies[receiver] == 0), 0, jnp.maximum(room, 0))
    passed = jax.random.randint(jax.random.fold_in(own, 4), (amount // 2,), 0, 1 << 20) % (room + 1)
    tallies = tallies.at[source_of].add(-passed).at[receiver].add(passed)
    items = jnp.searchsorted(jnp.cumsum(tallies), jnp.arange(rows * top), side="right").astype(jnp.int32)
    table = items.reshape(top, rows).T
    table = table[jax.random.permutation(jax.random.fold_in(own, 1), rows)]
    rotation = jax.random.randint(jax.random.fold_in(own, 2), (rows, 1), 0, top)
    return jnp.take_along_axis(table, (jnp.arange(top)[None, :] + rotation) % top, axis=1)


def load_shares(amount, total, most, slope, full):
    weights = [(1 << 20) // math.isqrt(grade ** slope) + 1 for grade in range(1, amount + 1)]
    largest = most if full else min(most, max(-(-total // amount), total * weights[0] // sum(weights)))
    least = 1 if total - largest >= amount - 1 else 0
    counts, surplus = [largest] + [least] * (amount - 1), total - largest - least * (amount - 1)
    while surplus > 0:
        candidates = [i for i in range(1, amount) if counts[i] < largest] or [i for i in range(1, amount) if counts[i] < most]
        whole, left = sum([weights[i] for i in candidates]), surplus
        for i in candidates:
            extra = min(most - counts[i], max(1, left * weights[i] // whole), surplus)
            counts[i] = counts[i] + extra
            surplus = surplus - extra
    return np.array(counts)


def normal_values(rng, dims, deviation, limit, pieces=(), held_as=jnp.bfloat16):
    values = jax.random.normal(rng, dims, jnp.float32) * deviation
    if len(pieces) > 0:
        values = level_of(rng, dims, pieces, -0.22, 0.18) * values
    return jnp.clip(values, min=-limit, max=limit).astype(held_as)


def setup_inputs(seed: int = 0) -> dict:
    seeds = jax.random.split(jax.random.key(seed), 17)
    layer_input = normal_values(seeds[0], (ROWS, SEG, D), 1.0, 6.0, ((0, 16),))
    memory = normal_values(seeds[1], (LAYERS, ROWS, MEM, D), 1.0, 6.0, ((1, 16),))
    doc_lengths = jax.vmap(lambda own: uneven_parts(own, DOCS, FILLED, MOST_DOC, 2))(jax.random.split(seeds[2], ROWS)).reshape((ROWS, DOCS)).astype(jnp.int32)
    neighbour_owner_keys = jax.random.split(jax.random.fold_in(seeds[3], 1), ROWS * SEG // (ROWS_DEV * SEG))
    neighbour_owner_turns = jax.random.permutation(jax.random.fold_in(seeds[3], 3), ROWS * SEG // (ROWS_DEV * SEG))
    neighbour_owner = jax.vmap(lambda own, number: shared_out(jax.random.fold_in(seeds[3], 2), own, number, ROWS_DEV * SEG, N_DP, K, CAP, 2))(neighbour_owner_keys, neighbour_owner_turns).reshape((ROWS, SEG, K))
    neighbour_row = plant(jax.random.randint(seeds[4], (ROWS, SEG, K), 0, TAB_DEV), jax.random.fold_in(seeds[4], 1), 0, TAB_DEV - 1).astype(jnp.int32)
    table = normal_values(seeds[5], (TABLE, D), 1.0, 6.0, ((0, 16),))
    gain_attn = jnp.clip(1.0 + 0.1 * jax.random.normal(seeds[6], (LAYERS, D), jnp.float32), 0.5, 1.5)
    w_query = normal_values(seeds[7], (LAYERS, D, HEADS * HD), D ** -0.5, 0.25, ((2, 2),))
    w_key = normal_values(seeds[8], (LAYERS, D, HEADS * HD), D ** -0.5, 0.25, ((2, 2),))
    w_value = normal_values(seeds[9], (LAYERS, D, HEADS * HD), D ** -0.5, 0.25, ((2, 2),))
    w_out = normal_values(seeds[10], (LAYERS, HEADS * HD, D), 16 ** -0.5, 1.5, ((1, 2),))
    gain_ffn = jnp.clip(1.0 + 0.1 * jax.random.normal(seeds[11], (LAYERS, D), jnp.float32), 0.5, 1.5)
    w_up = normal_values(seeds[12], (LAYERS, D, FF), D ** -0.5, 0.25, ((2, 2),))
    w_down = normal_values(seeds[13], (LAYERS, FF, D), FF ** -0.5, 0.125, ((1, 2),))
    w_gate = normal_values(seeds[14], (D,), D ** -0.5, 0.25, (), jnp.float32)
    cotangent = normal_values(seeds[15], (ROWS, SEG, D), 1.0, 6.0, ((0, 16),))
    return {"layer_input": layer_input, "memory": memory, "doc_lengths": doc_lengths, "neighbour_owner": neighbour_owner, "neighbour_row": neighbour_row, "table": table, "gain_attn": gain_attn, "w_query": w_query, "w_key": w_key, "w_value": w_value, "w_out": w_out, "gain_ffn": gain_ffn, "w_up": w_up, "w_down": w_down, "w_gate": w_gate, "cotangent": cotangent}


@jax.custom_vjp
def low(v):
    return lax.optimization_barrier(v.astype(jnp.bfloat16)).astype(jnp.float32)

@jax.custom_vjp
def low_back(v):
    return v

def low_keep(v):
    return (low(v), None)

def low_pass(kept, grad):
    return (grad,)

def back_keep(v):
    return (v, None)

def back_low(kept, grad):
    return (low(grad),)
low.defvjp(low_keep, low_pass)
low_back.defvjp(back_keep, back_low)
norm_eps = 1e-05

def layer_norm(values, gain_vector):
    average = lax.optimization_barrier(jnp.mean(values, axis=-1, keepdims=True))
    centred = values - average
    inverse = lax.rsqrt(lax.optimization_barrier(jnp.mean(centred * centred, axis=-1, keepdims=True)) + norm_eps)
    return centred * inverse * gain_vector

def matmul_high(left, right):
    return jnp.dot(left, right, precision=lax.Precision.HIGHEST)

def document_ids(doc_lengths):
    doc_ends = jnp.cumsum(doc_lengths, axis=-1).astype(jnp.int32)
    places = jnp.arange(SEG, dtype=jnp.int32)
    return lax.optimization_barrier(jnp.sum((places[:, None] >= doc_ends[..., None, :]).astype(jnp.int32), axis=-1)).astype(jnp.int32)

def allowed_keys(doc_ids):
    places = jnp.arange(doc_ids.shape[-1], dtype=jnp.int32)
    with_memory = jnp.broadcast_to((doc_ids == 0)[..., None], doc_ids.shape + (MEM,))
    same_doc = (doc_ids[..., :, None] == doc_ids[..., None, :]) & (places[:, None] >= places[None, :])
    return jnp.concatenate([with_memory, same_doc], axis=-1)

def txl_layer(hidden, memory_rows, allowed, weights):
    gain_attn, w_query, w_key, w_value, w_out, gain_ffn, w_up, w_down = weights
    score_scale = 1.0 / math.sqrt(HD)
    full_rows = jnp.concatenate([memory_rows, hidden], axis=0)
    normed = low(layer_norm(full_rows, gain_attn))
    queries = low(low_back(matmul_high(normed[MEM:], w_query))).reshape(SEG, HEADS, HD)
    key_rows = low(low_back(matmul_high(normed, w_key))).reshape(MEM + SEG, HEADS, HD)
    value_rows = low(low_back(matmul_high(normed, w_value))).reshape(MEM + SEG, HEADS, HD)
    scores = low_back(jnp.einsum('qhd,khd->hqk', queries, key_rows, precision=lax.Precision.HIGHEST) * score_scale)
    scores = jnp.where(allowed[None], scores, -1e+30)
    attn_probs = low(jax.nn.softmax(scores, axis=-1))
    head_mixed = jnp.einsum('hqk,khd->qhd', attn_probs, value_rows, precision=lax.Precision.HIGHEST)
    head_mixed = low(low_back(head_mixed.reshape(SEG, HEADS * HD)))
    middle = hidden + low_back(matmul_high(head_mixed, w_out))
    normed_ffn = low(layer_norm(middle, gain_ffn))
    pre_act = low_back(matmul_high(normed_ffn, w_up))
    act_low = low(jax.nn.gelu(pre_act))
    return middle + low_back(matmul_high(act_low, w_down))

def retrieve(top_rows, gate_vector, neighbours):
    near_score = jnp.einsum('...td,...tkd->...tk', top_rows, neighbours, precision=lax.Precision.HIGHEST) / math.sqrt(D)
    near_weight = jax.nn.softmax(near_score, axis=-1)
    pooled = jnp.einsum('...tk,...tkd->...td', near_weight, neighbours, precision=lax.Precision.HIGHEST)
    gate_value = jax.nn.sigmoid(lax.optimization_barrier(jnp.sum(top_rows * gate_vector, axis=-1, keepdims=True)))
    return top_rows + gate_value * (pooled - top_rows)

def reference(layer_input, memory, doc_lengths, neighbour_owner, neighbour_row, table, gain_attn, w_query, w_key, w_value, w_out, gain_ffn, w_up, w_down, w_gate, cotangent):
    table_index = (neighbour_owner * TAB_DEV + neighbour_row).astype(jnp.int32)
    rows_first = jnp.transpose(memory, (1, 0, 2, 3))

    def forward(input_rows, memory_rows, stacks, gate_vector):

        def one_row(scan_carry, row_item):
            row_input, row_memory, row_lengths, row_index = row_item
            allowed = allowed_keys(document_ids(row_lengths))
            neighbours = jnp.take(table, row_index, axis=0).astype(jnp.float32)
            hidden = row_input
            for layer_index in range(LAYERS):
                hidden = txl_layer(hidden, row_memory[layer_index], allowed, tuple((weight_stack[layer_index] for weight_stack in stacks)))
            return (scan_carry, retrieve(hidden, gate_vector, neighbours))
        scan_carry, outputs = lax.scan(jax.checkpoint(one_row), jnp.zeros((), jnp.float32), (input_rows, memory_rows, doc_lengths, table_index))
        return outputs
    stacks = tuple((weight_array.astype(jnp.float32) for weight_array in (gain_attn, w_query, w_key, w_value, w_out, gain_ffn, w_up, w_down)))
    final_rows, pullback = jax.vjp(forward, layer_input.astype(jnp.float32), rows_first.astype(jnp.float32), stacks, w_gate.astype(jnp.float32))
    grad_input, grad_memory, grad_stacks, grad_gate = pullback(cotangent.astype(jnp.float32))
    return (final_rows, grad_input, jnp.transpose(grad_memory, (1, 0, 2, 3)), grad_stacks[0], grad_stacks[1], grad_stacks[2], grad_stacks[3], grad_stacks[4], grad_stacks[5], grad_stacks[6], grad_stacks[7], grad_gate)
```

```python
import math

import jax
import jax.numpy as jnp
from jax import lax
from jax.sharding import PartitionSpec as P

D = 512
HD = 64
SEG = 512
MEM = 512
LAYERS = 2


norm_eps = 1e-05


def layer_norm(values, gain_vector):
    average = jnp.mean(values, axis=-1, keepdims=True)
    centred = values - average
    inverse = lax.rsqrt(jnp.mean(centred * centred, axis=-1, keepdims=True) + norm_eps)
    return centred * inverse * gain_vector


def document_ids(doc_lengths):
    doc_ends = jnp.cumsum(doc_lengths, axis=-1)
    places = jnp.arange(SEG, dtype=jnp.int32)
    return jnp.sum((places[:, None] >= doc_ends[..., None, :]).astype(jnp.int32), axis=-1)


def allowed_keys(doc_ids):
    places = jnp.arange(doc_ids.shape[-1], dtype=jnp.int32)
    with_memory = jnp.broadcast_to((doc_ids == 0)[..., None], doc_ids.shape + (MEM,))
    same_doc = (doc_ids[..., :, None] == doc_ids[..., None, :]) & (
        places[:, None] >= places[None, :]
    )
    return jnp.concatenate([with_memory, same_doc], axis=-1)


def heads_view(values):
    return values.reshape(values.shape[0], values.shape[1], -1, HD)


def flat_heads(values):
    return values.reshape(values.shape[0], values.shape[1], -1)


def project(normed_low, w_query, w_key, w_value):
    queries = jnp.einsum(
        "rtd,de->rte", normed_low[:, MEM:], w_query, preferred_element_type=jnp.float32
    ).astype(jnp.bfloat16)
    key_rows = jnp.einsum(
        "rtd,de->rte", normed_low, w_key, preferred_element_type=jnp.float32
    ).astype(jnp.bfloat16)
    value_rows = jnp.einsum(
        "rtd,de->rte", normed_low, w_value, preferred_element_type=jnp.float32
    ).astype(jnp.bfloat16)
    return (heads_view(queries), heads_view(key_rows), heads_view(value_rows))


def raw_scores(queries, key_rows, allowed):
    score_scale = 1.0 / math.sqrt(HD)
    scores = (
        jnp.einsum("rqhd,rkhd->rhqk", queries, key_rows, preferred_element_type=jnp.float32)
        * score_scale
    )
    return jnp.where(allowed[:, None], scores, -1e30)


def attend_values(probs_low, value_rows):
    head_mixed = jnp.einsum(
        "rhqk,rkhd->rqhd", probs_low, value_rows, preferred_element_type=jnp.float32
    )
    return flat_heads(head_mixed).astype(jnp.bfloat16)


def other_core(values):
    return lax.ppermute(values, "mp", [(0, 1), (1, 0)])


def across_cores(values):
    return values + other_core(values)


def partner(values, bit):
    size = lax.axis_size("dp")
    return lax.ppermute(values, "dp", [(i, i ^ (1 << bit)) for i in range(size)])


def add_low(left, right):
    return (left.astype(jnp.float32) + right.astype(jnp.float32)).astype(jnp.bfloat16)


def scatter_sum(pieces, order):
    me = lax.axis_index("dp")
    for bit in order:
        half = pieces.shape[0] // 2
        mine = (me >> bit) & 1
        shape = (half,) + pieces.shape[1:]
        sent = lax.dynamic_slice(pieces, ((1 - mine) * half, 0, 0), shape)
        kept = lax.dynamic_slice(pieces, (mine * half, 0, 0), shape)
        pieces = add_low(kept, partner(sent, bit))
    return pieces


def gather_all(pieces, order):
    me = lax.axis_index("dp")
    for bit in reversed(order):
        mine = (me >> bit) & 1
        other = partner(pieces, bit)
        pieces = jnp.concatenate(
            [jnp.where(mine == 0, pieces, other), jnp.where(mine == 0, other, pieces)], axis=0
        )
    return pieces


def sum_rows(values, turned):
    size = lax.axis_size("dp")
    bits = size.bit_length() - 1
    order = list(range(bits))
    if turned:
        order[0], order[1] = order[1], order[0]
    pieces = values.astype(jnp.bfloat16).reshape(size, values.shape[0] // size, values.shape[1])
    return gather_all(scatter_sum(pieces, order), order).reshape(values.shape)


def sum_small(values):
    for bit in range(lax.axis_size("dp").bit_length() - 1):
        values = values + partner(values, bit)
    return values


def sum_level(grads):
    gain_attn, wq, wk, wv, wout, gain_ffn, up, down = grads
    half = wv.shape[0] // 2
    up = sum_rows(up, False).astype(jnp.float32)
    down = sum_rows(down, True).astype(jnp.float32)
    qk = sum_rows(jnp.concatenate([wq, wk], axis=1), False).astype(jnp.float32)
    vo = jnp.concatenate([jnp.concatenate([wv[:half], wv[half:]], axis=1), wout], axis=0)
    vo = sum_rows(vo, True).astype(jnp.float32)
    cols = wq.shape[1]
    wv = jnp.concatenate([vo[:half, :cols], vo[:half, cols:]], axis=0)
    return (gain_attn, qk[:, :cols], qk[:, cols:], wv, vo[half:], gain_ffn, up, down)


def layer_forward(hidden, memory_rows, allowed, weights):
    gain_attn, w_query, w_key, w_value, w_out, gain_ffn, w_up, w_down = weights
    full_rows = jnp.concatenate([memory_rows, hidden], axis=1)
    normed_low = layer_norm(full_rows, gain_attn).astype(jnp.bfloat16)
    queries, key_rows, value_rows = project(normed_low, w_query, w_key, w_value)
    scores = raw_scores(queries, key_rows, allowed)
    top_score = jnp.max(scores, axis=-1, keepdims=True)
    exp_scores = jnp.exp(scores - top_score)
    row_total = jnp.sum(exp_scores, axis=-1, keepdims=True)
    log_total = top_score + jnp.log(row_total)
    head_mixed = attend_values((exp_scores / row_total).astype(jnp.bfloat16), value_rows)
    attn_part = jnp.einsum("rte,ed->rtd", head_mixed, w_out, preferred_element_type=jnp.float32)
    middle = hidden + across_cores(attn_part)
    normed_ffn = layer_norm(middle, gain_ffn).astype(jnp.bfloat16)
    pre_act = jnp.einsum("rtd,df->rtf", normed_ffn, w_up, preferred_element_type=jnp.float32)
    act_low = jax.nn.gelu(pre_act).astype(jnp.bfloat16)
    ffn_part = jnp.einsum("rtf,fd->rtd", act_low, w_down, preferred_element_type=jnp.float32)
    return (middle + across_cores(ffn_part), middle, log_total)


def layer_backward(grad_out, hidden, middle, log_total, memory_rows, allowed, weights):
    gain_attn, w_query, w_key, w_value, w_out, gain_ffn, w_up, w_down = weights
    score_scale = 1.0 / math.sqrt(HD)
    normed_ffn, ffn_norm_back = jax.vjp(layer_norm, middle, gain_ffn)
    ffn_low = normed_ffn.astype(jnp.bfloat16)
    pre_act = jnp.einsum("rtd,df->rtf", ffn_low, w_up, preferred_element_type=jnp.float32)
    act_value, gelu_back = jax.vjp(jax.nn.gelu, pre_act)
    act_low = act_value.astype(jnp.bfloat16)
    grad_low = grad_out.astype(jnp.bfloat16)
    grad_down = jnp.einsum("rtf,rtd->fd", act_low, grad_low, preferred_element_type=jnp.float32)
    grad_act = jnp.einsum("rtd,fd->rtf", grad_low, w_down, preferred_element_type=jnp.float32)
    grad_pre = gelu_back(grad_act)[0].astype(jnp.bfloat16)
    grad_up = jnp.einsum("rtd,rtf->df", ffn_low, grad_pre, preferred_element_type=jnp.float32)
    grad_normed = across_cores(
        jnp.einsum("rtf,df->rtd", grad_pre, w_up, preferred_element_type=jnp.float32)
    )
    grad_middle_norm, grad_gain_ffn = ffn_norm_back(grad_normed)
    grad_middle = grad_out + grad_middle_norm
    full_rows = jnp.concatenate([memory_rows, hidden], axis=1)
    normed_attn, attn_norm_back = jax.vjp(layer_norm, full_rows, gain_attn)
    normed_low = normed_attn.astype(jnp.bfloat16)
    queries, key_rows, value_rows = project(normed_low, w_query, w_key, w_value)
    attn_probs = jnp.exp(raw_scores(queries, key_rows, allowed) - log_total)
    probs_low = attn_probs.astype(jnp.bfloat16)
    head_mixed = attend_values(probs_low, value_rows)
    grad_branch = grad_middle.astype(jnp.bfloat16)
    grad_out_weight = jnp.einsum(
        "rte,rtd->ed", head_mixed, grad_branch, preferred_element_type=jnp.float32
    )
    grad_mixed = heads_view(
        jnp.einsum("rtd,ed->rte", grad_branch, w_out, preferred_element_type=jnp.float32).astype(
            jnp.bfloat16
        )
    )
    grad_probs = jnp.einsum(
        "rqhd,rkhd->rhqk", grad_mixed, value_rows, preferred_element_type=jnp.float32
    )
    grad_value = flat_heads(
        jnp.einsum(
            "rhqk,rqhd->rkhd", probs_low, grad_mixed, preferred_element_type=jnp.float32
        ).astype(jnp.bfloat16)
    )
    row_inner = jnp.sum(attn_probs * grad_probs, axis=-1, keepdims=True)
    grad_scores = (attn_probs * (grad_probs - row_inner)).astype(jnp.bfloat16)
    grad_query = flat_heads(
        (
            jnp.einsum("rhqk,rkhd->rqhd", grad_scores, key_rows, preferred_element_type=jnp.float32)
            * score_scale
        ).astype(jnp.bfloat16)
    )
    grad_key = flat_heads(
        (
            jnp.einsum("rhqk,rqhd->rkhd", grad_scores, queries, preferred_element_type=jnp.float32)
            * score_scale
        ).astype(jnp.bfloat16)
    )
    grad_wq = jnp.einsum(
        "rtd,rte->de", normed_low[:, MEM:], grad_query, preferred_element_type=jnp.float32
    )
    grad_wk = jnp.einsum("rtd,rte->de", normed_low, grad_key, preferred_element_type=jnp.float32)
    grad_wv = jnp.einsum("rtd,rte->de", normed_low, grad_value, preferred_element_type=jnp.float32)
    from_keys = jnp.einsum(
        "rte,de->rtd", grad_key, w_key, preferred_element_type=jnp.float32
    ) + jnp.einsum("rte,de->rtd", grad_value, w_value, preferred_element_type=jnp.float32)
    from_query = jnp.einsum("rte,de->rtd", grad_query, w_query, preferred_element_type=jnp.float32)
    from_query = jnp.concatenate([jnp.zeros_like(from_keys[:, :MEM]), from_query], axis=1)
    grad_normed_attn = across_cores(from_keys + from_query)
    grad_full, grad_gain_attn = attn_norm_back(grad_normed_attn)
    grad_hidden = grad_middle + grad_full[:, MEM:]
    level_grads = (
        grad_gain_attn,
        grad_wq,
        grad_wk,
        grad_wv,
        grad_out_weight,
        grad_gain_ffn,
        grad_up,
        grad_down,
    )
    return (grad_hidden, grad_full[:, :MEM], level_grads)


def fetch_neighbours(neighbour_owner, neighbour_row, table):
    owners = lax.axis_size("dp")
    capacity = max(2, 2 * neighbour_owner.size // owners)
    flat_owner = neighbour_owner.reshape(-1)
    flat_row = neighbour_row.reshape(-1)
    owner_hits = (flat_owner[:, None] == jnp.arange(owners, dtype=jnp.int32)[None, :]).astype(
        jnp.int32
    )
    slot_rank = jnp.sum((jnp.cumsum(owner_hits, axis=0) - owner_hits) * owner_hits, axis=1)
    requests = jnp.zeros((owners, capacity), jnp.int32).at[flat_owner, slot_rank].set(flat_row)
    fetched = lax.all_to_all(
        jnp.take(
            table, lax.all_to_all(requests, "dp", split_axis=0, concat_axis=0, tiled=True), axis=0
        ),
        "dp",
        split_axis=0,
        concat_axis=0,
        tiled=True,
    )
    return fetched[flat_owner, slot_rank].reshape(neighbour_owner.shape + (table.shape[1],))


def retrieve(top_rows, gate_vector, neighbours):
    near_score = jnp.einsum(
        "...td,...tkd->...tk", top_rows, neighbours, precision=lax.Precision.HIGHEST
    ) / math.sqrt(D)
    near_weight = jax.nn.softmax(near_score, axis=-1)
    pooled = jnp.einsum(
        "...tk,...tkd->...td", near_weight, neighbours, precision=lax.Precision.HIGHEST
    )
    gate_value = jax.nn.sigmoid(jnp.sum(top_rows * gate_vector, axis=-1, keepdims=True))
    return top_rows + gate_value * (pooled - top_rows)


def local(
    layer_input,
    memory,
    doc_lengths,
    neighbour_owner,
    neighbour_row,
    table,
    gain_attn,
    w_query,
    w_key,
    w_value,
    w_out,
    gain_ffn,
    w_up,
    w_down,
    w_gate,
    cotangent,
):
    allowed = allowed_keys(document_ids(doc_lengths))
    stacks = (gain_attn, w_query, w_key, w_value, w_out, gain_ffn, w_up, w_down)
    hidden = layer_input.astype(jnp.float32)
    kept_rows = []
    for layer_index in range(LAYERS):
        weights = tuple((weight_stack[layer_index] for weight_stack in stacks))
        next_hidden, middle, log_total = layer_forward(
            hidden, memory[layer_index].astype(jnp.float32), allowed, weights
        )
        kept_rows.append((hidden, middle, log_total))
        hidden = next_hidden
    neighbours = fetch_neighbours(neighbour_owner, neighbour_row, table)
    neighbour_rows = neighbours.astype(jnp.float32)

    def retrieval_step(top_rows, gate_vector):
        return retrieve(top_rows, gate_vector, neighbour_rows)

    final_rows, retrieval_back = jax.vjp(retrieval_step, hidden, w_gate)
    grad_rows, grad_gate = retrieval_back(cotangent.astype(jnp.float32))
    per_level = [None] * LAYERS
    memory_grads = [None] * LAYERS
    for layer_index in range(LAYERS - 1, -1, -1):
        hidden_in, middle, log_total = kept_rows[layer_index]
        weights = tuple((weight_stack[layer_index] for weight_stack in stacks))
        grad_rows, grad_memory, level_grads = layer_backward(
            grad_rows,
            hidden_in,
            middle,
            log_total,
            memory[layer_index].astype(jnp.float32),
            allowed,
            weights,
        )
        memory_grads[layer_index] = grad_memory
        per_level[layer_index] = sum_level(level_grads)
    stacked = tuple((jnp.stack(grad_parts) for grad_parts in zip(*per_level)))
    small = jnp.concatenate([stacked[0], stacked[5], grad_gate[None]], axis=0)
    small = sum_small(small)
    gate_total = small[2 * LAYERS]
    stacked = (small[:LAYERS],) + stacked[1:5] + (small[LAYERS : 2 * LAYERS],) + stacked[6:]
    return (
        final_rows,
        grad_rows,
        jnp.stack(memory_grads),
        stacked[0],
        stacked[1],
        stacked[2],
        stacked[3],
        stacked[4],
        stacked[5],
        stacked[6],
        stacked[7],
        gate_total,
    )


def solution(mesh):
    return jax.shard_map(
        local,
        mesh=mesh,
        in_specs=(
            P("dp", None, None),
            P(None, "dp", None, None),
            P("dp", None),
            P("dp", None, None),
            P("dp", None, None),
            P("dp", None),
            P(),
            P(None, None, "mp"),
            P(None, None, "mp"),
            P(None, None, "mp"),
            P(None, "mp", None),
            P(),
            P(None, None, "mp"),
            P(None, "mp", None),
            P(),
            P("dp", None, None),
        ),
        out_specs=(
            P("dp", None, None),
            P("dp", None, None),
            P(None, "dp", None, None),
            P(),
            P(None, None, "mp"),
            P(None, None, "mp"),
            P(None, None, "mp"),
            P(None, "mp", None),
            P(),
            P(None, None, "mp"),
            P(None, "mp", None),
            P(),
        ),
        check_vma=False,
    )
```

```python
import functools
import math

import jax
import jax.numpy as jnp
from jax import lax
from jax.experimental import pallas as pl
from jax.experimental.pallas import tpu as pltpu
from jax.sharding import PartitionSpec as P

D = 512
HD = 64
SEG = 512
MEM = 512
LAYERS = 2
NEIGHBOURS = 4
HALF = SEG // 2
KEYS_LOW = MEM + HALF
NORM_EPS = 1e-05
MASKED = -1e30
PARTS = 2
SUM_FLOPS = 2_000_000_000
SMALL = 2 * LAYERS + 1
BF16 = jnp.bfloat16
F32 = jnp.float32
HBM, RAW, KEEP = "hbm", "raw", "keep"


def dot(left, right):
    return lax.dot_general(left, right, (((1,), (0,)), ((), ())), preferred_element_type=F32)


def dot_nt(left, right):
    return lax.dot_general(left, right, (((1,), (1,)), ((), ())), preferred_element_type=F32)


def dot_tn(left, right):
    return lax.dot_general(left, right, (((0,), (0,)), ((), ())), preferred_element_type=F32)


class Fetched:
    def __init__(self, source, buffer, semaphore):
        self.buffer = buffer
        self.copy = pltpu.make_async_copy(source, buffer, semaphore)
        self.copy.start()
        self.waiting = True
        self.shape = buffer.shape
        self.dtype = buffer.dtype

    def arrive(self):
        if self.waiting:
            self.copy.wait()
            self.waiting = False

    def __getitem__(self, index):
        self.arrive()
        return self.buffer[index]


class Stored:
    def __init__(self, target, buffer, semaphore):
        self.buffer = buffer
        self.copy = pltpu.make_async_copy(buffer, target, semaphore)
        self.sent = False
        self.shape = buffer.shape
        self.dtype = buffer.dtype

    def __getitem__(self, index):
        return self.buffer[index]

    def __setitem__(self, index, values):
        self.buffer[index] = values

    def send(self):
        self.copy.start()
        self.sent = True


class Slow:
    def __init__(self, array, layer=None):
        self.array = array
        self.layer = layer
        self.shape = array.shape if layer is None else array.shape[1:]
        self.dtype = array.dtype


class Pinned:
    def __init__(self, array):
        self.array = array
        self.shape = array.shape
        self.dtype = array.dtype


class Split:
    def __init__(self, parts):
        self.parts = parts


class Rows:
    def __init__(self, refs):
        self.refs = refs

    def __getitem__(self, index):
        return jnp.concatenate([ref[...] for ref in self.refs], axis=0)


def placed(operand):
    if isinstance(operand, (Slow, Pinned)):
        space = pltpu.HBM if isinstance(operand, Slow) else pltpu.VMEM
        return pltpu.with_memory_space_constraint(operand.array, space)
    return operand


def send(*refs):
    for ref in refs:
        if isinstance(ref, Stored):
            ref.send()


class Vault:
    def __init__(self):
        self.arrays = {}

    def drop(self, *names):
        for name in names:
            del self.arrays[name]


def chain_call(vault, body, name, outs, *operands, adds=None, **options):
    adds = adds or {}
    scalars = len(options.get("scalars", ()))
    names = list(vault.arrays)
    given = sum(len(a.parts) if isinstance(a, Split) else 1 for a in operands)

    def whole(*refs):
        head, rest = refs[: scalars + len(operands)], refs[scalars + len(operands) + len(names) :]
        mine, kept = rest[: len(outs)], rest[len(outs) : len(outs) + len(names) + len(adds)]
        extra = rest[len(outs) + len(names) + len(adds) :]
        body(dict(zip(names + list(adds), kept)), *head, *mine, *extra)

    results = kernel_call(
        whole,
        name,
        list(outs)
        + [(vault.arrays[n].shape, vault.arrays[n].dtype, KEEP) for n in names]
        + [(shape, kind, KEEP) for shape, kind in adds.values()],
        *operands,
        *[Pinned(vault.arrays[n]) for n in names],
        aliases={scalars + given + i: len(outs) + i for i in range(len(names))},
        **options,
    )
    vault.arrays = dict(zip(names + list(adds), results[len(outs) :]))
    return results[: len(outs)]


def kernel_call(body, name, outs, *operands, scratch=(), scalars=(), aliases=None, vmem=4, flops=0):
    arrays, plan = [], []
    for operand in operands:
        parts = operand.parts if isinstance(operand, Split) else [operand]
        plan.append((operand, len(arrays), len(parts)))
        arrays.extend(parts)
    slow = [isinstance(a, Slow) for a in arrays]
    fetched = [s and a.layer != RAW for a, s in zip(arrays, slow)]
    spaces = [out[2] if len(out) > 2 else None for out in outs]
    stored = [space is HBM for space in spaces]
    specs = [pl.BlockSpec(memory_space=pltpu.SMEM)] * len(scalars)
    specs += [pl.BlockSpec(memory_space=pltpu.HBM if s else pltpu.VMEM) for s in slow]
    buffers = [pltpu.VMEM(a.shape, a.dtype) for a, f in zip(arrays, fetched) if f]
    buffers += [pltpu.VMEM(out[0], out[1]) for out, s in zip(outs, stored) if s]
    first = len(scalars)
    middle = first + len(arrays)
    last = middle + len(outs)

    def whole(*refs):
        held, extra = refs[last : last + len(buffers)], refs[last + len(buffers) :]
        semaphores = None
        if buffers:
            semaphores, extra = extra[0], extra[1:]
        count = 0
        ins, results = [], []
        for ref, array, f in zip(refs[first:middle], arrays, fetched):
            if f:
                source = ref if array.layer is None else ref.at[array.layer]
                ref = Fetched(source, held[count], semaphores.at[count])
                count += 1
            ins.append(ref)
        for ref, s in zip(refs[middle:last], stored):
            if s:
                ref = Stored(ref, held[count], semaphores.at[count])
                count += 1
            results.append(ref)
        given = [Rows(ins[at : at + n]) if isinstance(op, Split) else ins[at] for op, at, n in plan]
        body(*refs[:first], *given, *results, *extra)
        for ref in ins:
            if isinstance(ref, Fetched):
                ref.arrive()
        for ref in results:
            if isinstance(ref, Stored) and not ref.sent:
                ref.send()
        for ref in results:
            if isinstance(ref, Stored):
                ref.copy.wait()

    return pl.pallas_call(
        whole,
        out_shape=[
            jax.ShapeDtypeStruct(out[0], out[1])
            if space is None
            else (pltpu.VMEM if space is KEEP else pltpu.HBM)(out[0], out[1])
            for out, space in zip(outs, spaces)
        ],
        in_specs=specs,
        out_specs=[pl.BlockSpec(memory_space=pltpu.HBM if space in (HBM, RAW) else pltpu.VMEM) for space in spaces],
        scratch_shapes=(buffers + [pltpu.SemaphoreType.DMA((len(buffers),))] if buffers else []) + list(scratch),
        input_output_aliases=aliases or {},
        compiler_params=pltpu.CompilerParams(vmem_limit_bytes=vmem * 1024 * 1024),
        cost_estimate=pl.CostEstimate(flops=flops, bytes_accessed=1000, transcendentals=0),
        name=name,
    )(*scalars, *[placed(a) for a in arrays])


def norm_parts(values):
    average = jnp.mean(values, axis=-1, keepdims=True)
    centred = values - average
    inverse = lax.rsqrt(jnp.mean(centred * centred, axis=-1, keepdims=True) + NORM_EPS)
    return centred * inverse, inverse


def norm_backward(values, gain, grad):
    unit, inverse = norm_parts(values)
    scaled = grad * gain
    inner = jnp.mean(scaled * unit, axis=-1, keepdims=True)
    moved = inverse * (scaled - jnp.mean(scaled, axis=-1, keepdims=True) - unit * inner)
    return moved, jnp.sum(grad * unit, axis=0, keepdims=True)


def heads_stacked(values, first):
    rows = values[first : first + HALF]
    lanes = lax.broadcasted_iota(jnp.int32, rows.shape, 1) // HD
    heads = values.shape[1] // HD
    return jnp.concatenate(
        [jnp.where(lanes == h, rows, jnp.zeros_like(rows)) for h in range(heads)], axis=0
    )


def document_starts(lens_ref, first, heads):
    places = first + lax.broadcasted_iota(jnp.int32, (1, heads * HALF), 1) % HALF
    starts = jnp.zeros_like(places)
    end = 0
    for slot in range(lens_ref.shape[1]):
        end = end + lens_ref[0, slot]
        starts = jnp.where(places >= end, end, starts)
    return places, starts


def load_body(sources, v, *refs):
    semaphores = refs[-1]
    copies = []
    for i, (name, which, layer) in enumerate(sources):
        source = refs[which] if layer is None else refs[which].at[layer]
        copies.append(pltpu.make_async_copy(source, v[name], semaphores.at[i]))
        copies[-1].start()
    for copy in copies:
        copy.wait()


def load(vault, arrays, sources):
    adds = {}
    for name, which, layer in sources:
        shape = arrays[which].shape
        adds[name] = (shape if layer is None else shape[1:], arrays[which].dtype)
    chain_call(
        vault,
        functools.partial(load_body, sources),
        "load_weights",
        [],
        *[Slow(a, RAW) for a in arrays],
        adds=adds,
        scratch=[pltpu.SemaphoreType.DMA((len(sources),))],
    )


def attention_forward_body(layer, v, *refs):
    nm_ref, q_ref, k_ref, v_ref = v["nm", layer], v["q", layer], v["k", layer], v["v", layer]
    p_ref, linv_ref, mt_ref = v["p", layer], v["linv", layer], v["mt", layer]
    mem_ref = v["memory", layer]
    wq_ref, wk_ref, wv_ref, wo_ref = (v[n, layer] for n in ("query", "key", "value", "out"))
    if layer == 0:
        lens, gain_ref, part_ref, s_ref = refs
        hidden = v["x"][...].astype(F32)
    else:
        lens, own_ref, other_ref, gain_ref, part_ref, s_ref = refs
        hidden = v["middle", layer - 1][...] + (own_ref[...].astype(F32) + other_ref[...].astype(F32))
        v["hidden", layer][...] = hidden
    gain = gain_ref[layer : layer + 1]
    nm_ref[MEM:] = (norm_parts(hidden)[0] * gain).astype(BF16)
    nm_ref[:MEM] = (norm_parts(mem_ref[...].astype(F32))[0] * gain).astype(BF16)
    q_ref[...] = (dot(nm_ref[MEM:], wq_ref[...]).astype(BF16).astype(F32) * (1.0 / math.sqrt(HD))).astype(BF16)
    k_ref[...] = dot(nm_ref[...], wk_ref[...]).astype(BF16)
    value_rows = dot(nm_ref[...], wv_ref[...])
    v_ref[...] = value_rows.astype(BF16)
    value_turned = jnp.transpose(value_rows).astype(BF16)
    heads = q_ref.shape[1] // HD
    queries = q_ref[...]
    for block in range(2):
        places, starts = document_starts(lens, block * HALF, heads)
        stacked = heads_stacked(queries, block * HALF)
        first_key = 0 if block == 0 else MEM
        rows = KEYS_LOW if block == 0 else SEG
        top = None
        for chunk in range(rows // HALF):
            key = first_key + chunk * HALF
            scores = dot_nt(k_ref[key : key + HALF], stacked)
            if key < MEM:
                scores = scores + jnp.where(starts == 0, 0.0, MASKED)
            else:
                spots = key - MEM + lax.broadcasted_iota(jnp.int32, scores.shape, 0)
                seen = spots >= starts
                if key - MEM == block * HALF:
                    seen = seen & (spots <= places)
                scores = jnp.where(seen, scores, MASKED)
            s_ref[chunk * HALF : (chunk + 1) * HALF] = scores
            peak = jnp.max(scores, axis=0, keepdims=True)
            top = peak if top is None else jnp.maximum(top, peak)
        total = None
        first_row = 0 if block == 0 else KEYS_LOW
        for chunk in range(rows // HALF):
            weight = jnp.exp(s_ref[chunk * HALF : (chunk + 1) * HALF] - top)
            part = jnp.sum(weight, axis=0, keepdims=True)
            total = part if total is None else total + part
            p_ref[first_row + chunk * HALF : first_row + (chunk + 1) * HALF] = weight.astype(BF16)
        inverse = 1.0 / total
        linv_ref[block : block + 1] = inverse
        for h in range(heads):
            mixed = dot(
                value_turned[h * HD : (h + 1) * HD, first_key : first_key + rows],
                p_ref[first_row : first_row + rows, h * HALF : (h + 1) * HALF],
            )
            mt_ref[h * HD : (h + 1) * HD, block * HALF : (block + 1) * HALF] = (
                mixed * inverse[:, h * HALF : (h + 1) * HALF]
            ).astype(BF16)
    part_ref[...] = dot_tn(mt_ref[...], wo_ref[...]).astype(part_ref.dtype)


def attention_forward(vault, layer, lens, parts, gain):
    width = vault.arrays["query", layer].shape[1]
    heads = width // HD
    adds = {
        ("nm", layer): ((MEM + SEG, D), BF16),
        ("q", layer): ((SEG, width), BF16),
        ("k", layer): ((MEM + SEG, width), BF16),
        ("v", layer): ((MEM + SEG, width), BF16),
        ("p", layer): ((KEYS_LOW + SEG, heads * HALF), BF16),
        ("linv", layer): ((2, heads * HALF), F32),
        ("mt", layer): ((width, SEG), BF16),
    }
    if layer > 0:
        adds["hidden", layer] = ((SEG, D), F32)
    return chain_call(
        vault,
        functools.partial(attention_forward_body, layer),
        f"attention_forward_{layer}",
        [((SEG, D), BF16)],
        *parts,
        gain,
        adds=adds,
        scalars=(lens,),
        scratch=[pltpu.VMEM((KEYS_LOW, heads * HALF), F32)],
        vmem=6,
    )[0]


GELU_INNER = math.sqrt(2.0 / math.pi)
GELU_CUBE = 0.044715


def ffn_forward_body(layer, v, own_ref, other_ref, gain_ref, part_ref):
    x_ref = v["x"] if layer == 0 else v["hidden", layer]
    nf_ref, act_ref, slope_ref = v["nf", layer], v["act", layer], v["slope", layer]
    middle = x_ref[...].astype(F32) + (own_ref[...].astype(F32) + other_ref[...].astype(F32))
    v["middle", layer][...] = middle
    nf_ref[...] = (norm_parts(middle)[0] * gain_ref[layer : layer + 1]).astype(BF16)
    step = 128
    for row in range(0, SEG, step):
        rows = pl.ds(row, step)
        pre = dot(nf_ref[rows], v["up", layer][...])
        square = pre * pre
        bend = jnp.tanh(GELU_INNER * pre * (1.0 + GELU_CUBE * square))
        half = 0.5 * (1.0 + bend)
        act = (pre * half).astype(BF16)
        act_ref[rows] = act
        slope_ref[rows] = (
            half
            + (0.5 * GELU_INNER) * pre * (1.0 - bend * bend) * (1.0 + (3.0 * GELU_CUBE) * square)
        ).astype(BF16)
        part_ref[rows] = dot(act, v["down", layer][...]).astype(part_ref.dtype)


def ffn_forward(vault, layer, own, other, gain):
    units = vault.arrays["up", layer].shape[1]
    return chain_call(
        vault,
        functools.partial(ffn_forward_body, layer),
        f"ffn_forward_{layer}",
        [((SEG, D), BF16)],
        own,
        other,
        gain,
        adds={
            ("middle", layer): ((SEG, D), F32),
            ("nf", layer): ((SEG, D), BF16),
            ("act", layer): ((SEG, units), BF16),
            ("slope", layer): ((SEG, units), BF16),
        },
        vmem=3,
    )[0]


def requests_body(owners, turned, where_ref, owner_ref, row_ref, asked_ref, ranks_ref):
    half = owners // 2
    capacity = asked_ref.shape[2] // 2
    lanes, tokens = ranks_ref.shape[1], ranks_ref.shape[0]
    me = where_ref[0]
    names = owner_ref[...] ^ (me & half)
    spots = lax.broadcasted_iota(jnp.int32, (lanes, tokens), 0)
    hits = jnp.zeros((lanes, tokens), F32)
    for k in range(NEIGHBOURS):
        hits = hits + (names[k : k + 1] == spots).astype(F32)
    above = (
        lax.broadcasted_iota(jnp.int32, (tokens, tokens), 0)
        < lax.broadcasted_iota(jnp.int32, (tokens, tokens), 1)
    )
    ranks = dot(hits.astype(BF16), above.astype(F32).astype(BF16))
    slots = lax.broadcasted_iota(jnp.int32, (capacity, tokens), 0).astype(F32)
    high = jnp.zeros((lanes, capacity), F32)
    low = jnp.zeros((lanes, capacity), F32)
    kept = jnp.full((lanes, tokens), -1.0, F32)
    order = names ^ (me & (half - 1)) if turned else names
    for k in range(NEIGHBOURS):
        named = names[k : k + 1] == spots
        rank = jnp.sum(jnp.where(named, ranks, 0.0), axis=0, keepdims=True)
        kept = jnp.where(order[k : k + 1] == spots, rank, kept)
        taken = (slots == rank).astype(F32).astype(BF16)
        row = row_ref[k : k + 1]
        upper = row // 32
        high = high + dot_nt(jnp.where(named, upper.astype(F32), 0.0).astype(BF16), taken)
        low = low + dot_nt(jnp.where(named, (row - upper * 32).astype(F32), 0.0).astype(BF16), taken)
    ranks_ref[...] = jnp.transpose(kept).astype(BF16)
    asked = (high * 32.0 + low).astype(jnp.int32)
    asked_ref[:, 0, :capacity] = asked[:half]
    asked_ref[:, 0, capacity:] = asked[half : 2 * half]


def own_columns_body(where_ref, table_ref, out_ref, semaphore):
    columns = out_ref.shape[1]
    at = pl.ds(pl.multiple_of(where_ref[1] * columns, columns), columns)
    copy = pltpu.make_async_copy(table_ref.at[:, at], out_ref, semaphore)
    copy.start()
    copy.wait()


def own_columns(where, table):
    return kernel_call(
        own_columns_body,
        "own_columns",
        [((table.shape[0], table.shape[1] // 2), BF16)],
        Slow(table, RAW),
        scalars=(where,),
        scratch=[pltpu.SemaphoreType.DMA],
    )[0]


def build_requests(where, neighbour_owner, neighbour_row, owners, turned):
    tokens = neighbour_owner.shape[1]
    capacity = 2 * NEIGHBOURS * tokens // owners
    lanes = -(-owners // 128) * 128
    return kernel_call(
        functools.partial(requests_body, owners, turned),
        "build_requests",
        [((owners // 2, 1, 2 * capacity), jnp.int32), ((tokens, lanes), BF16, HBM)],
        Slow(neighbour_owner),
        Slow(neighbour_row),
        scalars=(where,),
        vmem=4,
    )


def answer_body(turned, where_ref, asked_ref, near_ref, far_ref, *outs):
    blocks, _, width = asked_ref.shape
    capacity = width // 2
    asked = jnp.transpose(asked_ref[:, 0, :].astype(F32))
    spots = lax.broadcasted_iota(jnp.int32, (capacity, near_ref.shape[0]), 1).astype(F32)
    columns = lax.broadcasted_iota(jnp.int32, asked.shape, 1)
    for block in range(blocks):
        if turned:
            source = block ^ (where_ref[0] & (blocks - 1))
            column = jnp.sum(jnp.where(columns == source, asked, 0.0), axis=1, keepdims=True)
        else:
            column = asked[:, block : block + 1]
        for side, table_ref in ((0, near_ref), (1, far_ref)):
            rows = slice(side * capacity, (side + 1) * capacity)
            picked = (column[rows] == spots).astype(F32).astype(BF16)
            found = dot(picked, table_ref[...]).astype(BF16)
            if turned:
                outs[block][rows] = found
            else:
                outs[0][block, rows] = found


def answer_requests(where, asked, near, far, turned):
    blocks, _, width = asked.shape
    shape = (width, near.shape[1])
    return kernel_call(
        functools.partial(answer_body, turned),
        "answer_requests",
        [(shape, BF16)] * blocks if turned else [((blocks,) + shape, BF16)],
        asked,
        near,
        far,
        scalars=(where,),
        vmem=16,
    )


def retrieval_body(
    capacity, v,
    where_ref, own_ref, other_ref, gate_ref, ranks_ref, *refs
):
    count = (len(refs) - 7) // 2
    near_own, near_other = refs[:count], refs[count : 2 * count]
    final_ref, grad_ref, gate_grad_ref, s_ref, g_ref, w_ref, h_ref = refs[2 * count :]
    core = where_ref[1]
    mid_ref, cot_ref = v["middle", LAYERS - 1], v["cot"]
    rows = pl.ds(pl.multiple_of(core * HALF, HALF), HALF)
    own_cols = pl.ds(pl.multiple_of(core * HALF, HALF), HALF)
    other_cols = pl.ds(pl.multiple_of((1 - core) * HALF, HALF), HALF)
    hidden = mid_ref[rows, :] + (own_ref[rows, :].astype(F32) + other_ref[rows, :].astype(F32))
    h_ref[...] = hidden
    h_own, h_other = h_ref[:, own_cols].astype(BF16), h_ref[:, other_cols].astype(BF16)
    cot = cot_ref[rows, :].astype(F32)
    c_own, c_other = cot_ref[rows, own_cols], cot_ref[rows, other_cols]
    ranks = ranks_ref[rows, :]
    per = near_own[0].shape[0]
    slots = count * per
    step = 512
    owners = slots // capacity
    span = 2 * capacity

    def table_rows(first):
        at = pl.ds(first % per, step)
        return near_own[first // per][at], near_other[first // per][at]

    top = jnp.full((HALF, 1), MASKED, F32)
    scale = 1.0 / math.sqrt(D)
    owner_lane = lax.broadcasted_iota(jnp.int32, (ranks.shape[1], step), 0)
    slot_lane = lax.broadcasted_iota(jnp.int32, (ranks.shape[1], step), 1)
    slot_rank = (lax.broadcasted_iota(jnp.int32, (HALF, step), 1) % capacity).astype(F32)
    for first in range(0, slots, step):
        place_of = slot_lane + first
        named = place_of // span + (place_of % span) // capacity * (owners // 2)
        spread = (named == owner_lane).astype(F32).astype(BF16)
        taken = dot(ranks, spread) == slot_rank
        rows_own, rows_other = table_rows(first)
        scores = (dot_nt(h_own, rows_own) + dot_nt(h_other, rows_other)) * scale
        scores = jnp.where(taken, scores, MASKED)
        top = jnp.maximum(top, jnp.max(scores, axis=1, keepdims=True))
        s_ref[:, first : first + step] = scores
        g_ref[:, first : first + step] = dot_nt(c_own, rows_own) + dot_nt(c_other, rows_other)
    total = jnp.zeros((HALF, 1), F32)
    inner = jnp.zeros((HALF, 1), F32)
    for first in range(0, slots, step):
        weight = jnp.exp(s_ref[:, first : first + step] - top)
        s_ref[:, first : first + step] = weight
        total = total + jnp.sum(weight, axis=1, keepdims=True)
        inner = inner + jnp.sum(weight * g_ref[:, first : first + step], axis=1, keepdims=True)
    inverse = 1.0 / total
    inner = inner * inverse
    gate = jax.nn.sigmoid(jnp.sum(hidden * gate_ref[...], axis=1, keepdims=True))
    pool_own = jnp.zeros((HALF, HALF), F32)
    pool_other = jnp.zeros((HALF, HALF), F32)
    back_own = jnp.zeros((HALF, HALF), F32)
    back_other = jnp.zeros((HALF, HALF), F32)
    for first in range(0, slots, step):
        weight = s_ref[:, first : first + step] * inverse
        slope = (weight * ((g_ref[:, first : first + step] - inner) * (gate * scale))).astype(BF16)
        weight = weight.astype(BF16)
        rows_own, rows_other = table_rows(first)
        pool_own += dot(weight, rows_own)
        pool_other += dot(weight, rows_other)
        back_own += dot(slope, rows_own)
        back_other += dot(slope, rows_other)
    w_ref[:, own_cols] = pool_own
    w_ref[:, other_cols] = pool_other
    away = w_ref[...] - hidden
    final_ref[...] = hidden + gate * away
    gate_grad = gate * (1.0 - gate) * jnp.sum(cot * away, axis=1, keepdims=True)
    gate_grad_ref[...] = jnp.sum(gate_grad * hidden, axis=0, keepdims=True)
    w_ref[:, own_cols] = back_own
    w_ref[:, other_cols] = back_other
    grad_ref[...] = (1.0 - gate) * cot + gate_grad * gate_ref[...] + w_ref[...]


def retrieval(vault, where, own, other, w_gate, ranks, near_own, near_other, capacity):
    slots = len(near_own) * near_own[0].shape[0]
    return chain_call(
        vault,
        functools.partial(retrieval_body, capacity),
        "retrieval",
        [((HALF, D), F32), ((HALF, D), F32), ((1, D), F32)],
        own,
        other,
        w_gate,
        ranks,
        *near_own,
        *near_other,
        scalars=(where,),
        scratch=[
            pltpu.VMEM((HALF, slots), F32),
            pltpu.VMEM((HALF, slots), F32),
            pltpu.VMEM((HALF, D), F32),
            pltpu.VMEM((HALF, D), F32),
        ],
        vmem=13,
    )


def ffn_backward_body(layer, v, *refs):
    grad_ref, low_ref, dpre_ref = v["grad", layer], v["low", layer], v["dpre", layer]
    if layer == LAYERS - 1:
        where_ref, own_ref, other_ref = refs[:3]
        parts = refs[3:]
        core = where_ref[1]
        grad_ref[pl.ds(pl.multiple_of(core * HALF, HALF), HALF), :] = own_ref[...]
        grad_ref[pl.ds(pl.multiple_of((1 - core) * HALF, HALF), HALF), :] = other_ref[...]
        grad = grad_ref[...]
    else:
        own_ref, other_ref, gain_ref, gain_grad_ref = refs[:4]
        parts = refs[4:]
        incoming = own_ref[...].astype(F32) + other_ref[...].astype(F32)
        moved, gain_grad_ref[...] = norm_backward(v["hidden", layer + 1][...], gain_ref[layer + 1 : layer + 2], incoming)
        grad = v["mid_grad", layer + 1][...] + moved
        grad_ref[...] = grad
    low_ref[...] = grad.astype(BF16)
    step = SEG // PARTS
    for part_ref, row in zip(parts, range(0, SEG, step)):
        rows = pl.ds(row, step)
        dact = dot_nt(low_ref[rows], v["down", layer][...])
        dpre = (v["slope", layer][rows].astype(F32) * dact).astype(BF16)
        dpre_ref[rows] = dpre
        part_ref[...] = dot_nt(dpre, v["up", layer][...]).astype(part_ref.dtype)


def ffn_backward(vault, layer, scalars, incoming):
    units = vault.arrays["up", layer].shape[1]
    outs = [((SEG // PARTS, D), BF16)] * PARTS
    if layer < LAYERS - 1:
        outs = [((1, D), F32)] + outs
    return chain_call(
        vault,
        functools.partial(ffn_backward_body, layer),
        f"ffn_backward_{layer}",
        outs,
        *incoming,
        adds={
            ("grad", layer): ((SEG, D), F32),
            ("low", layer): ((SEG, D), BF16),
            ("dpre", layer): ((SEG, units), BF16),
        },
        scalars=scalars,
        vmem=3,
    )


def halves_of(v, layer, place, orders, where_ref):
    mine = (where_ref[0] >> orders[place][0]) & 1
    return ((v[f"sent{place}", layer], 1 - mine), (v[f"kept{place}", layer], mine))


def ffn_weights_body(layer, orders, v, where_ref):
    nf_ref, dpre_ref, act_ref, low_ref = (v[n, layer] for n in ("nf", "dpre", "act", "low"))
    rows = D // 2
    for place in range(2):
        for out, half in halves_of(v, layer, place, orders, where_ref):
            if place == 0:
                left = nf_ref[:, pl.ds(pl.multiple_of(half * rows, rows), rows)]
                grads = dot_tn(left, dpre_ref[...]).astype(BF16)
                for j in range(2):
                    out[j] = grads[:, j * D : (j + 1) * D]
            else:
                for j in range(2):
                    left = act_ref[:, pl.ds(pl.multiple_of(j * D + half * rows, rows), rows)]
                    out[j] = dot_tn(left, low_ref[...]).astype(BF16)


def ffn_weights(vault, layer, where, orders):
    assert vault.arrays["act", layer].shape[1] == 2 * D
    shape = ((3, D // 2, D), BF16)
    chain_call(
        vault,
        functools.partial(ffn_weights_body, layer, orders),
        f"ffn_weights_{layer}",
        [],
        adds={(f"{n}{i}", layer): shape for i in range(2) for n in ("sent", "kept")},
        scalars=(where,),
        vmem=3,
    )


def attention_backward_body(
    layer, v, own_ref, other_ref, gain_ref, gain_grad_ref, *refs
):
    parts, (ds_ref, dkey_ref, dval_ref, dqt_ref) = refs[:PARTS], refs[PARTS:]
    grad_ref, mid_ref = v["grad", layer], v["middle", layer]
    wo_ref, wq_ref, wk_ref, wv_ref = (v[n, layer] for n in ("out", "query", "key", "value"))
    q_ref, k_ref, v_ref, p_ref, linv_ref = (v[n, layer] for n in ("q", "k", "v", "p", "linv"))
    mid_grad_ref, low_ref = v["mid_grad", layer], v["low_attn", layer]
    dq_ref, dk_ref, dv_ref = (v[n, layer] for n in ("dq", "dk", "dv"))
    incoming = own_ref[...].astype(F32) + other_ref[...].astype(F32)
    moved, gain_grad_ref[...] = norm_backward(mid_ref[...], gain_ref[layer : layer + 1], incoming)
    mid_grad = grad_ref[...] + moved
    mid_grad_ref[...] = mid_grad
    low_ref[...] = mid_grad.astype(BF16)
    heads = q_ref.shape[1] // HD
    mixed_turned = dot_nt(wo_ref[...], low_ref[...])
    spread = []
    for h in range(heads):
        spread.append(
            mixed_turned[h * HD : (h + 1) * HD]
            * jnp.concatenate(
                [linv_ref[b : b + 1, h * HALF : (h + 1) * HALF] for b in range(2)], axis=1
            )
        )
    dmixed = jnp.transpose(jnp.concatenate(spread, axis=0)).astype(BF16)
    queries = q_ref[...]
    key_turned = jnp.transpose(k_ref[...].astype(F32)).astype(BF16)
    for block in range(2):
        grads = heads_stacked(dmixed, block * HALF)
        stacked = heads_stacked(queries, block * HALF)
        first_key = 0 if block == 0 else MEM
        rows = KEYS_LOW if block == 0 else SEG
        first_row = 0 if block == 0 else KEYS_LOW
        inner = None
        dprobs = []
        for chunk in range(rows // HALF):
            key = first_key + chunk * HALF
            row = first_row + chunk * HALF
            dprob = dot_nt(v_ref[key : key + HALF], grads)
            dprobs.append(dprob)
            part = jnp.sum(p_ref[row : row + HALF].astype(F32) * dprob, axis=0, keepdims=True)
            inner = part if inner is None else inner + part
        inner = inner * linv_ref[block : block + 1]
        for chunk in range(rows // HALF):
            key = first_key + chunk * HALF
            row = first_row + chunk * HALF
            prob = p_ref[row : row + HALF]
            dscore = (prob.astype(F32) * (dprobs[chunk] - inner)).astype(BF16)
            ds_ref[chunk * HALF : (chunk + 1) * HALF] = dscore
            dkey = dot(dscore, stacked)
            dval = dot(prob, grads)
            if block == 1 and key < MEM + HALF:
                dkey = dkey + dkey_ref[key : key + HALF]
                dval = dval + dval_ref[key : key + HALF]
            dkey_ref[key : key + HALF] = dkey
            dval_ref[key : key + HALF] = dval
        for h in range(heads):
            dqt_ref[h * HD : (h + 1) * HD, block * HALF : (block + 1) * HALF] = dot(
                key_turned[h * HD : (h + 1) * HD, first_key : first_key + rows],
                ds_ref[:rows, h * HALF : (h + 1) * HALF],
            )
    dq_ref[...] = (jnp.transpose(dqt_ref[...]) * (1.0 / math.sqrt(HD))).astype(BF16)
    dk_ref[...] = dkey_ref[...].astype(BF16)
    dv_ref[...] = dval_ref[...].astype(BF16)
    step = SEG // PARTS
    for part_ref, row in zip(parts, range(0, SEG, step)):
        rows, seg_rows = pl.ds(row, step), pl.ds(MEM + row, step)
        part_ref[...] = (
            dot_nt(dk_ref[seg_rows], wk_ref[...])
            + dot_nt(dv_ref[seg_rows], wv_ref[...])
            + dot_nt(dq_ref[rows], wq_ref[...])
        ).astype(part_ref.dtype)


def attention_backward(vault, layer, own, other, gain):
    kept = vault.arrays
    q, k, val = kept["q", layer].shape, kept["k", layer].shape, kept["v", layer].shape
    width = q[1]
    heads = width // HD
    return chain_call(
        vault,
        functools.partial(attention_backward_body, layer),
        f"attention_backward_{layer}",
        [((1, D), F32)] + [((SEG // PARTS, D), BF16)] * PARTS,
        own,
        other,
        gain,
        adds={
            ("mid_grad", layer): ((SEG, D), F32),
            ("low_attn", layer): ((SEG, D), BF16),
            ("dq", layer): (q, BF16),
            ("dk", layer): (k, BF16),
            ("dv", layer): (val, BF16),
        },
        scratch=[
            pltpu.VMEM((KEYS_LOW, heads * HALF), BF16),
            pltpu.VMEM(k, F32),
            pltpu.VMEM(val, F32),
            pltpu.VMEM((width, SEG), F32),
        ],
        vmem=12,
    )


def attention_weights_body(layer, orders, v, where_ref, part_ref):
    nm_ref, dq_ref, dk_ref, dv_ref, mt_ref, low_ref = (
        v[n, layer] for n in ("nm", "dq", "dk", "dv", "mt", "low_attn")
    )
    width = dq_ref.shape[1]
    rows = D // 2
    for out, half in halves_of(v, layer, 0, orders, where_ref):
        cols = pl.ds(pl.multiple_of(half * rows, rows), rows)
        out[2, :, :width] = dot_tn(nm_ref[MEM:, cols], dq_ref[...]).astype(BF16)
        out[2, :, width:] = dot_tn(nm_ref[:, cols], dk_ref[...]).astype(BF16)
    for out, half in halves_of(v, layer, 1, orders, where_ref):

        @pl.when(half == 0)
        def _():
            for part in range(2):
                out[2, :, part * width : (part + 1) * width] = dot_tn(
                    nm_ref[:, part * rows : (part + 1) * rows], dv_ref[...]
                ).astype(BF16)

        @pl.when(half == 1)
        def _():
            out[2] = dot(mt_ref[...], low_ref[...]).astype(BF16)

    part_ref[...] = (dot_nt(dk_ref[:MEM], v["key", layer][...]) + dot_nt(dv_ref[:MEM], v["value", layer][...])).astype(
        part_ref.dtype
    )


def attention_weights(vault, layer, where, orders):
    width = vault.arrays["dq", layer].shape[1]
    assert D == 2 * width
    return chain_call(
        vault,
        functools.partial(attention_weights_body, layer, orders),
        f"attention_weights_{layer}",
        [((MEM, D), BF16)],
        scalars=(where,),
        vmem=4,
    )[0]


def finish_body(v, where_ref, *refs):
    own_ref, other_ref, part_ref, part_other, gain_ref, gain_attn_1, gain_ffn_0, gain_ffn_1, gate_own, gate_other = refs[:10]
    rest = refs[10 : 10 + 2 * LAYERS]
    out_ref, grad_ref, mem_grad_ref, small_ref = refs[10 + 2 * LAYERS :]
    core = where_ref[1]
    out_ref[pl.ds(pl.multiple_of(core * HALF, HALF), HALF), :] = own_ref[...]
    out_ref[pl.ds(pl.multiple_of((1 - core) * HALF, HALF), HALF), :] = other_ref[...]
    send(out_ref)
    incoming = part_ref[...].astype(F32) + part_other[...].astype(F32)
    moved, gain_part = norm_backward(v["x"][...].astype(F32), gain_ref[:1], incoming)
    grad_ref[...] = v["mid_grad", 0][...] + moved
    send(grad_ref)
    small_ref[...] = jnp.zeros_like(small_ref)
    for i, row in enumerate((gain_ffn_0[...], gain_ffn_1[...], gate_own[...] + gate_other[...])):
        small_ref[LAYERS + i : LAYERS + i + 1] = row
    for l in range(LAYERS):
        own, other = rest[2 * l : 2 * l + 2]
        incoming = own[...].astype(F32) + other[...].astype(F32)
        mem_grad_ref[l], gain_mem = norm_backward(v["memory", l][...].astype(F32), gain_ref[l : l + 1], incoming)
        small_ref[l : l + 1] = gain_mem + (gain_part if l == 0 else gain_attn_1[...])


def finish_rows(vault, where, *operands):
    return chain_call(
        vault,
        finish_body,
        "finish_rows",
        [((SEG, D), F32, HBM), ((SEG, D), F32, HBM), ((LAYERS, MEM, D), F32, HBM), ((8, D), F32)],
        *operands,
        scalars=(where,),
        vmem=14,
    )


def other_core(values):
    return lax.ppermute(values, "mp", [(0, 1), (1, 0)])


def other_core_split(parts):
    return Split([other_core(part) for part in parts])


def tie_split(split, *values):
    held = tie(*split.parts, *values)
    return (Split(list(held[: len(split.parts)])),) + tuple(held[len(split.parts) :])


def partner(values, bit):
    size = lax.axis_size("dp")
    return lax.ppermute(values, "dp", [(i, i ^ (1 << bit)) for i in range(size)])


def add_low(left, right):
    return (left.astype(F32) + right.astype(F32)).astype(BF16)


def fold_body(kept_name, bit, v, where_ref, *refs):
    come, out = refs[0], refs[-1]
    kept = v[kept_name]
    if bit is not None:
        half = come.shape[1] // 2
        mine = (where_ref[0] >> bit) & 1
        other, own = pl.ds((1 - mine) * half, half), pl.ds(mine * half, half)
        out[...] = add_low(kept[:, other], come[:, other])
        kept[:, :half] = add_low(kept[:, own], come[:, own])
        return
    total = add_low(kept[:, :1], come[...])
    if len(refs) == 2:
        out[...] = total
        return
    small = refs[1]
    rows, cols = kept.shape[2:]
    out[...] = jnp.zeros(out.shape, BF16)
    out[:, :, :, :cols] = total
    wide = D // 128
    for j in range(SMALL * wide):
        lane = cols + j // rows * 128
        out[0, 0, j % rows : j % rows + 1, lane : lane + 128] = small[
            j // wide : j // wide + 1, j % wide * 128 : (j % wide + 1) * 128
        ].astype(BF16)


def small_lanes(rows):
    return -(-SMALL * (D // 128) // rows) * 128


def fold(vault, name, kept_name, bit, where, come, small):
    kinds, pieces, rows, cols = come.shape
    if small is not None:
        cols += small_lanes(rows)
    return chain_call(
        vault,
        functools.partial(fold_body, kept_name, bit),
        name,
        [((kinds, 1 if bit is None else pieces // 2, rows, cols), BF16)],
        come,
        *([] if small is None else [small]),
        scalars=(where,),
        vmem=4,
        flops=SUM_FLOPS,
    )[0]


def join_body(bit, where_ref, mine_ref, other_ref, out_ref):
    pieces = mine_ref.shape[1]
    mine = (where_ref[0] >> bit) & 1
    out_ref[:, pl.ds(mine * pieces, pieces)] = mine_ref[...]
    out_ref[:, pl.ds((1 - mine) * pieces, pieces)] = other_ref[...]


def join(name, bit, where, mine, other):
    kinds, pieces, rows, cols = mine.shape
    return kernel_call(
        functools.partial(join_body, bit),
        name,
        [((kinds, 2 * pieces, rows, cols), BF16)],
        mine,
        other,
        scalars=(where,),
        vmem=4,
        flops=SUM_FLOPS,
    )[0]


def place_body(layer, place, bit, fresh, small, where_ref, mine_ref, other_ref, *refs):
    refs = refs if fresh else refs[3:]
    outs, refs = refs[:3], refs[3:]
    small_ref = None
    if small:
        small_ref, refs = refs[0], refs[1:]
    buffers, semaphores = refs[:-1], refs[-1]
    mine = (where_ref[0] >> bit) & 1
    pieces = mine_ref.shape[1]
    width = D // 2
    copies = []

    def put(buffer, target):
        copies.append(pltpu.make_async_copy(buffer, target, semaphores.at[len(copies)]))
        copies[-1].start()

    if place == 0:
        up, q, k = buffers
        for ref, side in ((mine_ref, mine), (other_ref, 1 - mine)):
            at = pl.ds(side * pieces, pieces)
            for j in range(2):
                up[at, :, j * D : (j + 1) * D] = ref[j, :, :, :D].astype(F32)
            q[at] = ref[2, :, :, :width].astype(F32)
            k[at] = ref[2, :, :, width:D].astype(F32)
    else:
        down, val, out = buffers
        for ref, side in ((mine_ref, mine), (other_ref, 1 - mine)):
            at = pl.ds(side * pieces, pieces)
            for j in range(2):
                down[j, at] = ref[j, :, :, :D].astype(F32)

        def rest(low_ref, high_ref):
            for j in range(2):
                val[j] = low_ref[2, :, :, j * width : (j + 1) * width].astype(F32)
            out[...] = high_ref[2, :, :, :D].astype(F32)

        pl.when(mine == 0)(lambda: rest(mine_ref, other_ref))
        pl.when(mine == 1)(lambda: rest(other_ref, mine_ref))
    for buffer, target in zip(buffers, outs):
        put(buffer, target.at[layer])
    if small:
        rows, wide = mine_ref.shape[2], D // 128
        total = jnp.sum(mine_ref[0, :, :, D:].astype(F32), axis=0) + jnp.sum(
            other_ref[0, :, :, D:].astype(F32), axis=0
        )
        for j in range(SMALL * wide):
            lane = j // rows * 128
            small_ref[j // wide : j // wide + 1, j % wide * 128 : (j % wide + 1) * 128] = total[
                j % rows : j % rows + 1, lane : lane + 128
            ]
    for copy in copies:
        copy.wait()


def place(layer, place_index, bit, where, mine, other, totals):
    kinds, pieces, rows, cols = mine.shape
    small = cols > D
    if place_index == 0:
        shapes = [(2 * pieces, rows, 2 * D), (2 * pieces, rows, D // 2), (2 * pieces, rows, D // 2)]
    else:
        shapes = [(2, 2 * pieces, rows, D), (2, pieces, rows, D // 2), (pieces, rows, D)]
    return kernel_call(
        functools.partial(place_body, layer, place_index, bit, totals is None, small),
        f"place{place_index}_{layer}",
        [((LAYERS,) + shape, F32, RAW) for shape in shapes] + ([((8, D), F32)] if small else []),
        mine,
        other,
        *([] if totals is None else [Slow(t, RAW) for t in totals]),
        scalars=(where,),
        scratch=[pltpu.VMEM(shape, F32) for shape in shapes] + [pltpu.SemaphoreType.DMA((3,))],
        aliases=None if totals is None else {3 + i: i for i in range(3)},
        vmem=8,
        flops=SUM_FLOPS,
    )


def in_pieces(values, size):
    kinds, rows, cols = values.shape
    return values.reshape(kinds, size // 2, 2 * rows // size, cols)


def tie(*values):
    return lax.optimization_barrier(values)


class Stream:
    def __init__(self, vault, layer, place_index, order, where, sent):
        self.vault, self.layer, self.place, self.order, self.where = vault, layer, place_index, order, where
        self.come = partner(sent, order[0])
        self.pieces = None
        self.step = 0

    def advance(self, after, small=None):
        steps = len(self.order)
        self.step += 1
        s = self.step
        name = f"sum{self.place}_{self.layer}_step{s}"
        kept_name = (f"kept{self.place}", self.layer)
        if s <= steps:
            come, after = tie(self.come, after)
            bit = None if s == steps else self.order[s]
            out = fold(self.vault, name, kept_name, bit, self.where, come, small if s == steps else None)
            at = min(s, steps - 1)
            if s == steps:
                self.vault.drop(kept_name)
        else:
            at = 2 * steps - s - 1
            come, after = tie(self.come, after)
            out = join(name, self.order[at + 1], self.where, self.pieces, come)
        if s >= steps:
            self.pieces = out
        self.come = partner(out, self.order[at])
        return out

    def settle(self, totals, after):
        come, after = tie(self.come, after)
        return place(self.layer, self.place, self.order[0], self.where, self.pieces, come, totals)


def local(
    layer_input, memory, doc_lengths, neighbour_owner, neighbour_row, table, gain_attn, w_query, w_key, w_value,
    w_out, gain_ffn, w_up, w_down, w_gate, cotangent,
):
    size = lax.axis_size("dp")
    bits_count = size.bit_length() - 1
    rest = list(range(3, bits_count))
    orders = (([1, 0, 2] + rest, [2, 1, 0] + rest), ([0, 1, 2] + rest, [2, 0, 1] + rest))
    where = jnp.stack([lax.axis_index("dp"), lax.axis_index("mp")])
    x = layer_input[0]

    columns = table.shape[1] // 2
    table_own = own_columns(where, table)
    table_far = partner(table_own, bits_count - 1)
    half = size // 2
    turned = half <= 8
    table_own, owner_rows = tie(table_own, neighbour_owner[0].T)
    wanted, ranks = build_requests(where, owner_rows, neighbour_row[0].T, size, turned)
    capacity = wanted.shape[2] // 2
    halves = [list(range(half)), list(range(half, size))]

    def exchange(values):
        return lax.all_to_all(values, "dp", split_axis=0, concat_axis=0, tiled=True, axis_index_groups=halves)

    asked, x = tie(exchange(wanted), x)
    vault = Vault()
    stacks = (w_query, w_key, w_value, w_out, w_up, w_down, memory[:, 0], x, cotangent[0])
    names = ("query", "key", "value", "out", "up", "down", "memory")
    sources = [("x", 7, None)] + [((n, l), i, l) for l in range(LAYERS) for i, n in enumerate(names)] + [("cot", 8, None)]
    load(vault, stacks, sources)
    parts = ()
    for l in range(LAYERS):
        part = attention_forward(vault, l, doc_lengths, parts, gain_attn)
        if l == 0:
            part, asked, table_far = tie(part, asked, table_far)
            answers = answer_requests(where, asked, table_own, table_far, turned)
            part, *answers = tie(part, *answers)
            if turned:
                early = [m for m in range(1, half) if bin(m).count("1") != 2]
                late = [m for m in range(1, half) if bin(m).count("1") == 2]
                moved = {m: lax.ppermute(answers[m], "dp", [(i, i ^ m) for i in range(size)]) for m in early + late}
        if l == 1 and turned:
            part, *got = tie(part, *[moved[m] for m in late])
            moved.update(zip(late, got))
        ffn_part = ffn_forward(vault, l, part, other_core(part), gain_ffn)
        if l == 0 and turned:
            ffn_part, *got = tie(ffn_part, *[moved[m] for m in early])
            moved.update(zip(early, got))
        parts = (ffn_part, other_core(ffn_part))
    if turned:
        near_own = [answers[0]] + [moved[m] for m in range(1, half)]
    else:
        near_own = [exchange(answers[0]).reshape(-1, columns)]
    near_other = [other_core(a) for a in near_own]

    final, grad, gate_part = retrieval(
        vault, where, *parts, w_gate[None], Slow(ranks), near_own, near_other, capacity
    )
    vault.drop("cot")
    incoming = (grad, other_core(grad))
    scalars = (where,)
    memory_parts = []
    gain_attn_1 = None
    gains_ffn = [None] * LAYERS
    streams = {}
    for l in range(LAYERS - 1, -1, -1):
        part = ffn_backward(vault, l, scalars, incoming)
        if l < LAYERS - 1:
            gain_attn_1, *part = part
            vault.drop(("hidden", l + 1), ("mid_grad", l + 1))
        vault.drop(("slope", l))
        part_other = other_core_split(part)
        ffn_weights(vault, l, where, orders[l])
        vault.drop(*((n, l) for n in ("nf", "dpre", "act", "low", "up", "down")))
        gains_ffn[l], *part = attention_backward(vault, l, Split(part), part_other, gain_ffn)
        vault.drop(*((n, l) for n in ("q", "k", "v", "p", "linv", "grad", "middle", "out", "query")))
        part_other = other_core_split(part)
        mem_part = attention_weights(vault, l, where, orders[l])
        vault.drop(*((n, l) for n in ("nm", "dq", "dk", "dv", "mt", "low_attn", "key", "value")))
        for i in range(2):
            vault.arrays[f"kept{i}", l] = in_pieces(vault.arrays[f"kept{i}", l], size)
            sent = in_pieces(vault.arrays.pop((f"sent{i}", l)), size)
            streams[l, i] = Stream(vault, l, i, orders[l][i], where, sent)
        part_other, mem_part = tie_split(part_other, mem_part)
        memory_parts = [mem_part, other_core(mem_part)] + memory_parts
        incoming = (Split(part), part_other, gain_attn)
        scalars = ()
    last = 2 * bits_count - 1
    lag = {(1, 1): 0.0, (1, 0): 0.25, (0, 0): 0.8, (0, 1): 1.05}
    events = sorted((s + lag[key], key) for key in streams for s in range(1, last + 1))
    events += [(0.0, key) for key in ((1, 1), (1, 0), (0, 0), (0, 1))]
    after, small = mem_part, None
    totals = [None, None]
    for count, (_, key) in enumerate(events):
        if count == 2:
            gate_part, final, after = tie(gate_part, final, after)
            layer_output, input_grad, memory_grad, small = finish_rows(
                vault, where, final, other_core(final), *incoming[:2], gain_attn, gain_attn_1, *gains_ffn,
                gate_part, other_core(gate_part), *memory_parts,
            )
            vault.drop("x", ("mid_grad", 0), *(("memory", l) for l in range(LAYERS)))
            after = small
        stream = streams[key]
        if stream.step < last:
            after = stream.advance(after, small if key == (1, 1) else None)
        else:
            result = stream.settle(totals[key[1]], after)
            totals[key[1]] = result[:3]
            after = result[0]
            if len(result) > 3:
                small = result[3]
    (up, wq, wk), (down, wv, wo) = totals
    up = up.reshape(LAYERS, D, -1)
    down = down.reshape(LAYERS, -1, D)
    width = wq.shape[-1]
    return (
        layer_output[None],
        input_grad[None],
        memory_grad[:, None],
        small[:LAYERS],
        wq.reshape(LAYERS, D, width),
        wk.reshape(LAYERS, D, width),
        wv.reshape(LAYERS, D, width),
        wo.reshape(LAYERS, width, D),
        small[LAYERS : 2 * LAYERS],
        up,
        down,
        small[2 * LAYERS],
    )


def solution(mesh):
    return jax.shard_map(
        local,
        mesh=mesh,
        in_specs=(
            P("dp", None, None),
            P(None, "dp", None, None),
            P("dp", None),
            P("dp", None, None),
            P("dp", None, None),
            P("dp", None),
            P(),
            P(None, None, "mp"),
            P(None, None, "mp"),
            P(None, None, "mp"),
            P(None, "mp", None),
            P(),
            P(None, None, "mp"),
            P(None, "mp", None),
            P(),
            P("dp", None, None),
        ),
        out_specs=(
            P("dp", None, None),
            P("dp", None, None),
            P(None, "dp", None, None),
            P(),
            P(None, None, "mp"),
            P(None, None, "mp"),
            P(None, None, "mp"),
            P(None, "mp", None),
            P(),
            P(None, None, "mp"),
            P(None, "mp", None),
            P(),
        ),
        check_vma=False,
    )
```

```python
import functools
import math

import jax
import jax.numpy as jnp
from jax import lax
from jax.experimental import pallas as pl
from jax.experimental.pallas import tpu as pltpu
from jax.sharding import PartitionSpec as P

D = 512
HD = 64
SEG = 512
MEM = 512
LAYERS = 2
NEIGHBOURS = 4
HALF = SEG // 2
KEYS_LOW = MEM + HALF
NORM_EPS = 1e-05
MASKED = -1e30
PARTS = 2
MASKS = ((1, 6), (2, 5), (4, 3), (7, 0))
SUM_FLOPS = 2_000_000_000
SMALL = 2 * LAYERS + 1
BF16 = jnp.bfloat16
F32 = jnp.float32
HBM, RAW, KEEP = "hbm", "raw", "keep"


def dot(left, right):
    return lax.dot_general(left, right, (((1,), (0,)), ((), ())), preferred_element_type=F32)


def dot_nt(left, right):
    return lax.dot_general(left, right, (((1,), (1,)), ((), ())), preferred_element_type=F32)


def dot_tn(left, right):
    return lax.dot_general(left, right, (((0,), (0,)), ((), ())), preferred_element_type=F32)


class Fetched:
    def __init__(self, source, buffer, semaphore):
        self.buffer = buffer
        self.copy = pltpu.make_async_copy(source, buffer, semaphore)
        self.copy.start()
        self.waiting = True
        self.shape = buffer.shape
        self.dtype = buffer.dtype

    def arrive(self):
        if self.waiting:
            self.copy.wait()
            self.waiting = False

    def __getitem__(self, index):
        self.arrive()
        return self.buffer[index]


class Stored:
    def __init__(self, target, buffer, semaphore):
        self.buffer = buffer
        self.copy = pltpu.make_async_copy(buffer, target, semaphore)
        self.sent = False
        self.shape = buffer.shape
        self.dtype = buffer.dtype

    def __getitem__(self, index):
        return self.buffer[index]

    def __setitem__(self, index, values):
        self.buffer[index] = values

    def send(self):
        self.copy.start()
        self.sent = True


class Slow:
    def __init__(self, array, layer=None):
        self.array = array
        self.layer = layer
        self.shape = array.shape if layer is None else array.shape[1:]
        self.dtype = array.dtype


class Pinned:
    def __init__(self, array):
        self.array = array
        self.shape = array.shape
        self.dtype = array.dtype


class Split:
    def __init__(self, parts):
        self.parts = parts


class Rows:
    def __init__(self, refs):
        self.refs = refs

    def __getitem__(self, index):
        return jnp.concatenate([ref[...] for ref in self.refs], axis=0)


def placed(operand):
    if isinstance(operand, (Slow, Pinned)):
        space = pltpu.HBM if isinstance(operand, Slow) else pltpu.VMEM
        return pltpu.with_memory_space_constraint(operand.array, space)
    return operand


def send(*refs):
    for ref in refs:
        if isinstance(ref, Stored):
            ref.send()


class Here:
    def __getitem__(self, index):
        return lax.axis_index(("dp", "mp")[index])


class Vault:
    def __init__(self):
        self.arrays = {}

    def drop(self, *names):
        for name in names:
            del self.arrays[name]


def chain_call(vault, body, name, outs, *operands, adds=None, here=False, **options):
    adds = adds or {}
    scalars = len(options.get("scalars", ()))
    names = list(vault.arrays)
    given = sum(len(a.parts) if isinstance(a, Split) else 1 for a in operands)

    def whole(*refs):
        head, rest = refs[: scalars + len(operands)], refs[scalars + len(operands) + len(names) :]
        mine, kept = rest[: len(outs)], rest[len(outs) : len(outs) + len(names) + len(adds)]
        extra = rest[len(outs) + len(names) + len(adds) :]
        body(dict(zip(names + list(adds), kept)), *([Here()] if here else []), *head, *mine, *extra)

    results = kernel_call(
        whole,
        name,
        list(outs)
        + [(vault.arrays[n].shape, vault.arrays[n].dtype, KEEP) for n in names]
        + [(shape, kind, KEEP) for shape, kind in adds.values()],
        *operands,
        *[Pinned(vault.arrays[n]) for n in names],
        aliases={scalars + given + i: len(outs) + i for i in range(len(names))},
        **options,
    )
    vault.arrays = dict(zip(names + list(adds), results[len(outs) :]))
    return results[: len(outs)]


def kernel_call(body, name, outs, *operands, scratch=(), scalars=(), aliases=None, vmem=4, flops=0, here=False):
    arrays, plan = [], []
    for operand in operands:
        parts = operand.parts if isinstance(operand, Split) else [operand]
        plan.append((operand, len(arrays), len(parts)))
        arrays.extend(parts)
    slow = [isinstance(a, Slow) for a in arrays]
    fetched = [s and a.layer != RAW for a, s in zip(arrays, slow)]
    spaces = [out[2] if len(out) > 2 else None for out in outs]
    stored = [space is HBM for space in spaces]
    specs = [pl.BlockSpec(memory_space=pltpu.SMEM)] * len(scalars)
    specs += [pl.BlockSpec(memory_space=pltpu.HBM if s else pltpu.VMEM) for s in slow]
    buffers = [pltpu.VMEM(a.shape, a.dtype) for a, f in zip(arrays, fetched) if f]
    buffers += [pltpu.VMEM(out[0], out[1]) for out, s in zip(outs, stored) if s]
    first = len(scalars)
    middle = first + len(arrays)
    last = middle + len(outs)

    def whole(*refs):
        held, extra = refs[last : last + len(buffers)], refs[last + len(buffers) :]
        semaphores = None
        if buffers:
            semaphores, extra = extra[0], extra[1:]
        count = 0
        ins, results = [], []
        for ref, array, f in zip(refs[first:middle], arrays, fetched):
            if f:
                source = ref if array.layer is None else ref.at[array.layer]
                ref = Fetched(source, held[count], semaphores.at[count])
                count += 1
            ins.append(ref)
        for ref, s in zip(refs[middle:last], stored):
            if s:
                ref = Stored(ref, held[count], semaphores.at[count])
                count += 1
            results.append(ref)
        given = [Rows(ins[at : at + n]) if isinstance(op, Split) else ins[at] for op, at, n in plan]
        body(*([Here()] if here else []), *refs[:first], *given, *results, *extra)
        for ref in ins:
            if isinstance(ref, Fetched):
                ref.arrive()
        for ref in results:
            if isinstance(ref, Stored) and not ref.sent:
                ref.send()
        for ref in results:
            if isinstance(ref, Stored):
                ref.copy.wait()

    return pl.pallas_call(
        whole,
        out_shape=[
            jax.ShapeDtypeStruct(out[0], out[1])
            if space is None
            else (pltpu.VMEM if space is KEEP else pltpu.HBM)(out[0], out[1])
            for out, space in zip(outs, spaces)
        ],
        in_specs=specs,
        out_specs=[pl.BlockSpec(memory_space=pltpu.HBM if space in (HBM, RAW) else pltpu.VMEM) for space in spaces],
        scratch_shapes=(buffers + [pltpu.SemaphoreType.DMA((len(buffers),))] if buffers else []) + list(scratch),
        input_output_aliases=aliases or {},
        compiler_params=pltpu.CompilerParams(vmem_limit_bytes=vmem * 1024 * 1024),
        cost_estimate=pl.CostEstimate(flops=flops, bytes_accessed=1000, transcendentals=0),
        name=name,
    )(*scalars, *[placed(a) for a in arrays])


def norm_parts(values):
    average = jnp.mean(values, axis=-1, keepdims=True)
    centred = values - average
    inverse = lax.rsqrt(jnp.mean(centred * centred, axis=-1, keepdims=True) + NORM_EPS)
    return centred * inverse, inverse


def norm_backward(values, gain, grad):
    unit, inverse = norm_parts(values)
    scaled = grad * gain
    inner = jnp.mean(scaled * unit, axis=-1, keepdims=True)
    moved = inverse * (scaled - jnp.mean(scaled, axis=-1, keepdims=True) - unit * inner)
    return moved, jnp.sum(grad * unit, axis=0, keepdims=True)


def heads_stacked(values, first):
    rows = values[first : first + HALF]
    lanes = lax.broadcasted_iota(jnp.int32, rows.shape, 1) // HD
    heads = values.shape[1] // HD
    return jnp.concatenate(
        [jnp.where(lanes == h, rows, jnp.zeros_like(rows)) for h in range(heads)], axis=0
    )


def document_starts(lens_ref, first, heads):
    places = first + lax.broadcasted_iota(jnp.int32, (1, heads * HALF), 1) % HALF
    starts = jnp.zeros_like(places)
    end = 0
    for slot in range(lens_ref.shape[1]):
        end = end + lens_ref[0, slot]
        starts = jnp.where(places >= end, end, starts)
    return places, starts


def load_body(sources, v, *refs):
    semaphores = refs[-1]
    copies = []
    for i, (name, which, layer) in enumerate(sources):
        source = refs[which] if layer is None else refs[which].at[layer]
        copies.append(pltpu.make_async_copy(source, v[name], semaphores.at[i]))
        copies[-1].start()
    for copy in copies:
        copy.wait()


def load(vault, arrays, sources):
    adds = {}
    for name, which, layer in sources:
        shape = arrays[which].shape
        adds[name] = (shape if layer is None else shape[1:], arrays[which].dtype)
    chain_call(
        vault,
        functools.partial(load_body, sources),
        "load_weights",
        [],
        *[Slow(a, RAW) for a in arrays],
        adds=adds,
        scratch=[pltpu.SemaphoreType.DMA((len(sources),))],
    )


def attention_forward_body(layer, v, *refs):
    nm_ref, q_ref, k_ref, v_ref = v["nm", layer], v["q", layer], v["k", layer], v["v", layer]
    p_ref, linv_ref, mt_ref = v["p", layer], v["linv", layer], v["mt", layer]
    mem_ref = v["memory", layer]
    wq_ref, wk_ref, wv_ref, wo_ref = (v[n, layer] for n in ("query", "key", "value", "out"))
    if layer == 0:
        lens, gain_ref, part_ref, s_ref = refs
        hidden = v["x"][...].astype(F32)
    else:
        lens, own_ref, other_ref, gain_ref, part_ref, s_ref = refs
        hidden = v["middle", layer - 1][...] + (own_ref[...].astype(F32) + other_ref[...].astype(F32))
        v["hidden", layer][...] = hidden
    gain = gain_ref[layer : layer + 1]
    nm_ref[MEM:] = (norm_parts(hidden)[0] * gain).astype(BF16)
    nm_ref[:MEM] = (norm_parts(mem_ref[...].astype(F32))[0] * gain).astype(BF16)
    q_ref[...] = (dot(nm_ref[MEM:], wq_ref[...]).astype(BF16).astype(F32) * (1.0 / math.sqrt(HD))).astype(BF16)
    k_ref[...] = dot(nm_ref[...], wk_ref[...]).astype(BF16)
    value_rows = dot(nm_ref[...], wv_ref[...])
    v_ref[...] = value_rows.astype(BF16)
    value_turned = jnp.transpose(value_rows).astype(BF16)
    heads = q_ref.shape[1] // HD
    queries = q_ref[...]
    for block in range(2):
        places, starts = document_starts(lens, block * HALF, heads)
        stacked = heads_stacked(queries, block * HALF)
        first_key = 0 if block == 0 else MEM
        rows = KEYS_LOW if block == 0 else SEG
        top = None
        for chunk in range(rows // HALF):
            key = first_key + chunk * HALF
            scores = dot_nt(k_ref[key : key + HALF], stacked)
            if key < MEM:
                scores = scores + jnp.where(starts == 0, 0.0, MASKED)
            else:
                spots = key - MEM + lax.broadcasted_iota(jnp.int32, scores.shape, 0)
                seen = spots >= starts
                if key - MEM == block * HALF:
                    seen = seen & (spots <= places)
                scores = jnp.where(seen, scores, MASKED)
            s_ref[chunk * HALF : (chunk + 1) * HALF] = scores
            peak = jnp.max(scores, axis=0, keepdims=True)
            top = peak if top is None else jnp.maximum(top, peak)
        total = None
        first_row = 0 if block == 0 else KEYS_LOW
        for chunk in range(rows // HALF):
            weight = jnp.exp(s_ref[chunk * HALF : (chunk + 1) * HALF] - top)
            part = jnp.sum(weight, axis=0, keepdims=True)
            total = part if total is None else total + part
            p_ref[first_row + chunk * HALF : first_row + (chunk + 1) * HALF] = weight.astype(BF16)
        inverse = 1.0 / total
        linv_ref[block : block + 1] = inverse
        for h in range(heads):
            mixed = dot(
                value_turned[h * HD : (h + 1) * HD, first_key : first_key + rows],
                p_ref[first_row : first_row + rows, h * HALF : (h + 1) * HALF],
            )
            mt_ref[h * HD : (h + 1) * HD, block * HALF : (block + 1) * HALF] = (
                mixed * inverse[:, h * HALF : (h + 1) * HALF]
            ).astype(BF16)
    part_ref[...] = dot_tn(mt_ref[...], wo_ref[...]).astype(part_ref.dtype)


def attention_forward(vault, layer, lens, parts, gain):
    width = vault.arrays["query", layer].shape[1]
    heads = width // HD
    adds = {
        ("nm", layer): ((MEM + SEG, D), BF16),
        ("q", layer): ((SEG, width), BF16),
        ("k", layer): ((MEM + SEG, width), BF16),
        ("v", layer): ((MEM + SEG, width), BF16),
        ("p", layer): ((KEYS_LOW + SEG, heads * HALF), BF16),
        ("linv", layer): ((2, heads * HALF), F32),
        ("mt", layer): ((width, SEG), BF16),
    }
    if layer > 0:
        adds["hidden", layer] = ((SEG, D), F32)
    return chain_call(
        vault,
        functools.partial(attention_forward_body, layer),
        f"attention_forward_{layer}",
        [((SEG, D), BF16)],
        *parts,
        gain,
        adds=adds,
        scalars=(lens,),
        scratch=[pltpu.VMEM((KEYS_LOW, heads * HALF), F32)],
        vmem=5,
    )[0]


GELU_INNER = math.sqrt(2.0 / math.pi)
GELU_CUBE = 0.044715


def ffn_forward_body(layer, v, own_ref, other_ref, gain_ref, part_ref):
    x_ref = v["x"] if layer == 0 else v["hidden", layer]
    nf_ref, act_ref, slope_ref = v["nf", layer], v["act", layer], v["slope", layer]
    middle = x_ref[...].astype(F32) + (own_ref[...].astype(F32) + other_ref[...].astype(F32))
    v["middle", layer][...] = middle
    nf_ref[...] = (norm_parts(middle)[0] * gain_ref[layer : layer + 1]).astype(BF16)
    step = 128
    for row in range(0, SEG, step):
        rows = pl.ds(row, step)
        pre = dot(nf_ref[rows], v["up", layer][...])
        square = pre * pre
        bend = jnp.tanh(GELU_INNER * pre * (1.0 + GELU_CUBE * square))
        half = 0.5 * (1.0 + bend)
        act = (pre * half).astype(BF16)
        act_ref[rows] = act
        slope_ref[rows] = (
            half
            + (0.5 * GELU_INNER) * pre * (1.0 - bend * bend) * (1.0 + (3.0 * GELU_CUBE) * square)
        ).astype(BF16)
        part_ref[rows] = dot(act, v["down", layer][...]).astype(part_ref.dtype)


def ffn_forward(vault, layer, own, other, gain):
    units = vault.arrays["up", layer].shape[1]
    return chain_call(
        vault,
        functools.partial(ffn_forward_body, layer),
        f"ffn_forward_{layer}",
        [((SEG, D), BF16)],
        own,
        other,
        gain,
        adds={
            ("middle", layer): ((SEG, D), F32),
            ("nf", layer): ((SEG, D), BF16),
            ("act", layer): ((SEG, units), BF16),
            ("slope", layer): ((SEG, units), BF16),
        },
        vmem=3,
    )[0]


def requests_body(owners, turned, where_ref, owner_ref, row_ref, asked_ref, ranks_ref):
    half = owners // 2
    capacity = asked_ref.shape[2] // 2
    lanes, tokens = ranks_ref.shape[1], ranks_ref.shape[0]
    me = where_ref[0]
    names = owner_ref[...] ^ (me & half)
    spots = lax.broadcasted_iota(jnp.int32, (lanes, tokens), 0)
    hits = jnp.zeros((lanes, tokens), F32)
    for k in range(NEIGHBOURS):
        hits = hits + (names[k : k + 1] == spots).astype(F32)
    above = (
        lax.broadcasted_iota(jnp.int32, (tokens, tokens), 0)
        < lax.broadcasted_iota(jnp.int32, (tokens, tokens), 1)
    )
    ranks = dot(hits.astype(BF16), above.astype(F32).astype(BF16))
    slots = lax.broadcasted_iota(jnp.int32, (capacity, tokens), 0).astype(F32)
    high = jnp.zeros((lanes, capacity), F32)
    low = jnp.zeros((lanes, capacity), F32)
    kept = jnp.full((lanes, tokens), -1.0, F32)
    order = names ^ (me & (half - 1)) if turned else names
    for k in range(NEIGHBOURS):
        named = names[k : k + 1] == spots
        rank = jnp.sum(jnp.where(named, ranks, 0.0), axis=0, keepdims=True)
        kept = jnp.where(order[k : k + 1] == spots, rank, kept)
        taken = (slots == rank).astype(F32).astype(BF16)
        row = row_ref[k : k + 1]
        upper = row // 32
        high = high + dot_nt(jnp.where(named, upper.astype(F32), 0.0).astype(BF16), taken)
        low = low + dot_nt(jnp.where(named, (row - upper * 32).astype(F32), 0.0).astype(BF16), taken)
    ranks_ref[...] = jnp.transpose(kept).astype(BF16)
    asked = (high * 32.0 + low).astype(jnp.int32)
    asked_ref[:, 0, :capacity] = asked[:half]
    asked_ref[:, 0, capacity:] = asked[half : 2 * half]


def own_rows_body(where_ref, table_ref, out_ref, semaphore):
    rows = out_ref.shape[0]
    at = pl.ds(pl.multiple_of(where_ref[1] * rows, rows), rows)
    copy = pltpu.make_async_copy(table_ref.at[at], out_ref, semaphore)
    copy.start()
    copy.wait()


def own_rows(table):
    return kernel_call(
        own_rows_body,
        "own_rows",
        [((table.shape[0] // 2, table.shape[1]), BF16)],
        Slow(table, RAW),
        here=True,
        scratch=[pltpu.SemaphoreType.DMA],
    )[0]


def build_requests(neighbour_owner, neighbour_row, owners, turned):
    tokens = neighbour_owner.shape[1]
    capacity = 2 * NEIGHBOURS * tokens // owners
    lanes = -(-owners // 128) * 128
    return kernel_call(
        functools.partial(requests_body, owners, turned),
        "build_requests",
        [((owners // 2, 1, 2 * capacity), jnp.int32), ((tokens, lanes), BF16, HBM)],
        Slow(neighbour_owner),
        Slow(neighbour_row),
        here=True,
        vmem=4,
    )


def picked_rows(column, parts, core):
    total = None
    for i, ref in enumerate(parts):
        rows = ref.shape[0]
        base = 0 if len(parts) == 1 else (core if i == 0 else 1 - core) * rows
        spots = lax.broadcasted_iota(jnp.int32, (column.shape[0], rows), 1) + base
        found = dot((column == spots.astype(F32)).astype(F32).astype(BF16), ref[...])
        total = found if total is None else total + found
    return total.astype(BF16)


def answer_body(v, where_ref, asked_ref, far_own, far_other, *outs):
    blocks, _, width = asked_ref.shape
    capacity = width // 2
    me, core = where_ref[0], where_ref[1]
    asked = jnp.transpose(asked_ref[:, 0, :].astype(F32))
    near, far = (v["table"],), (far_own, far_other)
    if len(outs) > 1:
        columns = lax.broadcasted_iota(jnp.int32, asked.shape, 1)
        for out, masks in zip(outs, MASKS):
            source = (me & (blocks - 1)) ^ jnp.where(core == 0, masks[0], masks[1])
            column = jnp.sum(jnp.where(columns == source, asked, 0.0), axis=1, keepdims=True)
            out[:capacity] = picked_rows(column[:capacity], near, core)
            out[capacity:] = picked_rows(column[capacity:], far, core)
        return
    for side, parts in enumerate((near, far)):

        @pl.when(core == side)
        def _():
            for block in range(blocks):
                column = asked[side * capacity : (side + 1) * capacity, block : block + 1]
                outs[0][block] = picked_rows(column, parts, core)


def answer_requests(vault, asked, far_own, far_other, turned):
    blocks, _, width = asked.shape
    cols = far_own.shape[1]
    return chain_call(
        vault,
        answer_body,
        "answer_requests",
        [((width, cols), BF16)] * len(MASKS) if turned else [((blocks, width // 2, cols), BF16)],
        asked,
        far_own,
        far_other,
        here=True,
        vmem=6,
    )


def retrieval_body(capacity, owners, v, where_ref, own_ref, other_ref, gate_ref, ranks_ref, *refs):
    count = len(refs) - 5
    near = refs[:count]
    final_ref, grad_ref, gate_grad_ref, s_ref, g_ref = refs[count:]
    core = where_ref[1]
    mid_ref, cot_ref = v["middle", LAYERS - 1], v["cot"]
    rows = pl.ds(pl.multiple_of(core * HALF, HALF), HALF)
    hidden = mid_ref[rows, :] + (own_ref[rows, :].astype(F32) + other_ref[rows, :].astype(F32))
    low = hidden.astype(BF16)
    cot = cot_ref[rows, :]
    ranks = ranks_ref[rows, :]
    step = 512
    scale = 1.0 / math.sqrt(D)
    owner_lane = lax.broadcasted_iota(jnp.int32, (ranks.shape[1], step), 0)
    slot_lane = lax.broadcasted_iota(jnp.int32, (ranks.shape[1], step), 1)
    slot_rank = (lax.broadcasted_iota(jnp.int32, (HALF, step), 1) % capacity).astype(F32)
    blocks = [(i, first) for i in range(count) for first in range(0, near[i].shape[0], step)]

    def named(i, first):
        here = i < count // 2
        if count > 2:
            masks = MASKS[i % (count // 2)]
            mask = jnp.where(core == 0, masks[0 if here else 1], masks[1 if here else 0])
            return mask + slot_lane // capacity * (owners // 2)
        return (slot_lane + first) // capacity + (core if here else 1 - core) * (owners // 2)

    pair = jnp.concatenate([low, cot], axis=0)
    top = jnp.full((HALF, 1), MASKED, F32)
    for number, (i, first) in enumerate(blocks):
        at = pl.ds(number * step, step)
        spread = (named(i, first) == owner_lane).astype(F32).astype(BF16)
        taken = dot(ranks, spread) == slot_rank
        both = dot_nt(pair, near[i][pl.ds(first, step)])
        scores = jnp.where(taken, both[:HALF] * scale, MASKED)
        top = jnp.maximum(top, jnp.max(scores, axis=1, keepdims=True))
        s_ref[:, at] = scores
        g_ref[:, at] = both[HALF:]
    total = jnp.zeros((HALF, 1), F32)
    inner = jnp.zeros((HALF, 1), F32)
    for number in range(len(blocks)):
        at = pl.ds(number * step, step)
        weight = jnp.exp(s_ref[:, at] - top)
        s_ref[:, at] = weight
        total = total + jnp.sum(weight, axis=1, keepdims=True)
        inner = inner + jnp.sum(weight * g_ref[:, at], axis=1, keepdims=True)
    inverse = 1.0 / total
    inner = inner * inverse
    gate = jax.nn.sigmoid(jnp.sum(hidden * gate_ref[...], axis=1, keepdims=True))
    slope_scale = gate * scale
    found = jnp.zeros((2 * HALF, D), F32)
    for number, (i, first) in enumerate(blocks):
        at = pl.ds(number * step, step)
        weight = s_ref[:, at] * inverse
        slope = weight * ((g_ref[:, at] - inner) * slope_scale)
        found += dot(jnp.concatenate([weight.astype(BF16), slope.astype(BF16)], axis=0), near[i][pl.ds(first, step)])
    pooled, back = found[:HALF], found[HALF:]
    cot = cot.astype(F32)
    away = pooled - hidden
    final_ref[...] = hidden + gate * away
    gate_grad = gate * (1.0 - gate) * jnp.sum(cot * away, axis=1, keepdims=True)
    gate_grad_ref[...] = jnp.sum(gate_grad * hidden, axis=0, keepdims=True)
    grad_ref[...] = (1.0 - gate) * cot + gate_grad * gate_ref[...] + back


def retrieval(vault, own, other, w_gate, ranks, near, capacity, owners):
    slots = sum(a.shape[0] for a in near)
    return chain_call(
        vault,
        functools.partial(retrieval_body, capacity, owners),
        "retrieval",
        [((HALF, D), F32), ((HALF, D), F32), ((1, D), F32)],
        own,
        other,
        w_gate,
        ranks,
        *near,
        here=True,
        scratch=[pltpu.VMEM((HALF, slots), F32), pltpu.VMEM((HALF, slots), F32)],
        vmem=13,
    )


def ffn_backward_body(layer, v, *refs):
    grad_ref, low_ref, dpre_ref = v["grad", layer], v["low", layer], v["dpre", layer]
    if layer == LAYERS - 1:
        where_ref, own_ref, other_ref = refs[:3]
        parts = refs[3:]
        core = where_ref[1]
        grad_ref[pl.ds(pl.multiple_of(core * HALF, HALF), HALF), :] = own_ref[...]
        grad_ref[pl.ds(pl.multiple_of((1 - core) * HALF, HALF), HALF), :] = other_ref[...]
        grad = grad_ref[...]
    else:
        own_ref, other_ref, gain_ref, gain_grad_ref = refs[:4]
        parts = refs[4:]
        incoming = own_ref[...].astype(F32) + other_ref[...].astype(F32)
        moved, gain_grad_ref[...] = norm_backward(v["hidden", layer + 1][...], gain_ref[layer + 1 : layer + 2], incoming)
        grad = v["mid_grad", layer + 1][...] + moved
        grad_ref[...] = grad
    low_ref[...] = grad.astype(BF16)
    step = SEG // PARTS
    for part_ref, row in zip(parts, range(0, SEG, step)):
        rows = pl.ds(row, step)
        dact = dot_nt(low_ref[rows], v["down", layer][...])
        dpre = (v["slope", layer][rows].astype(F32) * dact).astype(BF16)
        dpre_ref[rows] = dpre
        part_ref[...] = dot_nt(dpre, v["up", layer][...]).astype(part_ref.dtype)


def ffn_backward(vault, layer, incoming):
    units = vault.arrays["up", layer].shape[1]
    outs = [((SEG // PARTS, D), BF16)] * PARTS
    if layer < LAYERS - 1:
        outs = [((1, D), F32)] + outs
    return chain_call(
        vault,
        functools.partial(ffn_backward_body, layer),
        f"ffn_backward_{layer}",
        outs,
        *incoming,
        adds={
            ("grad", layer): ((SEG, D), F32),
            ("low", layer): ((SEG, D), BF16),
            ("dpre", layer): ((SEG, units), BF16),
        },
        here=layer == LAYERS - 1,
        vmem=3,
    )


def side_of(where_ref, bits):
    return (where_ref[0] >> jnp.where(where_ref[1] == 0, bits[0], bits[1])) & 1


def halves_of(v, layer, place, orders, where_ref):
    mine = side_of(where_ref, orders[place][0])
    return ((v[f"sent{place}", layer], 1 - mine), (v[f"kept{place}", layer], mine))


def ffn_weights_body(layer, orders, v, where_ref):
    nf_ref, dpre_ref, act_ref, low_ref = (v[n, layer] for n in ("nf", "dpre", "act", "low"))
    rows = D // 2
    for place in range(2):
        for out, half in halves_of(v, layer, place, orders, where_ref):
            if place == 0:
                left = nf_ref[:, pl.ds(pl.multiple_of(half * rows, rows), rows)]
                grads = dot_tn(left, dpre_ref[...]).astype(BF16)
                for j in range(2):
                    out[j] = grads[:, j * D : (j + 1) * D]
            else:
                for j in range(2):
                    left = act_ref[:, pl.ds(pl.multiple_of(j * D + half * rows, rows), rows)]
                    out[j] = dot_tn(left, low_ref[...]).astype(BF16)


def ffn_weights(vault, layer, orders):
    assert vault.arrays["act", layer].shape[1] == 2 * D
    shape = ((3, D // 2, D), BF16)
    chain_call(
        vault,
        functools.partial(ffn_weights_body, layer, orders),
        f"ffn_weights_{layer}",
        [],
        adds={(f"{n}{i}", layer): shape for i in range(2) for n in ("sent", "kept")},
        here=True,
        vmem=3,
    )


def attention_backward_body(
    layer, v, own_ref, other_ref, gain_ref, gain_grad_ref, *refs
):
    parts, (ds_ref, dkey_ref, dval_ref, dqt_ref) = refs[:PARTS], refs[PARTS:]
    grad_ref, mid_ref = v["grad", layer], v["middle", layer]
    wo_ref, wq_ref, wk_ref, wv_ref = (v[n, layer] for n in ("out", "query", "key", "value"))
    q_ref, k_ref, v_ref, p_ref, linv_ref = (v[n, layer] for n in ("q", "k", "v", "p", "linv"))
    mid_grad_ref, low_ref = v["mid_grad", layer], v["low_attn", layer]
    dq_ref, dk_ref, dv_ref = (v[n, layer] for n in ("dq", "dk", "dv"))
    incoming = own_ref[...].astype(F32) + other_ref[...].astype(F32)
    moved, gain_grad_ref[...] = norm_backward(mid_ref[...], gain_ref[layer : layer + 1], incoming)
    mid_grad = grad_ref[...] + moved
    mid_grad_ref[...] = mid_grad
    low_ref[...] = mid_grad.astype(BF16)
    heads = q_ref.shape[1] // HD
    mixed_turned = dot_nt(wo_ref[...], low_ref[...])
    spread = []
    for h in range(heads):
        spread.append(
            mixed_turned[h * HD : (h + 1) * HD]
            * jnp.concatenate(
                [linv_ref[b : b + 1, h * HALF : (h + 1) * HALF] for b in range(2)], axis=1
            )
        )
    dmixed = jnp.transpose(jnp.concatenate(spread, axis=0)).astype(BF16)
    queries = q_ref[...]
    key_turned = jnp.transpose(k_ref[...].astype(F32)).astype(BF16)
    for block in range(2):
        grads = heads_stacked(dmixed, block * HALF)
        stacked = heads_stacked(queries, block * HALF)
        first_key = 0 if block == 0 else MEM
        rows = KEYS_LOW if block == 0 else SEG
        first_row = 0 if block == 0 else KEYS_LOW
        inner = None
        dprobs = []
        for chunk in range(rows // HALF):
            key = first_key + chunk * HALF
            row = first_row + chunk * HALF
            dprob = dot_nt(v_ref[key : key + HALF], grads)
            dprobs.append(dprob)
            part = jnp.sum(p_ref[row : row + HALF].astype(F32) * dprob, axis=0, keepdims=True)
            inner = part if inner is None else inner + part
        inner = inner * linv_ref[block : block + 1]
        for chunk in range(rows // HALF):
            key = first_key + chunk * HALF
            row = first_row + chunk * HALF
            prob = p_ref[row : row + HALF]
            dscore = (prob.astype(F32) * (dprobs[chunk] - inner)).astype(BF16)
            ds_ref[chunk * HALF : (chunk + 1) * HALF] = dscore
            dkey = dot(dscore, stacked)
            dval = dot(prob, grads)
            if block == 1 and key < MEM + HALF:
                dkey = dkey + dkey_ref[key : key + HALF]
                dval = dval + dval_ref[key : key + HALF]
            dkey_ref[key : key + HALF] = dkey
            dval_ref[key : key + HALF] = dval
        for h in range(heads):
            dqt_ref[h * HD : (h + 1) * HD, block * HALF : (block + 1) * HALF] = dot(
                key_turned[h * HD : (h + 1) * HD, first_key : first_key + rows],
                ds_ref[:rows, h * HALF : (h + 1) * HALF],
            )
    dq_ref[...] = (jnp.transpose(dqt_ref[...]) * (1.0 / math.sqrt(HD))).astype(BF16)
    dk_ref[...] = dkey_ref[...].astype(BF16)
    dv_ref[...] = dval_ref[...].astype(BF16)
    step = SEG // PARTS
    for part_ref, row in zip(parts, range(0, SEG, step)):
        rows, seg_rows = pl.ds(row, step), pl.ds(MEM + row, step)
        part_ref[...] = (
            dot_nt(dk_ref[seg_rows], wk_ref[...])
            + dot_nt(dv_ref[seg_rows], wv_ref[...])
            + dot_nt(dq_ref[rows], wq_ref[...])
        ).astype(part_ref.dtype)


def attention_backward(vault, layer, own, other, gain):
    kept = vault.arrays
    q, k, val = kept["q", layer].shape, kept["k", layer].shape, kept["v", layer].shape
    width = q[1]
    heads = width // HD
    return chain_call(
        vault,
        functools.partial(attention_backward_body, layer),
        f"attention_backward_{layer}",
        [((1, D), F32)] + [((SEG // PARTS, D), BF16)] * PARTS,
        own,
        other,
        gain,
        adds={
            ("mid_grad", layer): ((SEG, D), F32),
            ("low_attn", layer): ((SEG, D), BF16),
            ("dq", layer): (q, BF16),
            ("dk", layer): (k, BF16),
            ("dv", layer): (val, BF16),
        },
        scratch=[
            pltpu.VMEM((KEYS_LOW, heads * HALF), BF16),
            pltpu.VMEM(k, F32),
            pltpu.VMEM(val, F32),
            pltpu.VMEM((width, SEG), F32),
        ],
        vmem=7,
    )


def attention_weights_body(layer, orders, v, where_ref, part_ref):
    nm_ref, dq_ref, dk_ref, dv_ref, mt_ref, low_ref = (
        v[n, layer] for n in ("nm", "dq", "dk", "dv", "mt", "low_attn")
    )
    width = dq_ref.shape[1]
    rows = D // 2
    for out, half in halves_of(v, layer, 0, orders, where_ref):
        cols = pl.ds(pl.multiple_of(half * rows, rows), rows)
        out[2, :, :width] = dot_tn(nm_ref[MEM:, cols], dq_ref[...]).astype(BF16)
        out[2, :, width:] = dot_tn(nm_ref[:, cols], dk_ref[...]).astype(BF16)
    for out, half in halves_of(v, layer, 1, orders, where_ref):

        @pl.when(half == 0)
        def _():
            for part in range(2):
                out[2, :, part * width : (part + 1) * width] = dot_tn(
                    nm_ref[:, part * rows : (part + 1) * rows], dv_ref[...]
                ).astype(BF16)

        @pl.when(half == 1)
        def _():
            out[2] = dot(mt_ref[...], low_ref[...]).astype(BF16)

    part_ref[...] = (dot_nt(dk_ref[:MEM], v["key", layer][...]) + dot_nt(dv_ref[:MEM], v["value", layer][...])).astype(
        part_ref.dtype
    )


def attention_weights(vault, layer, orders):
    width = vault.arrays["dq", layer].shape[1]
    assert D == 2 * width
    return chain_call(
        vault,
        functools.partial(attention_weights_body, layer, orders),
        f"attention_weights_{layer}",
        [((MEM, D), BF16)],
        here=True,
        vmem=4,
    )[0]


def finish_body(v, where_ref, *refs):
    own_ref, other_ref, part_ref, part_other, gain_ref, gain_attn_1, gain_ffn_0, gain_ffn_1, gate_own, gate_other = refs[:10]
    rest = refs[10 : 10 + 2 * LAYERS]
    out_ref, grad_ref, mem_grad_out, small_ref, mem_grad_ref, semaphores = refs[10 + 2 * LAYERS :]
    copies = []
    core = where_ref[1]
    out_ref[pl.ds(pl.multiple_of(core * HALF, HALF), HALF), :] = own_ref[...]
    out_ref[pl.ds(pl.multiple_of((1 - core) * HALF, HALF), HALF), :] = other_ref[...]
    send(out_ref)
    incoming = part_ref[...].astype(F32) + part_other[...].astype(F32)
    moved, gain_part = norm_backward(v["x"][...].astype(F32), gain_ref[:1], incoming)
    grad_ref[...] = v["mid_grad", 0][...] + moved
    send(grad_ref)
    small_ref[...] = jnp.zeros_like(small_ref)
    for i, row in enumerate((gain_ffn_0[...], gain_ffn_1[...], gate_own[...] + gate_other[...])):
        small_ref[LAYERS + i : LAYERS + i + 1] = row
    for l in range(LAYERS):
        own, other = rest[2 * l : 2 * l + 2]
        incoming = own[...].astype(F32) + other[...].astype(F32)
        mem_grad_ref[l], gain_mem = norm_backward(v["memory", l][...].astype(F32), gain_ref[l : l + 1], incoming)
        small_ref[l : l + 1] = gain_mem + (gain_part if l == 0 else gain_attn_1[...])
        copies.append(pltpu.make_async_copy(mem_grad_ref.at[l], mem_grad_out.at[l], semaphores.at[l]))
        copies[-1].start()
    for copy in copies:
        copy.wait()


def finish_rows(vault, *operands):
    return chain_call(
        vault,
        finish_body,
        "finish_rows",
        [((SEG, D), F32, HBM), ((SEG, D), F32, HBM), ((LAYERS, MEM, D), F32, RAW), ((8, D), F32)],
        *operands,
        scratch=[pltpu.VMEM((LAYERS, MEM, D), F32), pltpu.SemaphoreType.DMA((LAYERS,))],
        here=True,
        vmem=8,
    )


def other_core(values):
    return lax.ppermute(values, "mp", [(0, 1), (1, 0)])


def other_core_split(parts):
    return Split([other_core(part) for part in parts])


def tie_split(split, *values):
    held = tie(*split.parts, *values)
    return (Split(list(held[: len(split.parts)])),) + tuple(held[len(split.parts) :])


def partner(values, bits):
    size = lax.axis_size("dp")
    pairs = [(2 * i + core, 2 * (i ^ (1 << bits[core])) + core) for i in range(size) for core in range(2)]
    return lax.ppermute(values, ("dp", "mp"), pairs)


def add_low(left, right):
    return (left.astype(F32) + right.astype(F32)).astype(BF16)


def fold_body(kept_name, bit, v, where_ref, *refs):
    come, out = refs[0], refs[-1]
    kept = v[kept_name]
    if bit is not None:
        half = come.shape[1] // 2
        mine = side_of(where_ref, bit)
        other, own = pl.ds((1 - mine) * half, half), pl.ds(mine * half, half)
        out[...] = add_low(kept[:, other], come[:, other])
        kept[:, :half] = add_low(kept[:, own], come[:, own])
        return
    total = add_low(kept[:, :1], come[...])
    if len(refs) == 2:
        out[...] = total
        return
    small = refs[1]
    rows, cols = kept.shape[2:]
    out[...] = jnp.zeros(out.shape, BF16)
    out[:, :, :, :cols] = total
    wide = D // 128
    for j in range(SMALL * wide):
        lane = cols + j // rows * 128
        out[0, 0, j % rows : j % rows + 1, lane : lane + 128] = small[
            j // wide : j // wide + 1, j % wide * 128 : (j % wide + 1) * 128
        ].astype(BF16)


def small_lanes(rows):
    return -(-SMALL * (D // 128) // rows) * 128


def fold(vault, name, kept_name, bit, come, small):
    kinds, pieces, rows, cols = come.shape
    if small is not None:
        cols += small_lanes(rows)
    return chain_call(
        vault,
        functools.partial(fold_body, kept_name, bit),
        name,
        [((kinds, 1 if bit is None else pieces // 2, rows, cols), BF16)],
        come,
        *([] if small is None else [small]),
        here=True,
        vmem=4,
        flops=SUM_FLOPS,
    )[0]


def join_body(bit, where_ref, mine_ref, other_ref, out_ref):
    pieces = mine_ref.shape[1]
    mine = side_of(where_ref, bit)
    out_ref[:, pl.ds(mine * pieces, pieces)] = mine_ref[...]
    out_ref[:, pl.ds((1 - mine) * pieces, pieces)] = other_ref[...]


def join(name, bit, mine, other):
    kinds, pieces, rows, cols = mine.shape
    return kernel_call(
        functools.partial(join_body, bit),
        name,
        [((kinds, 2 * pieces, rows, cols), BF16)],
        mine,
        other,
        here=True,
        vmem=4,
        flops=SUM_FLOPS,
    )[0]


def place_body(place, layer, bit, turned, fresh, small, where_ref, ref, *refs):
    if small:
        mine_ref, refs = refs[0], refs[1:]
    refs = refs if fresh else refs[3:]
    outs, refs = refs[:3], refs[3:]
    if small:
        small_ref, refs = refs[0], refs[1:]
    buffers, semaphores = refs[:3], refs[3]
    side = side_of(where_ref, bit) ^ turned
    pieces = ref.shape[1]
    width = D // 2
    at = pl.ds(side * pieces, pieces)
    copies = []

    def put(buffer, target, number):
        copy = pltpu.make_async_copy(buffer, target, semaphores.at[number])
        copy.start()
        return copy

    if place == 0:
        up, q, k = buffers
        for j in range(2):
            up[:, :, j * D : (j + 1) * D] = ref[j, :, :, :D].astype(F32)
        copies.append(put(up, outs[0].at[layer, at], 0))
        q[...] = ref[2, :, :, :width].astype(F32)
        copies.append(put(q, outs[1].at[layer, at], 1))
        k[...] = ref[2, :, :, width:D].astype(F32)
        copies.append(put(k, outs[2].at[layer, at], 2))
    else:
        down, val, out = buffers
        for j in range(2):
            down[j] = ref[j, :, :, :D].astype(F32)
            copies.append(put(down.at[j], outs[0].at[layer, j, at], j))

        @pl.when(side == 0)
        def _():
            for j in range(2):
                val[j] = ref[2, :, :, j * width : (j + 1) * width].astype(F32)
            put(val, outs[1].at[layer], 2).wait()

        @pl.when(side == 1)
        def _():
            out[...] = ref[2, :, :, :D].astype(F32)
            put(out, outs[2].at[layer], 2).wait()

    if small:
        rows, wide = ref.shape[2], D // 128
        total = jnp.sum(ref[0, :, :, D:].astype(F32), axis=0) + jnp.sum(mine_ref[0, :, :, D:].astype(F32), axis=0)
        for j in range(SMALL * wide):
            lane = j // rows * 128
            small_ref[j // wide : j // wide + 1, j % wide * 128 : (j % wide + 1) * 128] = total[
                j % rows : j % rows + 1, lane : lane + 128
            ]
    for copy in copies:
        copy.wait()


def place(place_index, layer, bit, turned, values, mine, totals):
    kinds, pieces, rows, cols = values.shape
    small = turned == 1 and cols > D
    if place_index == 0:
        shapes = [(2 * pieces, rows, 2 * D), (2 * pieces, rows, D // 2), (2 * pieces, rows, D // 2)]
        held = [(pieces, rows, 2 * D), (pieces, rows, D // 2), (pieces, rows, D // 2)]
    else:
        shapes = [(2, 2 * pieces, rows, D), (2, pieces, rows, D // 2), (pieces, rows, D)]
        held = [(2, pieces, rows, D), (2, pieces, rows, D // 2), (pieces, rows, D)]
    first = 2 if small else 1
    return kernel_call(
        functools.partial(place_body, place_index, layer, bit, turned, totals is None, small),
        f"place{place_index}_{layer}_{'other' if turned else 'mine'}",
        [((LAYERS,) + shape, F32, RAW) for shape in shapes] + ([((8, D), F32)] if small else []),
        values,
        *([mine] if small else []),
        *([] if totals is None else [Slow(t, RAW) for t in totals]),
        here=True,
        scratch=[pltpu.VMEM(shape, F32) for shape in held] + [pltpu.SemaphoreType.DMA((3,))],
        aliases=None if totals is None else {first + i: i for i in range(3)},
        vmem=6,
        flops=SUM_FLOPS,
    )


def in_pieces(values, size):
    kinds, rows, cols = values.shape
    return values.reshape(kinds, size // 2, 2 * rows // size, cols)


def tie(*values):
    return lax.optimization_barrier(values)


class Stream:
    def __init__(self, vault, layer, place_index, order, sent):
        self.vault, self.layer, self.place, self.order = vault, layer, place_index, order
        self.come = partner(sent, order[0])
        self.pieces = None
        self.step = 0

    def advance(self, after, small=None):
        steps = len(self.order)
        self.step += 1
        s = self.step
        name = f"sum{self.place}_{self.layer}_step{s}"
        kept_name = (f"kept{self.place}", self.layer)
        if s <= steps:
            come, after = tie(self.come, after)
            bit = None if s == steps else self.order[s]
            out = fold(self.vault, name, kept_name, bit, come, small if s == steps else None)
            at = min(s, steps - 1)
            if s == steps:
                self.vault.drop(kept_name)
        else:
            at = 2 * steps - s - 1
            come, after = tie(self.come, after)
            out = join(name, self.order[at + 1], self.pieces, come)
        if s >= steps:
            self.pieces = out
        self.come = partner(out, self.order[at])
        return out

    def settle(self, turned, totals, after):
        values, after = tie(self.come if turned else self.pieces, after)
        return place(self.place, self.layer, self.order[0], turned, values, self.pieces, totals)


def local(
    layer_input, memory, doc_lengths, neighbour_owner, neighbour_row, table, gain_attn, w_query, w_key, w_value,
    w_out, gain_ffn, w_up, w_down, w_gate, cotangent,
):
    size = lax.axis_size("dp")
    bits_count = size.bit_length() - 1
    rest = list(range(3, bits_count))
    plans = (
        (((2, 0, 1), (0, 1, 2)), ((2, 0, 1), (1, 2, 0))),
        (((0, 1, 2), (2, 0, 1)), ((2, 1, 0), (1, 0, 2))),
    )
    orders = tuple(tuple(list(zip(*plan)) + [(bit, bit) for bit in rest] for plan in pair) for pair in plans)
    x = layer_input[0]

    half = size // 2
    turned = half == 8
    far_own = partner(own_rows(table), (bits_count - 1, bits_count - 1))
    wanted, ranks = build_requests(neighbour_owner[0].T, neighbour_row[0].T, size, turned)
    capacity = wanted.shape[2] // 2
    halves = [list(range(half)), list(range(half, size))]

    def exchange(values):
        return lax.all_to_all(values, "dp", split_axis=0, concat_axis=0, tiled=True, axis_index_groups=halves)

    asked, x = tie(exchange(wanted), x)
    vault = Vault()
    stacks = (w_query, w_key, w_value, w_out, w_up, w_down, memory[:, 0], x, cotangent[0], table)
    names = ("query", "key", "value", "out", "up", "down", "memory")
    sources = [("x", 7, None)] + [((n, l), i, l) for l in range(LAYERS) for i, n in enumerate(names)] + [("cot", 8, None), ("table", 9, None)]
    load(vault, stacks, sources)
    parts = ()
    for l in range(LAYERS):
        part = attention_forward(vault, l, doc_lengths, parts, gain_attn)
        if l == 0:
            part, asked, far_own = tie(part, asked, far_own)
            answers = answer_requests(vault, asked, far_own, other_core(far_own), turned)
            vault.drop("table")
            part, *answers = tie(part, *answers)
            if turned:
                near = [
                    lax.ppermute(a, ("dp", "mp"), [(2 * i + c, 2 * (i ^ m[c]) + c) for i in range(size) for c in range(2)])
                    for a, m in zip(answers, MASKS)
                ]
        if l == 1 and turned:
            part, near[3] = tie(part, near[3])
        ffn_part = ffn_forward(vault, l, part, other_core(part), gain_ffn)
        if l == 0 and turned:
            ffn_part, *near[:3] = tie(ffn_part, *near[:3])
        parts = (ffn_part, other_core(ffn_part))
    if not turned:
        near = [exchange(answers[0]).reshape(-1, D)]
    near = near + [other_core(a) for a in near]

    final, grad, gate_part = retrieval(vault, *parts, w_gate[None], Slow(ranks), near, capacity, size)
    vault.drop("cot")
    incoming = (grad, other_core(grad))
    memory_parts = []
    gain_attn_1 = None
    gains_ffn = [None] * LAYERS
    streams = {}
    for l in range(LAYERS - 1, -1, -1):
        part = ffn_backward(vault, l, incoming)
        if l < LAYERS - 1:
            gain_attn_1, *part = part
            vault.drop(("hidden", l + 1), ("mid_grad", l + 1))
        vault.drop(("slope", l))
        part_other = other_core_split(part)
        ffn_weights(vault, l, orders[l])
        vault.drop(*((n, l) for n in ("nf", "dpre", "act", "low", "up", "down")))
        gains_ffn[l], *part = attention_backward(vault, l, Split(part), part_other, gain_ffn)
        vault.drop(*((n, l) for n in ("q", "k", "v", "p", "linv", "grad", "middle", "out", "query")))
        part_other = other_core_split(part)
        mem_part = attention_weights(vault, l, orders[l])
        vault.drop(*((n, l) for n in ("nm", "dq", "dk", "dv", "mt", "low_attn", "key", "value")))
        for i in range(2):
            vault.arrays[f"kept{i}", l] = in_pieces(vault.arrays[f"kept{i}", l], size)
            sent = in_pieces(vault.arrays.pop((f"sent{i}", l)), size)
            streams[l, i] = Stream(vault, l, i, orders[l][i], sent)
        part_other, mem_part = tie_split(part_other, mem_part)
        memory_parts = [mem_part, other_core(mem_part)] + memory_parts
        incoming = (Split(part), part_other, gain_attn)
    last = 2 * bits_count - 1
    lag = {(1, 1): 0.29, (1, 0): 0.11, (0, 0): 2.33, (0, 1): 2.18}
    events = sorted((s + lag[key], key) for key in streams for s in range(1, last + 1))
    after, small = mem_part, None
    totals = [None, None]

    def settle(key, turned, after):
        result = streams[key].settle(turned, totals[key[1]], after)
        totals[key[1]] = result[:3]
        return result

    ended = []
    for count, (_, key) in enumerate(events):
        if count == 2:
            gate_part, final, after = tie(gate_part, final, after)
            layer_output, input_grad, memory_grad, small = finish_rows(
                vault, final, other_core(final), *incoming[:2], gain_attn, gain_attn_1, *gains_ffn,
                gate_part, other_core(gate_part), *memory_parts,
            )
            vault.drop("x", ("mid_grad", 0), *(("memory", l) for l in range(LAYERS)))
            after = small
        stream = streams[key]
        after = stream.advance(after, small if key == (1, 1) else None)
        if stream.step == last:
            after = settle(key, 0, after)[0]
            ended.append(key)
    for key in ended:
        result = settle(key, 1, after)
        after = result[0]
        if len(result) > 3:
            small = result[3]
    (up, wq, wk), (down, wv, wo) = totals
    up = up.reshape(LAYERS, D, -1)
    down = down.reshape(LAYERS, -1, D)
    width = wq.shape[-1]
    return (
        layer_output[None],
        input_grad[None],
        memory_grad[:, None],
        small[:LAYERS],
        wq.reshape(LAYERS, D, width),
        wk.reshape(LAYERS, D, width),
        wv.reshape(LAYERS, D, width),
        wo.reshape(LAYERS, width, D),
        small[LAYERS : 2 * LAYERS],
        up,
        down,
        small[2 * LAYERS],
    )


def solution(mesh):
    return jax.shard_map(
        local,
        mesh=mesh,
        in_specs=(
            P("dp", None, None),
            P(None, "dp", None, None),
            P("dp", None),
            P("dp", None, None),
            P("dp", None, None),
            P("dp", None),
            P(),
            P(None, None, "mp"),
            P(None, None, "mp"),
            P(None, None, "mp"),
            P(None, "mp", None),
            P(),
            P(None, None, "mp"),
            P(None, "mp", None),
            P(),
            P("dp", None, None),
        ),
        out_specs=(
            P("dp", None, None),
            P("dp", None, None),
            P(None, "dp", None, None),
            P(),
            P(None, None, "mp"),
            P(None, None, "mp"),
            P(None, None, "mp"),
            P(None, "mp", None),
            P(),
            P(None, None, "mp"),
            P(None, "mp", None),
            P(),
        ),
        check_vma=False,
    )
```

```python
import functools
import math

import jax
import jax.numpy as jnp
from jax import lax
from jax.experimental import pallas as pl
from jax.experimental.pallas import tpu as pltpu
from jax.sharding import PartitionSpec as P

D = 512
HD = 64
SEG = 512
MEM = 512
LAYERS = 2
NEIGHBOURS = 4
HALF = SEG // 2
KEYS_LOW = MEM + HALF
NORM_EPS = 1e-05
MASKED = -1e30
PARTS = 2
SPARE = 16
MASKS = ((1, 6), (2, 5), (4, 3), (7, 0))
SUM_FLOPS = 2_000_000_000
SMALL = 2 * LAYERS + 1
BF16 = jnp.bfloat16
F32 = jnp.float32
HBM, RAW, KEEP = "hbm", "raw", "keep"


def dot(left, right):
    return lax.dot_general(left, right, (((1,), (0,)), ((), ())), preferred_element_type=F32)


def dot_nt(left, right):
    return lax.dot_general(left, right, (((1,), (1,)), ((), ())), preferred_element_type=F32)


def dot_tn(left, right):
    return lax.dot_general(left, right, (((0,), (0,)), ((), ())), preferred_element_type=F32)


class Fetched:
    def __init__(self, source, buffer, semaphore):
        self.buffer = buffer
        self.copy = pltpu.make_async_copy(source, buffer, semaphore)
        self.copy.start()
        self.waiting = True
        self.shape = buffer.shape
        self.dtype = buffer.dtype

    def arrive(self):
        if self.waiting:
            self.copy.wait()
            self.waiting = False

    def __getitem__(self, index):
        self.arrive()
        return self.buffer[index]


class Stored:
    def __init__(self, target, buffer, semaphore):
        self.buffer = buffer
        self.copy = pltpu.make_async_copy(buffer, target, semaphore)
        self.sent = False
        self.shape = buffer.shape
        self.dtype = buffer.dtype

    def __getitem__(self, index):
        return self.buffer[index]

    def __setitem__(self, index, values):
        self.buffer[index] = values

    def send(self):
        self.copy.start()
        self.sent = True


class Slow:
    def __init__(self, array, layer=None):
        self.array = array
        self.layer = layer
        self.shape = array.shape if layer is None else array.shape[1:]
        self.dtype = array.dtype


class Pinned:
    def __init__(self, array):
        self.array = array
        self.shape = array.shape
        self.dtype = array.dtype


class Split:
    def __init__(self, parts):
        self.parts = parts


class Rows:
    def __init__(self, refs):
        self.refs = refs

    def __getitem__(self, index):
        return jnp.concatenate([ref[...] for ref in self.refs], axis=0)


def placed(operand):
    if isinstance(operand, (Slow, Pinned)):
        space = pltpu.HBM if isinstance(operand, Slow) else pltpu.VMEM
        return pltpu.with_memory_space_constraint(operand.array, space)
    return operand


def send(*refs):
    for ref in refs:
        if isinstance(ref, Stored):
            ref.send()


class Here:
    def __getitem__(self, index):
        return lax.axis_index(("dp", "mp")[index])


class Vault:
    def __init__(self):
        self.arrays = {}

    def drop(self, *names):
        for name in names:
            del self.arrays[name]


def chain_call(vault, body, name, outs, *operands, adds=None, here=False, **options):
    adds = adds or {}
    scalars = len(options.get("scalars", ()))
    names = list(vault.arrays)
    given = sum(len(a.parts) if isinstance(a, Split) else 1 for a in operands)

    def whole(*refs):
        head, rest = refs[: scalars + len(operands)], refs[scalars + len(operands) + len(names) :]
        mine, kept = rest[: len(outs)], rest[len(outs) : len(outs) + len(names) + len(adds)]
        extra = rest[len(outs) + len(names) + len(adds) :]
        body(dict(zip(names + list(adds), kept)), *([Here()] if here else []), *head, *mine, *extra)

    results = kernel_call(
        whole,
        name,
        list(outs)
        + [(vault.arrays[n].shape, vault.arrays[n].dtype, KEEP) for n in names]
        + [(shape, kind, KEEP) for shape, kind in adds.values()],
        *operands,
        *[Pinned(vault.arrays[n]) for n in names],
        aliases={scalars + given + i: len(outs) + i for i in range(len(names))},
        **options,
    )
    vault.arrays = dict(zip(names + list(adds), results[len(outs) :]))
    return results[: len(outs)]


def kernel_call(body, name, outs, *operands, scratch=(), scalars=(), aliases=None, vmem=4, flops=0, here=False):
    arrays, plan = [], []
    for operand in operands:
        parts = operand.parts if isinstance(operand, Split) else [operand]
        plan.append((operand, len(arrays), len(parts)))
        arrays.extend(parts)
    slow = [isinstance(a, Slow) for a in arrays]
    fetched = [s and a.layer != RAW for a, s in zip(arrays, slow)]
    spaces = [out[2] if len(out) > 2 else None for out in outs]
    stored = [space is HBM for space in spaces]
    specs = [pl.BlockSpec(memory_space=pltpu.SMEM)] * len(scalars)
    specs += [pl.BlockSpec(memory_space=pltpu.HBM if s else pltpu.VMEM) for s in slow]
    buffers = [pltpu.VMEM(a.shape, a.dtype) for a, f in zip(arrays, fetched) if f]
    buffers += [pltpu.VMEM(out[0], out[1]) for out, s in zip(outs, stored) if s]
    first = len(scalars)
    middle = first + len(arrays)
    last = middle + len(outs)

    def whole(*refs):
        held, extra = refs[last : last + len(buffers)], refs[last + len(buffers) :]
        semaphores = None
        if buffers:
            semaphores, extra = extra[0], extra[1:]
        count = 0
        ins, results = [], []
        for ref, array, f in zip(refs[first:middle], arrays, fetched):
            if f:
                source = ref if array.layer is None else ref.at[array.layer]
                ref = Fetched(source, held[count], semaphores.at[count])
                count += 1
            ins.append(ref)
        for ref, s in zip(refs[middle:last], stored):
            if s:
                ref = Stored(ref, held[count], semaphores.at[count])
                count += 1
            results.append(ref)
        given = [Rows(ins[at : at + n]) if isinstance(op, Split) else ins[at] for op, at, n in plan]
        body(*([Here()] if here else []), *refs[:first], *given, *results, *extra)
        for ref in ins:
            if isinstance(ref, Fetched):
                ref.arrive()
        for ref in results:
            if isinstance(ref, Stored) and not ref.sent:
                ref.send()
        for ref in results:
            if isinstance(ref, Stored):
                ref.copy.wait()

    return pl.pallas_call(
        whole,
        out_shape=[
            jax.ShapeDtypeStruct(out[0], out[1])
            if space is None
            else (pltpu.VMEM if space is KEEP else pltpu.HBM)(out[0], out[1])
            for out, space in zip(outs, spaces)
        ],
        in_specs=specs,
        out_specs=[pl.BlockSpec(memory_space=pltpu.HBM if space in (HBM, RAW) else pltpu.VMEM) for space in spaces],
        scratch_shapes=(buffers + [pltpu.SemaphoreType.DMA((len(buffers),))] if buffers else []) + list(scratch),
        input_output_aliases=aliases or {},
        compiler_params=pltpu.CompilerParams(vmem_limit_bytes=vmem * 1024 * 1024),
        cost_estimate=pl.CostEstimate(flops=flops, bytes_accessed=1000, transcendentals=0),
        name=name,
    )(*scalars, *[placed(a) for a in arrays])


def norm_parts(values):
    average = jnp.mean(values, axis=-1, keepdims=True)
    centred = values - average
    inverse = lax.rsqrt(jnp.mean(centred * centred, axis=-1, keepdims=True) + NORM_EPS)
    return centred * inverse, inverse


def norm_backward(values, gain, grad):
    unit, inverse = norm_parts(values)
    scaled = grad * gain
    inner = jnp.mean(scaled * unit, axis=-1, keepdims=True)
    moved = inverse * (scaled - jnp.mean(scaled, axis=-1, keepdims=True) - unit * inner)
    return moved, jnp.sum(grad * unit, axis=0, keepdims=True)


def heads_stacked(values, first):
    rows = values[first : first + HALF]
    lanes = lax.broadcasted_iota(jnp.int32, rows.shape, 1) // HD
    heads = values.shape[1] // HD
    return jnp.concatenate(
        [jnp.where(lanes == h, rows, jnp.zeros_like(rows)) for h in range(heads)], axis=0
    )


def document_starts(lens_ref, first, heads):
    places = first + lax.broadcasted_iota(jnp.int32, (1, heads * HALF), 1) % HALF
    starts = jnp.zeros_like(places)
    end = 0
    for slot in range(lens_ref.shape[1]):
        end = end + lens_ref[0, slot]
        starts = jnp.where(places >= end, end, starts)
    return places, starts


def load_body(sources, v, *refs):
    semaphores = refs[-1]
    copies = []
    for i, (name, which, layer) in enumerate(sources):
        source = refs[which] if layer is None else refs[which].at[layer]
        copies.append(pltpu.make_async_copy(source, v[name], semaphores.at[i]))
        copies[-1].start()
    for copy in copies:
        copy.wait()


def load(vault, arrays, sources):
    adds = {}
    for name, which, layer in sources:
        shape = arrays[which].shape
        adds[name] = (shape if layer is None else shape[1:], arrays[which].dtype)
    chain_call(
        vault,
        functools.partial(load_body, sources),
        "load_weights",
        [],
        *[Slow(a, RAW) for a in arrays],
        adds=adds,
        scratch=[pltpu.SemaphoreType.DMA((len(sources),))],
    )


def attention_forward_body(layer, v, *refs):
    nm_ref, q_ref, k_ref, v_ref = v["nm", layer], v["q", layer], v["k", layer], v["v", layer]
    p_ref, linv_ref, mt_ref = v["p", layer], v["linv", layer], v["mt", layer]
    mem_ref = v["memory", layer]
    wq_ref, wk_ref, wv_ref, wo_ref = (v[n, layer] for n in ("query", "key", "value", "out"))
    if layer == 0:
        lens, gain_ref, part_ref, s_ref = refs
        hidden = v["x"][...].astype(F32)
    else:
        lens, own_ref, other_ref, gain_ref, part_ref, s_ref = refs
        hidden = v["middle", layer - 1][...] + (own_ref[...].astype(F32) + other_ref[...].astype(F32))
        v["hidden", layer][...] = hidden
    gain = gain_ref[layer : layer + 1]
    nm_ref[MEM:] = (norm_parts(hidden)[0] * gain).astype(BF16)
    nm_ref[:MEM] = (norm_parts(mem_ref[...].astype(F32))[0] * gain).astype(BF16)
    q_ref[...] = (dot(nm_ref[MEM:], wq_ref[...]).astype(BF16).astype(F32) * (1.0 / math.sqrt(HD))).astype(BF16)
    k_ref[...] = dot(nm_ref[...], wk_ref[...]).astype(BF16)
    value_rows = dot(nm_ref[...], wv_ref[...])
    v_ref[...] = value_rows.astype(BF16)
    value_turned = jnp.transpose(value_rows).astype(BF16)
    heads = q_ref.shape[1] // HD
    queries = q_ref[...]
    for block in range(2):
        places, starts = document_starts(lens, block * HALF, heads)
        stacked = heads_stacked(queries, block * HALF)
        first_key = 0 if block == 0 else MEM
        rows = KEYS_LOW if block == 0 else SEG
        top = None
        for chunk in range(rows // HALF):
            key = first_key + chunk * HALF
            scores = dot_nt(k_ref[key : key + HALF], stacked)
            if key < MEM:
                scores = scores + jnp.where(starts == 0, 0.0, MASKED)
            else:
                spots = key - MEM + lax.broadcasted_iota(jnp.int32, scores.shape, 0)
                seen = spots >= starts
                if key - MEM == block * HALF:
                    seen = seen & (spots <= places)
                scores = jnp.where(seen, scores, MASKED)
            s_ref[chunk * HALF : (chunk + 1) * HALF] = scores
            peak = jnp.max(scores, axis=0, keepdims=True)
            top = peak if top is None else jnp.maximum(top, peak)
        total = None
        first_row = 0 if block == 0 else KEYS_LOW
        for chunk in range(rows // HALF):
            weight = jnp.exp(s_ref[chunk * HALF : (chunk + 1) * HALF] - top)
            part = jnp.sum(weight, axis=0, keepdims=True)
            total = part if total is None else total + part
            p_ref[first_row + chunk * HALF : first_row + (chunk + 1) * HALF] = weight.astype(BF16)
        inverse = 1.0 / total
        linv_ref[block : block + 1] = inverse
        for h in range(heads):
            mixed = dot(
                value_turned[h * HD : (h + 1) * HD, first_key : first_key + rows],
                p_ref[first_row : first_row + rows, h * HALF : (h + 1) * HALF],
            )
            mt_ref[h * HD : (h + 1) * HD, block * HALF : (block + 1) * HALF] = (
                mixed * inverse[:, h * HALF : (h + 1) * HALF]
            ).astype(BF16)
    part_ref[...] = dot_tn(mt_ref[...], wo_ref[...]).astype(part_ref.dtype)


def attention_forward(vault, layer, lens, parts, gain):
    width = vault.arrays["query", layer].shape[1]
    heads = width // HD
    adds = {
        ("nm", layer): ((MEM + SEG, D), BF16),
        ("q", layer): ((SEG, width), BF16),
        ("k", layer): ((MEM + SEG, width), BF16),
        ("v", layer): ((MEM + SEG, width), BF16),
        ("p", layer): ((KEYS_LOW + SEG, heads * HALF), BF16),
        ("linv", layer): ((2, heads * HALF), F32),
        ("mt", layer): ((width, SEG), BF16),
    }
    if layer > 0:
        adds["hidden", layer] = ((SEG, D), F32)
    return chain_call(
        vault,
        functools.partial(attention_forward_body, layer),
        f"attention_forward_{layer}",
        [((SEG, D), BF16)],
        *parts,
        gain,
        adds=adds,
        scalars=(lens,),
        scratch=[pltpu.VMEM((KEYS_LOW, heads * HALF), F32)],
        vmem=5,
    )[0]


GELU_INNER = math.sqrt(2.0 / math.pi)
GELU_CUBE = 0.044715


def ffn_forward_body(layer, v, own_ref, other_ref, gain_ref, part_ref):
    x_ref = v["x"] if layer == 0 else v["hidden", layer]
    nf_ref, act_ref, slope_ref = v["nf", layer], v["act", layer], v["slope", layer]
    middle = x_ref[...].astype(F32) + (own_ref[...].astype(F32) + other_ref[...].astype(F32))
    v["middle", layer][...] = middle
    nf_ref[...] = (norm_parts(middle)[0] * gain_ref[layer : layer + 1]).astype(BF16)
    step = 128
    for row in range(0, SEG, step):
        rows = pl.ds(row, step)
        pre = dot(nf_ref[rows], v["up", layer][...])
        square = pre * pre
        bend = jnp.tanh(GELU_INNER * pre * (1.0 + GELU_CUBE * square))
        half = 0.5 * (1.0 + bend)
        act = (pre * half).astype(BF16)
        act_ref[rows] = act
        slope_ref[rows] = (
            half
            + (0.5 * GELU_INNER) * pre * (1.0 - bend * bend) * (1.0 + (3.0 * GELU_CUBE) * square)
        ).astype(BF16)
        part_ref[rows] = dot(act, v["down", layer][...]).astype(part_ref.dtype)


def ffn_forward(vault, layer, own, other, gain):
    units = vault.arrays["up", layer].shape[1]
    return chain_call(
        vault,
        functools.partial(ffn_forward_body, layer),
        f"ffn_forward_{layer}",
        [((SEG, D), BF16)],
        own,
        other,
        gain,
        adds={
            ("middle", layer): ((SEG, D), F32),
            ("nf", layer): ((SEG, D), BF16),
            ("act", layer): ((SEG, units), BF16),
            ("slope", layer): ((SEG, units), BF16),
        },
        vmem=3,
    )[0]


def requests_body(owners, turned, where_ref, owner_ref, row_ref, asked_ref, ranks_ref):
    half = owners // 2
    capacity = asked_ref.shape[2] // 2
    lanes, tokens = ranks_ref.shape[1], ranks_ref.shape[0]
    me = where_ref[0]
    names = owner_ref[...] ^ (me & half)
    spots = lax.broadcasted_iota(jnp.int32, (lanes, tokens), 0)
    hits = jnp.zeros((lanes, tokens), F32)
    for k in range(NEIGHBOURS):
        hits = hits + (names[k : k + 1] == spots).astype(F32)
    above = (
        lax.broadcasted_iota(jnp.int32, (tokens, tokens), 0)
        < lax.broadcasted_iota(jnp.int32, (tokens, tokens), 1)
    )
    ranks = dot(hits.astype(BF16), above.astype(F32).astype(BF16))
    slots = lax.broadcasted_iota(jnp.int32, (capacity, tokens), 0).astype(F32)
    high = jnp.zeros((lanes, capacity), F32)
    low = jnp.zeros((lanes, capacity), F32)
    kept = jnp.full((lanes, tokens), -1.0, F32)
    order = names ^ (me & (half - 1)) if turned else names
    for k in range(NEIGHBOURS):
        named = names[k : k + 1] == spots
        rank = jnp.sum(jnp.where(named, ranks, 0.0), axis=0, keepdims=True)
        kept = jnp.where(order[k : k + 1] == spots, rank, kept)
        taken = (slots == rank).astype(F32).astype(BF16)
        row = row_ref[k : k + 1]
        upper = row // 32
        high = high + dot_nt(jnp.where(named, upper.astype(F32), 0.0).astype(BF16), taken)
        low = low + dot_nt(jnp.where(named, (row - upper * 32).astype(F32), 0.0).astype(BF16), taken)
    ranks_ref[...] = jnp.transpose(kept).astype(BF16)
    asked = (high * 32.0 + low).astype(jnp.int32)
    asked_ref[:, 0, :capacity] = asked[:half]
    asked_ref[:, 0, capacity:] = asked[half : 2 * half]


def own_rows_body(where_ref, table_ref, out_ref, semaphore):
    rows = out_ref.shape[0]
    at = pl.ds(pl.multiple_of(where_ref[1] * rows, rows), rows)
    copy = pltpu.make_async_copy(table_ref.at[at], out_ref, semaphore)
    copy.start()
    copy.wait()


def own_rows(table):
    return kernel_call(
        own_rows_body,
        "own_rows",
        [((table.shape[0] // 2, table.shape[1]), BF16)],
        Slow(table, RAW),
        here=True,
        scratch=[pltpu.SemaphoreType.DMA],
    )[0]


def build_requests(neighbour_owner, neighbour_row, owners, turned):
    tokens = neighbour_owner.shape[1]
    capacity = 2 * NEIGHBOURS * tokens // owners
    lanes = -(-owners // 128) * 128
    return kernel_call(
        functools.partial(requests_body, owners, turned),
        "build_requests",
        [((owners // 2, 1, 2 * capacity), jnp.int32), ((tokens, lanes), BF16, HBM)],
        Slow(neighbour_owner),
        Slow(neighbour_row),
        here=True,
        vmem=4,
    )


def picked_rows(column, parts, core):
    total = None
    for i, ref in enumerate(parts):
        rows = ref.shape[0]
        base = 0 if len(parts) == 1 else (core if i == 0 else 1 - core) * rows
        spots = lax.broadcasted_iota(jnp.int32, (column.shape[0], rows), 1) + base
        found = dot((column == spots.astype(F32)).astype(F32).astype(BF16), ref[...])
        total = found if total is None else total + found
    return total.astype(BF16)


def answer_body(v, where_ref, asked_ref, far_own, far_other, *outs):
    blocks, _, width = asked_ref.shape
    capacity = width // 2
    me, core = where_ref[0], where_ref[1]
    asked = jnp.transpose(asked_ref[:, 0, :].astype(F32))
    near, far = (v["table"],), (far_own, far_other)
    if len(outs) > 1:
        columns = lax.broadcasted_iota(jnp.int32, asked.shape, 1)
        for out, masks in zip(outs, MASKS):
            source = (me & (blocks - 1)) ^ jnp.where(core == 0, masks[0], masks[1])
            column = jnp.sum(jnp.where(columns == source, asked, 0.0), axis=1, keepdims=True)
            out[:capacity] = picked_rows(column[:capacity], near, core)
            out[capacity:width] = picked_rows(column[capacity:], far, core)
            out[width:] = jnp.zeros((out.shape[0] - width, out.shape[1]), BF16)
        return
    for side, parts in enumerate((near, far)):

        @pl.when(core == side)
        def _():
            for block in range(blocks):
                column = asked[side * capacity : (side + 1) * capacity, block : block + 1]
                outs[0][block] = picked_rows(column, parts, core)


def answer_requests(vault, asked, far_own, far_other, turned):
    blocks, _, width = asked.shape
    cols = far_own.shape[1]
    return chain_call(
        vault,
        answer_body,
        "answer_requests",
        [((width + SPARE, cols), BF16)] * len(MASKS) if turned else [((blocks, width // 2, cols), BF16)],
        asked,
        far_own,
        far_other,
        here=True,
        vmem=6,
    )


def retrieval_body(capacity, owners, v, where_ref, own_ref, other_ref, gate_ref, ranks_ref, *refs):
    count = len(refs) - 5
    near = refs[:count]
    final_ref, grad_ref, gate_grad_ref, s_ref, g_ref = refs[count:]
    core = where_ref[1]
    mid_ref, cot_ref = v["middle", LAYERS - 1], v["cot"]
    rows = pl.ds(pl.multiple_of(core * HALF, HALF), HALF)
    hidden = mid_ref[rows, :] + (own_ref[rows, :].astype(F32) + other_ref[rows, :].astype(F32))
    low = hidden.astype(BF16)
    cot = cot_ref[rows, :]
    ranks = ranks_ref[rows, :]
    step = 512
    scale = 1.0 / math.sqrt(D)
    owner_lane = lax.broadcasted_iota(jnp.int32, (ranks.shape[1], step), 0)
    slot_lane = lax.broadcasted_iota(jnp.int32, (ranks.shape[1], step), 1)
    slot_rank = (lax.broadcasted_iota(jnp.int32, (HALF, step), 1) % capacity).astype(F32)
    blocks = [(i, first) for i in range(count) for first in range(0, near[i].shape[0] // step * step, step)]

    def named(i, first):
        here = i < count // 2
        if count > 2:
            masks = MASKS[i % (count // 2)]
            mask = jnp.where(core == 0, masks[0 if here else 1], masks[1 if here else 0])
            return mask + slot_lane // capacity * (owners // 2)
        return (slot_lane + first) // capacity + (core if here else 1 - core) * (owners // 2)

    pair = jnp.concatenate([low, cot], axis=0)
    top = jnp.full((HALF, 1), MASKED, F32)
    for number, (i, first) in enumerate(blocks):
        at = pl.ds(number * step, step)
        spread = (named(i, first) == owner_lane).astype(F32).astype(BF16)
        taken = dot(ranks, spread) == slot_rank
        both = dot_nt(pair, near[i][pl.ds(first, step)])
        scores = jnp.where(taken, both[:HALF] * scale, MASKED)
        top = jnp.maximum(top, jnp.max(scores, axis=1, keepdims=True))
        s_ref[:, at] = scores
        g_ref[:, at] = both[HALF:]
    total = jnp.zeros((HALF, 1), F32)
    inner = jnp.zeros((HALF, 1), F32)
    for number in range(len(blocks)):
        at = pl.ds(number * step, step)
        weight = jnp.exp(s_ref[:, at] - top)
        s_ref[:, at] = weight
        total = total + jnp.sum(weight, axis=1, keepdims=True)
        inner = inner + jnp.sum(weight * g_ref[:, at], axis=1, keepdims=True)
    inverse = 1.0 / total
    inner = inner * inverse
    gate = jax.nn.sigmoid(jnp.sum(hidden * gate_ref[...], axis=1, keepdims=True))
    slope_scale = gate * scale
    found = jnp.zeros((2 * HALF, D), F32)
    for number, (i, first) in enumerate(blocks):
        at = pl.ds(number * step, step)
        weight = s_ref[:, at] * inverse
        slope = weight * ((g_ref[:, at] - inner) * slope_scale)
        found += dot(jnp.concatenate([weight.astype(BF16), slope.astype(BF16)], axis=0), near[i][pl.ds(first, step)])
    pooled, back = found[:HALF], found[HALF:]
    cot = cot.astype(F32)
    away = pooled - hidden
    final_ref[...] = hidden + gate * away
    gate_grad = gate * (1.0 - gate) * jnp.sum(cot * away, axis=1, keepdims=True)
    gate_grad_ref[...] = jnp.sum(gate_grad * hidden, axis=0, keepdims=True)
    grad_ref[...] = (1.0 - gate) * cot + gate_grad * gate_ref[...] + back


def retrieval(vault, own, other, w_gate, ranks, near, capacity, owners):
    slots = sum(a.shape[0] // 512 * 512 for a in near)
    return chain_call(
        vault,
        functools.partial(retrieval_body, capacity, owners),
        "retrieval",
        [((HALF, D), F32), ((HALF, D), F32), ((1, D), F32)],
        own,
        other,
        w_gate,
        ranks,
        *near,
        here=True,
        scratch=[pltpu.VMEM((HALF, slots), F32), pltpu.VMEM((HALF, slots), F32)],
        vmem=13,
    )


def ffn_backward_body(layer, v, *refs):
    grad_ref, low_ref, dpre_ref = v["grad", layer], v["low", layer], v["dpre", layer]
    if layer == LAYERS - 1:
        where_ref, own_ref, other_ref = refs[:3]
        parts = refs[3:]
        core = where_ref[1]
        grad_ref[pl.ds(pl.multiple_of(core * HALF, HALF), HALF), :] = own_ref[...]
        grad_ref[pl.ds(pl.multiple_of((1 - core) * HALF, HALF), HALF), :] = other_ref[...]
        grad = grad_ref[...]
    else:
        own_ref, other_ref, gain_ref, gain_grad_ref = refs[:4]
        parts = refs[4:]
        incoming = own_ref[...].astype(F32) + other_ref[...].astype(F32)
        moved, gain_grad_ref[...] = norm_backward(v["hidden", layer + 1][...], gain_ref[layer + 1 : layer + 2], incoming)
        grad = v["mid_grad", layer + 1][...] + moved
        grad_ref[...] = grad
    low_ref[...] = grad.astype(BF16)
    step = SEG // PARTS
    for part_ref, row in zip(parts, range(0, SEG, step)):
        rows = pl.ds(row, step)
        dact = dot_nt(low_ref[rows], v["down", layer][...])
        dpre = (v["slope", layer][rows].astype(F32) * dact).astype(BF16)
        dpre_ref[rows] = dpre
        part_ref[...] = dot_nt(dpre, v["up", layer][...]).astype(part_ref.dtype)


def ffn_backward(vault, layer, incoming):
    units = vault.arrays["up", layer].shape[1]
    outs = [((SEG // PARTS, D), BF16)] * PARTS
    if layer < LAYERS - 1:
        outs = [((1, D), F32)] + outs
    return chain_call(
        vault,
        functools.partial(ffn_backward_body, layer),
        f"ffn_backward_{layer}",
        outs,
        *incoming,
        adds={
            ("grad", layer): ((SEG, D), F32),
            ("low", layer): ((SEG, D), BF16),
            ("dpre", layer): ((SEG, units), BF16),
        },
        here=layer == LAYERS - 1,
        vmem=3,
    )


def side_of(where_ref, bits):
    return (where_ref[0] >> jnp.where(where_ref[1] == 0, bits[0], bits[1])) & 1


def halves_of(v, layer, place, orders, where_ref):
    mine = side_of(where_ref, orders[place][0])
    return ((v[f"sent{place}", layer], 1 - mine), (v[f"kept{place}", layer], mine))


def ffn_weights_body(layer, orders, v, where_ref):
    nf_ref, dpre_ref, act_ref, low_ref = (v[n, layer] for n in ("nf", "dpre", "act", "low"))
    rows = D // 2
    for place in range(2):
        for out, half in halves_of(v, layer, place, orders, where_ref):
            if place == 0:
                left = nf_ref[:, pl.ds(pl.multiple_of(half * rows, rows), rows)]
                grads = dot_tn(left, dpre_ref[...]).astype(BF16)
                for j in range(2):
                    out[j] = grads[:, j * D : (j + 1) * D]
            else:
                for j in range(2):
                    left = act_ref[:, pl.ds(pl.multiple_of(j * D + half * rows, rows), rows)]
                    out[j] = dot_tn(left, low_ref[...]).astype(BF16)


def ffn_weights(vault, layer, orders):
    assert vault.arrays["act", layer].shape[1] == 2 * D
    shape = ((3, D // 2, D), BF16)
    chain_call(
        vault,
        functools.partial(ffn_weights_body, layer, orders),
        f"ffn_weights_{layer}",
        [],
        adds={(f"{n}{i}", layer): shape for i in range(2) for n in ("sent", "kept")},
        here=True,
        vmem=3,
    )


def attention_backward_body(
    layer, v, own_ref, other_ref, gain_ref, gain_grad_ref, *refs
):
    parts, (ds_ref, dkey_ref, dval_ref, dqt_ref) = refs[:PARTS], refs[PARTS:]
    grad_ref, mid_ref = v["grad", layer], v["middle", layer]
    wo_ref, wq_ref, wk_ref, wv_ref = (v[n, layer] for n in ("out", "query", "key", "value"))
    q_ref, k_ref, v_ref, p_ref, linv_ref = (v[n, layer] for n in ("q", "k", "v", "p", "linv"))
    mid_grad_ref, low_ref = v["mid_grad", layer], v["low_attn", layer]
    dq_ref, dk_ref, dv_ref = (v[n, layer] for n in ("dq", "dk", "dv"))
    incoming = own_ref[...].astype(F32) + other_ref[...].astype(F32)
    moved, gain_grad_ref[...] = norm_backward(mid_ref[...], gain_ref[layer : layer + 1], incoming)
    mid_grad = grad_ref[...] + moved
    mid_grad_ref[...] = mid_grad
    low_ref[...] = mid_grad.astype(BF16)
    heads = q_ref.shape[1] // HD
    mixed_turned = dot_nt(wo_ref[...], low_ref[...])
    spread = []
    for h in range(heads):
        spread.append(
            mixed_turned[h * HD : (h + 1) * HD]
            * jnp.concatenate(
                [linv_ref[b : b + 1, h * HALF : (h + 1) * HALF] for b in range(2)], axis=1
            )
        )
    dmixed = jnp.transpose(jnp.concatenate(spread, axis=0)).astype(BF16)
    queries = q_ref[...]
    key_turned = jnp.transpose(k_ref[...].astype(F32)).astype(BF16)
    for block in range(2):
        grads = heads_stacked(dmixed, block * HALF)
        stacked = heads_stacked(queries, block * HALF)
        first_key = 0 if block == 0 else MEM
        rows = KEYS_LOW if block == 0 else SEG
        first_row = 0 if block == 0 else KEYS_LOW
        inner = None
        dprobs = []
        for chunk in range(rows // HALF):
            key = first_key + chunk * HALF
            row = first_row + chunk * HALF
            dprob = dot_nt(v_ref[key : key + HALF], grads)
            dprobs.append(dprob)
            part = jnp.sum(p_ref[row : row + HALF].astype(F32) * dprob, axis=0, keepdims=True)
            inner = part if inner is None else inner + part
        inner = inner * linv_ref[block : block + 1]
        for chunk in range(rows // HALF):
            key = first_key + chunk * HALF
            row = first_row + chunk * HALF
            prob = p_ref[row : row + HALF]
            dscore = (prob.astype(F32) * (dprobs[chunk] - inner)).astype(BF16)
            ds_ref[chunk * HALF : (chunk + 1) * HALF] = dscore
            dkey = dot(dscore, stacked)
            dval = dot(prob, grads)
            if block == 1 and key < MEM + HALF:
                dkey = dkey + dkey_ref[key : key + HALF]
                dval = dval + dval_ref[key : key + HALF]
            dkey_ref[key : key + HALF] = dkey
            dval_ref[key : key + HALF] = dval
        for h in range(heads):
            dqt_ref[h * HD : (h + 1) * HD, block * HALF : (block + 1) * HALF] = dot(
                key_turned[h * HD : (h + 1) * HD, first_key : first_key + rows],
                ds_ref[:rows, h * HALF : (h + 1) * HALF],
            )
    dq_ref[...] = (jnp.transpose(dqt_ref[...]) * (1.0 / math.sqrt(HD))).astype(BF16)
    dk_ref[...] = dkey_ref[...].astype(BF16)
    dv_ref[...] = dval_ref[...].astype(BF16)
    step = SEG // PARTS
    for part_ref, row in zip(parts, range(0, SEG, step)):
        rows, seg_rows = pl.ds(row, step), pl.ds(MEM + row, step)
        part_ref[...] = (
            dot_nt(dk_ref[seg_rows], wk_ref[...])
            + dot_nt(dv_ref[seg_rows], wv_ref[...])
            + dot_nt(dq_ref[rows], wq_ref[...])
        ).astype(part_ref.dtype)


def attention_backward(vault, layer, own, other, gain):
    kept = vault.arrays
    q, k, val = kept["q", layer].shape, kept["k", layer].shape, kept["v", layer].shape
    width = q[1]
    heads = width // HD
    return chain_call(
        vault,
        functools.partial(attention_backward_body, layer),
        f"attention_backward_{layer}",
        [((1, D), F32)] + [((SEG // PARTS, D), BF16)] * PARTS,
        own,
        other,
        gain,
        adds={
            ("mid_grad", layer): ((SEG, D), F32),
            ("low_attn", layer): ((SEG, D), BF16),
            ("dq", layer): (q, BF16),
            ("dk", layer): (k, BF16),
            ("dv", layer): (val, BF16),
        },
        scratch=[
            pltpu.VMEM((KEYS_LOW, heads * HALF), BF16),
            pltpu.VMEM(k, F32),
            pltpu.VMEM(val, F32),
            pltpu.VMEM((width, SEG), F32),
        ],
        vmem=7,
    )


def attention_weights_body(layer, orders, v, where_ref, part_ref):
    nm_ref, dq_ref, dk_ref, dv_ref, mt_ref, low_ref = (
        v[n, layer] for n in ("nm", "dq", "dk", "dv", "mt", "low_attn")
    )
    width = dq_ref.shape[1]
    rows = D // 2
    for out, half in halves_of(v, layer, 0, orders, where_ref):
        cols = pl.ds(pl.multiple_of(half * rows, rows), rows)
        out[2, :, :width] = dot_tn(nm_ref[MEM:, cols], dq_ref[...]).astype(BF16)
        out[2, :, width:] = dot_tn(nm_ref[:, cols], dk_ref[...]).astype(BF16)
    for out, half in halves_of(v, layer, 1, orders, where_ref):

        @pl.when(half == 0)
        def _():
            for part in range(2):
                out[2, :, part * width : (part + 1) * width] = dot_tn(
                    nm_ref[:, part * rows : (part + 1) * rows], dv_ref[...]
                ).astype(BF16)

        @pl.when(half == 1)
        def _():
            out[2] = dot(mt_ref[...], low_ref[...]).astype(BF16)

    part_ref[...] = (dot_nt(dk_ref[:MEM], v["key", layer][...]) + dot_nt(dv_ref[:MEM], v["value", layer][...])).astype(
        part_ref.dtype
    )


def attention_weights(vault, layer, orders):
    width = vault.arrays["dq", layer].shape[1]
    assert D == 2 * width
    return chain_call(
        vault,
        functools.partial(attention_weights_body, layer, orders),
        f"attention_weights_{layer}",
        [((MEM, D), BF16)],
        here=True,
        vmem=4,
    )[0]


def finish_body(v, where_ref, *refs):
    own_ref, other_ref, part_ref, part_other, gain_ref, gain_attn_1, gain_ffn_0, gain_ffn_1, gate_own, gate_other = refs[:10]
    rest = refs[10 : 10 + 2 * LAYERS]
    out_ref, grad_ref, mem_grad_out, small_ref, mem_grad_ref, semaphores = refs[10 + 2 * LAYERS :]
    copies = []
    core = where_ref[1]
    out_ref[pl.ds(pl.multiple_of(core * HALF, HALF), HALF), :] = own_ref[...]
    out_ref[pl.ds(pl.multiple_of((1 - core) * HALF, HALF), HALF), :] = other_ref[...]
    send(out_ref)
    incoming = part_ref[...].astype(F32) + part_other[...].astype(F32)
    moved, gain_part = norm_backward(v["x"][...].astype(F32), gain_ref[:1], incoming)
    grad_ref[...] = v["mid_grad", 0][...] + moved
    send(grad_ref)
    small_ref[...] = jnp.zeros_like(small_ref)
    for i, row in enumerate((gain_ffn_0[...], gain_ffn_1[...], gate_own[...] + gate_other[...])):
        small_ref[LAYERS + i : LAYERS + i + 1] = row
    for l in range(LAYERS):
        own, other = rest[2 * l : 2 * l + 2]
        incoming = own[...].astype(F32) + other[...].astype(F32)
        mem_grad_ref[l], gain_mem = norm_backward(v["memory", l][...].astype(F32), gain_ref[l : l + 1], incoming)
        small_ref[l : l + 1] = gain_mem + (gain_part if l == 0 else gain_attn_1[...])
        copies.append(pltpu.make_async_copy(mem_grad_ref.at[l], mem_grad_out.at[l], semaphores.at[l]))
        copies[-1].start()
    for copy in copies:
        copy.wait()


def finish_rows(vault, *operands):
    return chain_call(
        vault,
        finish_body,
        "finish_rows",
        [((SEG, D), F32, HBM), ((SEG, D), F32, HBM), ((LAYERS, MEM, D), F32, RAW), ((8, D), F32)],
        *operands,
        scratch=[pltpu.VMEM((LAYERS, MEM, D), F32), pltpu.SemaphoreType.DMA((LAYERS,))],
        here=True,
        vmem=8,
    )


def other_core(values):
    return lax.ppermute(values, "mp", [(0, 1), (1, 0)])


def other_core_split(parts):
    return Split([other_core(part) for part in parts])


def tie_split(split, *values):
    held = tie(*split.parts, *values)
    return (Split(list(held[: len(split.parts)])),) + tuple(held[len(split.parts) :])


def partner(values, bits):
    size = lax.axis_size("dp")
    pairs = [(2 * i + core, 2 * (i ^ (1 << bits[core])) + core) for i in range(size) for core in range(2)]
    return lax.ppermute(values, ("dp", "mp"), pairs)


def add_low(left, right):
    return (left.astype(F32) + right.astype(F32)).astype(BF16)


def fold_body(kept_name, bit, v, where_ref, *refs):
    come, out = refs[0], refs[-1]
    kept = v[kept_name]
    if bit is not None:
        half = come.shape[1] // 2
        mine = side_of(where_ref, bit)
        other, own = pl.ds((1 - mine) * half, half), pl.ds(mine * half, half)
        out[...] = add_low(kept[:, other], come[:, other])
        kept[:, :half] = add_low(kept[:, own], come[:, own])
        return
    total = add_low(kept[:, :1], come[...])
    if len(refs) == 2:
        out[...] = total
        return
    small = refs[1]
    rows, cols = kept.shape[2:]
    out[...] = jnp.zeros(out.shape, BF16)
    out[:, :, :, :cols] = total
    wide = D // 128
    for j in range(SMALL * wide):
        lane = cols + j // rows * 128
        out[0, 0, j % rows : j % rows + 1, lane : lane + 128] = small[
            j // wide : j // wide + 1, j % wide * 128 : (j % wide + 1) * 128
        ].astype(BF16)


def small_lanes(rows):
    return -(-SMALL * (D // 128) // rows) * 128


def fold(vault, name, kept_name, bit, come, small):
    kinds, pieces, rows, cols = come.shape
    if small is not None:
        cols += small_lanes(rows)
    return chain_call(
        vault,
        functools.partial(fold_body, kept_name, bit),
        name,
        [((kinds, 1 if bit is None else pieces // 2, rows, cols), BF16)],
        come,
        *([] if small is None else [small]),
        here=True,
        vmem=4,
        flops=SUM_FLOPS,
    )[0]


def join_body(bit, where_ref, mine_ref, other_ref, out_ref):
    pieces = mine_ref.shape[1]
    mine = side_of(where_ref, bit)
    out_ref[:, pl.ds(mine * pieces, pieces)] = mine_ref[...]
    out_ref[:, pl.ds((1 - mine) * pieces, pieces)] = other_ref[...]


def join(name, bit, mine, other):
    kinds, pieces, rows, cols = mine.shape
    return kernel_call(
        functools.partial(join_body, bit),
        name,
        [((kinds, 2 * pieces, rows, cols), BF16)],
        mine,
        other,
        here=True,
        vmem=4,
        flops=SUM_FLOPS,
    )[0]


def place_body(place, layer, bit, turned, fresh, small, where_ref, ref, *refs):
    if small:
        mine_ref, refs = refs[0], refs[1:]
    refs = refs if fresh else refs[3:]
    outs, refs = refs[:3], refs[3:]
    if small:
        small_ref, refs = refs[0], refs[1:]
    buffers, semaphores = refs[:3], refs[3]
    side = side_of(where_ref, bit) ^ turned
    pieces = ref.shape[1]
    width = D // 2
    at = pl.ds(side * pieces, pieces)
    copies = []

    def put(buffer, target, number):
        copy = pltpu.make_async_copy(buffer, target, semaphores.at[number])
        copy.start()
        return copy

    if place == 0:
        up, q, k = buffers
        for j in range(2):
            up[:, :, j * D : (j + 1) * D] = ref[j, :, :, :D].astype(F32)
        copies.append(put(up, outs[0].at[layer, at], 0))
        q[...] = ref[2, :, :, :width].astype(F32)
        copies.append(put(q, outs[1].at[layer, at], 1))
        k[...] = ref[2, :, :, width:D].astype(F32)
        copies.append(put(k, outs[2].at[layer, at], 2))
    else:
        down, val, out = buffers
        for j in range(2):
            down[j] = ref[j, :, :, :D].astype(F32)
            copies.append(put(down.at[j], outs[0].at[layer, j, at], j))

        @pl.when(side == 0)
        def _():
            for j in range(2):
                val[j] = ref[2, :, :, j * width : (j + 1) * width].astype(F32)
            put(val, outs[1].at[layer], 2).wait()

        @pl.when(side == 1)
        def _():
            out[...] = ref[2, :, :, :D].astype(F32)
            put(out, outs[2].at[layer], 2).wait()

    if small:
        rows, wide = ref.shape[2], D // 128
        total = jnp.sum(ref[0, :, :, D:].astype(F32), axis=0) + jnp.sum(mine_ref[0, :, :, D:].astype(F32), axis=0)
        for j in range(SMALL * wide):
            lane = j // rows * 128
            small_ref[j // wide : j // wide + 1, j % wide * 128 : (j % wide + 1) * 128] = total[
                j % rows : j % rows + 1, lane : lane + 128
            ]
    for copy in copies:
        copy.wait()


def place(place_index, layer, bit, turned, values, mine, totals):
    kinds, pieces, rows, cols = values.shape
    small = turned == 1 and cols > D
    if place_index == 0:
        shapes = [(2 * pieces, rows, 2 * D), (2 * pieces, rows, D // 2), (2 * pieces, rows, D // 2)]
        held = [(pieces, rows, 2 * D), (pieces, rows, D // 2), (pieces, rows, D // 2)]
    else:
        shapes = [(2, 2 * pieces, rows, D), (2, pieces, rows, D // 2), (pieces, rows, D)]
        held = [(2, pieces, rows, D), (2, pieces, rows, D // 2), (pieces, rows, D)]
    first = 2 if small else 1
    return kernel_call(
        functools.partial(place_body, place_index, layer, bit, turned, totals is None, small),
        f"place{place_index}_{layer}_{'other' if turned else 'mine'}",
        [((LAYERS,) + shape, F32, RAW) for shape in shapes] + ([((8, D), F32)] if small else []),
        values,
        *([mine] if small else []),
        *([] if totals is None else [Slow(t, RAW) for t in totals]),
        here=True,
        scratch=[pltpu.VMEM(shape, F32) for shape in held] + [pltpu.SemaphoreType.DMA((3,))],
        aliases=None if totals is None else {first + i: i for i in range(3)},
        vmem=6,
        flops=SUM_FLOPS,
    )


def in_pieces(values, size):
    kinds, rows, cols = values.shape
    return values.reshape(kinds, size // 2, 2 * rows // size, cols)


def tie(*values):
    return lax.optimization_barrier(values)


class Stream:
    def __init__(self, vault, layer, place_index, order, sent):
        self.vault, self.layer, self.place, self.order = vault, layer, place_index, order
        self.come = partner(sent, order[0])
        self.pieces = None
        self.step = 0

    def advance(self, after, small=None):
        steps = len(self.order)
        self.step += 1
        s = self.step
        name = f"sum{self.place}_{self.layer}_step{s}"
        kept_name = (f"kept{self.place}", self.layer)
        if s <= steps:
            come, after = tie(self.come, after)
            bit = None if s == steps else self.order[s]
            out = fold(self.vault, name, kept_name, bit, come, small if s == steps else None)
            at = min(s, steps - 1)
            if s == steps:
                self.vault.drop(kept_name)
        else:
            at = 2 * steps - s - 1
            come, after = tie(self.come, after)
            out = join(name, self.order[at + 1], self.pieces, come)
        if s >= steps:
            self.pieces = out
        self.come = partner(out, self.order[at])
        return out

    def settle(self, turned, totals, after):
        values, after = tie(self.come if turned else self.pieces, after)
        return place(self.place, self.layer, self.order[0], turned, values, self.pieces, totals)


def local(
    layer_input, memory, doc_lengths, neighbour_owner, neighbour_row, table, gain_attn, w_query, w_key, w_value,
    w_out, gain_ffn, w_up, w_down, w_gate, cotangent,
):
    size = lax.axis_size("dp")
    bits_count = size.bit_length() - 1
    rest = list(range(3, bits_count))
    plans = (
        (((2, 0, 1), (0, 1, 2)), ((2, 0, 1), (1, 2, 0))),
        (((0, 1, 2), (2, 0, 1)), ((2, 1, 0), (1, 0, 2))),
    )
    orders = tuple(tuple(list(zip(*plan)) + [(bit, bit) for bit in rest] for plan in pair) for pair in plans)
    x = layer_input[0]

    half = size // 2
    turned = half == 8
    far_own = partner(own_rows(table), (bits_count - 1, bits_count - 1))
    wanted, ranks = build_requests(neighbour_owner[0].T, neighbour_row[0].T, size, turned)
    capacity = wanted.shape[2] // 2
    halves = [list(range(half)), list(range(half, size))]

    def exchange(values):
        return lax.all_to_all(values, "dp", split_axis=0, concat_axis=0, tiled=True, axis_index_groups=halves)

    asked, x = tie(exchange(wanted), x)
    vault = Vault()
    stacks = (w_query, w_key, w_value, w_out, w_up, w_down, memory[:, 0], x, cotangent[0], table)
    names = ("query", "key", "value", "out", "up", "down", "memory")
    sources = [("x", 7, None)] + [((n, l), i, l) for l in range(LAYERS) for i, n in enumerate(names)] + [("cot", 8, None), ("table", 9, None)]
    load(vault, stacks, sources)
    parts = ()
    for l in range(LAYERS):
        part = attention_forward(vault, l, doc_lengths, parts, gain_attn)
        if l == 0:
            part, asked, far_own = tie(part, asked, far_own)
            answers = answer_requests(vault, asked, far_own, other_core(far_own), turned)
            vault.drop("table")
            part, *answers = tie(part, *answers)
            if turned:
                near = [
                    lax.ppermute(a, ("dp", "mp"), [(2 * i + c, 2 * (i ^ m[c]) + c) for i in range(size) for c in range(2)])
                    for a, m in zip(answers, MASKS)
                ]
        if l == 1 and turned:
            part, *near[:3] = tie(part, *near[:3])
        ffn_part = ffn_forward(vault, l, part, other_core(part), gain_ffn)
        if l == 1 and turned:
            ffn_part, near[3] = tie(ffn_part, near[3])
        parts = (ffn_part, other_core(ffn_part))
    if not turned:
        near = [exchange(answers[0]).reshape(-1, D)]
    near = near + [other_core(a) for a in near]

    final, grad, gate_part = retrieval(vault, *parts, w_gate[None], Slow(ranks), near, capacity, size)
    vault.drop("cot")
    incoming = (grad, other_core(grad))
    memory_parts = []
    gain_attn_1 = None
    gains_ffn = [None] * LAYERS
    streams = {}
    for l in range(LAYERS - 1, -1, -1):
        part = ffn_backward(vault, l, incoming)
        if l < LAYERS - 1:
            gain_attn_1, *part = part
            vault.drop(("hidden", l + 1), ("mid_grad", l + 1))
        vault.drop(("slope", l))
        part_other = other_core_split(part)
        ffn_weights(vault, l, orders[l])
        vault.drop(*((n, l) for n in ("nf", "dpre", "act", "low", "up", "down")))
        gains_ffn[l], *part = attention_backward(vault, l, Split(part), part_other, gain_ffn)
        vault.drop(*((n, l) for n in ("q", "k", "v", "p", "linv", "grad", "middle", "out", "query")))
        part_other = other_core_split(part)
        mem_part = attention_weights(vault, l, orders[l])
        vault.drop(*((n, l) for n in ("nm", "dq", "dk", "dv", "mt", "low_attn", "key", "value")))
        for i in range(2):
            vault.arrays[f"kept{i}", l] = in_pieces(vault.arrays[f"kept{i}", l], size)
            sent = in_pieces(vault.arrays.pop((f"sent{i}", l)), size)
            streams[l, i] = Stream(vault, l, i, orders[l][i], sent)
        part_other, mem_part = tie_split(part_other, mem_part)
        memory_parts = [mem_part, other_core(mem_part)] + memory_parts
        incoming = (Split(part), part_other, gain_attn)
    last = 2 * bits_count - 1
    lag = {(1, 1): 0.29, (1, 0): 0.11, (0, 0): 2.33, (0, 1): 2.18}
    events = sorted((s + lag[key], key) for key in streams for s in range(1, last + 1))
    after, small = mem_part, None
    totals = [None, None]

    def settle(key, turned, after):
        result = streams[key].settle(turned, totals[key[1]], after)
        totals[key[1]] = result[:3]
        return result

    ended = []
    for count, (_, key) in enumerate(events):
        if count == 2:
            gate_part, final, after = tie(gate_part, final, after)
            layer_output, input_grad, memory_grad, small = finish_rows(
                vault, final, other_core(final), *incoming[:2], gain_attn, gain_attn_1, *gains_ffn,
                gate_part, other_core(gate_part), *memory_parts,
            )
            vault.drop("x", ("mid_grad", 0), *(("memory", l) for l in range(LAYERS)))
            after = small
        stream = streams[key]
        after = stream.advance(after, small if key == (1, 1) else None)
        if stream.step == last:
            after = settle(key, 0, after)[0]
            ended.append(key)
    for key in ended:
        result = settle(key, 1, after)
        after = result[0]
        if len(result) > 3:
            small = result[3]
    (up, wq, wk), (down, wv, wo) = totals
    up = up.reshape(LAYERS, D, -1)
    down = down.reshape(LAYERS, -1, D)
    width = wq.shape[-1]
    return (
        layer_output[None],
        input_grad[None],
        memory_grad[:, None],
        small[:LAYERS],
        wq.reshape(LAYERS, D, width),
        wk.reshape(LAYERS, D, width),
        wv.reshape(LAYERS, D, width),
        wo.reshape(LAYERS, width, D),
        small[LAYERS : 2 * LAYERS],
        up,
        down,
        small[2 * LAYERS],
    )


def solution(mesh):
    return jax.shard_map(
        local,
        mesh=mesh,
        in_specs=(
            P("dp", None, None),
            P(None, "dp", None, None),
            P("dp", None),
            P("dp", None, None),
            P("dp", None, None),
            P("dp", None),
            P(),
            P(None, None, "mp"),
            P(None, None, "mp"),
            P(None, None, "mp"),
            P(None, "mp", None),
            P(),
            P(None, None, "mp"),
            P(None, "mp", None),
            P(),
            P("dp", None, None),
        ),
        out_specs=(
            P("dp", None, None),
            P("dp", None, None),
            P(None, "dp", None, None),
            P(),
            P(None, None, "mp"),
            P(None, None, "mp"),
            P(None, None, "mp"),
            P(None, "mp", None),
            P(),
            P(None, None, "mp"),
            P(None, "mp", None),
            P(),
        ),
        check_vma=False,
    )
```

```python
import functools
import math

import jax
import jax.numpy as jnp
from jax import lax
from jax.experimental import pallas as pl
from jax.experimental.pallas import tpu as pltpu
from jax.sharding import PartitionSpec as P

D = 512
HD = 64
SEG = 512
MEM = 512
LAYERS = 2
NEIGHBOURS = 4
HALF = SEG // 2
KEYS_LOW = MEM + HALF
NORM_EPS = 1e-05
MASKED = -1e30
PARTS = 2
SPARE = 16
MASKS = ((1, 6), (2, 5), (4, 3), (7, 0))
SUM_FLOPS = 2_000_000_000
SMALL = 2 * LAYERS + 1
BF16 = jnp.bfloat16
F32 = jnp.float32
HBM, RAW, KEEP = "hbm", "raw", "keep"


def dot(left, right):
    return lax.dot_general(left, right, (((1,), (0,)), ((), ())), preferred_element_type=F32)


def dot_nt(left, right):
    return lax.dot_general(left, right, (((1,), (1,)), ((), ())), preferred_element_type=F32)


def dot_tn(left, right):
    return lax.dot_general(left, right, (((0,), (0,)), ((), ())), preferred_element_type=F32)


class Fetched:
    def __init__(self, source, buffer, semaphore):
        self.buffer = buffer
        self.copy = pltpu.make_async_copy(source, buffer, semaphore)
        self.copy.start()
        self.waiting = True
        self.shape = buffer.shape
        self.dtype = buffer.dtype

    def arrive(self):
        if self.waiting:
            self.copy.wait()
            self.waiting = False

    def __getitem__(self, index):
        self.arrive()
        return self.buffer[index]


class Stored:
    def __init__(self, target, buffer, semaphore):
        self.buffer = buffer
        self.copy = pltpu.make_async_copy(buffer, target, semaphore)
        self.sent = False
        self.shape = buffer.shape
        self.dtype = buffer.dtype

    def __getitem__(self, index):
        return self.buffer[index]

    def __setitem__(self, index, values):
        self.buffer[index] = values

    def send(self):
        self.copy.start()
        self.sent = True


class Slow:
    def __init__(self, array, layer=None):
        self.array = array
        self.layer = layer
        self.shape = array.shape if layer is None else array.shape[1:]
        self.dtype = array.dtype


class Pinned:
    def __init__(self, array):
        self.array = array
        self.shape = array.shape
        self.dtype = array.dtype


class Split:
    def __init__(self, parts):
        self.parts = parts


class Rows:
    def __init__(self, refs):
        self.refs = refs

    def __getitem__(self, index):
        return jnp.concatenate([ref[...] for ref in self.refs], axis=0)


def placed(operand):
    if isinstance(operand, (Slow, Pinned)):
        space = pltpu.HBM if isinstance(operand, Slow) else pltpu.VMEM
        return pltpu.with_memory_space_constraint(operand.array, space)
    return operand


def send(*refs):
    for ref in refs:
        if isinstance(ref, Stored):
            ref.send()


class Here:
    def __getitem__(self, index):
        return lax.axis_index(("dp", "mp")[index])


class Vault:
    def __init__(self):
        self.arrays = {}

    def drop(self, *names):
        for name in names:
            del self.arrays[name]


def chain_call(vault, body, name, outs, *operands, adds=None, here=False, **options):
    adds = adds or {}
    scalars = len(options.get("scalars", ()))
    names = list(vault.arrays)
    given = sum(len(a.parts) if isinstance(a, Split) else 1 for a in operands)

    def whole(*refs):
        head, rest = refs[: scalars + len(operands)], refs[scalars + len(operands) + len(names) :]
        mine, kept = rest[: len(outs)], rest[len(outs) : len(outs) + len(names) + len(adds)]
        extra = rest[len(outs) + len(names) + len(adds) :]
        body(dict(zip(names + list(adds), kept)), *([Here()] if here else []), *head, *mine, *extra)

    results = kernel_call(
        whole,
        name,
        list(outs)
        + [(vault.arrays[n].shape, vault.arrays[n].dtype, KEEP) for n in names]
        + [(shape, kind, KEEP) for shape, kind in adds.values()],
        *operands,
        *[Pinned(vault.arrays[n]) for n in names],
        aliases={scalars + given + i: len(outs) + i for i in range(len(names))},
        **options,
    )
    vault.arrays = dict(zip(names + list(adds), results[len(outs) :]))
    return results[: len(outs)]


def kernel_call(body, name, outs, *operands, scratch=(), scalars=(), aliases=None, vmem=4, flops=0, here=False):
    arrays, plan = [], []
    for operand in operands:
        parts = operand.parts if isinstance(operand, Split) else [operand]
        plan.append((operand, len(arrays), len(parts)))
        arrays.extend(parts)
    slow = [isinstance(a, Slow) for a in arrays]
    fetched = [s and a.layer != RAW for a, s in zip(arrays, slow)]
    spaces = [out[2] if len(out) > 2 else None for out in outs]
    stored = [space is HBM for space in spaces]
    specs = [pl.BlockSpec(memory_space=pltpu.SMEM)] * len(scalars)
    specs += [pl.BlockSpec(memory_space=pltpu.HBM if s else pltpu.VMEM) for s in slow]
    buffers = [pltpu.VMEM(a.shape, a.dtype) for a, f in zip(arrays, fetched) if f]
    buffers += [pltpu.VMEM(out[0], out[1]) for out, s in zip(outs, stored) if s]
    first = len(scalars)
    middle = first + len(arrays)
    last = middle + len(outs)

    def whole(*refs):
        held, extra = refs[last : last + len(buffers)], refs[last + len(buffers) :]
        semaphores = None
        if buffers:
            semaphores, extra = extra[0], extra[1:]
        count = 0
        ins, results = [], []
        for ref, array, f in zip(refs[first:middle], arrays, fetched):
            if f:
                source = ref if array.layer is None else ref.at[array.layer]
                ref = Fetched(source, held[count], semaphores.at[count])
                count += 1
            ins.append(ref)
        for ref, s in zip(refs[middle:last], stored):
            if s:
                ref = Stored(ref, held[count], semaphores.at[count])
                count += 1
            results.append(ref)
        given = [Rows(ins[at : at + n]) if isinstance(op, Split) else ins[at] for op, at, n in plan]
        body(*([Here()] if here else []), *refs[:first], *given, *results, *extra)
        for ref in ins:
            if isinstance(ref, Fetched):
                ref.arrive()
        for ref in results:
            if isinstance(ref, Stored) and not ref.sent:
                ref.send()
        for ref in results:
            if isinstance(ref, Stored):
                ref.copy.wait()

    return pl.pallas_call(
        whole,
        out_shape=[
            jax.ShapeDtypeStruct(out[0], out[1])
            if space is None
            else (pltpu.VMEM if space is KEEP else pltpu.HBM)(out[0], out[1])
            for out, space in zip(outs, spaces)
        ],
        in_specs=specs,
        out_specs=[pl.BlockSpec(memory_space=pltpu.HBM if space in (HBM, RAW) else pltpu.VMEM) for space in spaces],
        scratch_shapes=(buffers + [pltpu.SemaphoreType.DMA((len(buffers),))] if buffers else []) + list(scratch),
        input_output_aliases=aliases or {},
        compiler_params=pltpu.CompilerParams(vmem_limit_bytes=vmem * 1024 * 1024),
        cost_estimate=pl.CostEstimate(flops=flops, bytes_accessed=1000, transcendentals=0),
        name=name,
    )(*scalars, *[placed(a) for a in arrays])


def norm_parts(values):
    average = jnp.mean(values, axis=-1, keepdims=True)
    centred = values - average
    inverse = lax.rsqrt(jnp.mean(centred * centred, axis=-1, keepdims=True) + NORM_EPS)
    return centred * inverse, inverse


def norm_backward(values, gain, grad):
    unit, inverse = norm_parts(values)
    scaled = grad * gain
    inner = jnp.mean(scaled * unit, axis=-1, keepdims=True)
    moved = inverse * (scaled - jnp.mean(scaled, axis=-1, keepdims=True) - unit * inner)
    return moved, jnp.sum(grad * unit, axis=0, keepdims=True)


def heads_stacked(values, first):
    rows = values[first : first + HALF]
    lanes = lax.broadcasted_iota(jnp.int32, rows.shape, 1) // HD
    heads = values.shape[1] // HD
    return jnp.concatenate(
        [jnp.where(lanes == h, rows, jnp.zeros_like(rows)) for h in range(heads)], axis=0
    )


def document_starts(lens_ref, first, heads):
    places = first + lax.broadcasted_iota(jnp.int32, (1, heads * HALF), 1) % HALF
    starts = jnp.zeros_like(places)
    end = 0
    for slot in range(lens_ref.shape[1]):
        end = end + lens_ref[0, slot]
        starts = jnp.where(places >= end, end, starts)
    return places, starts


def load_body(sources, v, *refs):
    semaphores = refs[-1]
    copies = []
    for i, (name, which, layer) in enumerate(sources):
        source = refs[which] if layer is None else refs[which].at[layer]
        copies.append(pltpu.make_async_copy(source, v[name], semaphores.at[i]))
        copies[-1].start()
    for copy in copies:
        copy.wait()


def load(vault, arrays, sources):
    adds = {}
    for name, which, layer in sources:
        shape = arrays[which].shape
        adds[name] = (shape if layer is None else shape[1:], arrays[which].dtype)
    chain_call(
        vault,
        functools.partial(load_body, sources),
        "load_weights",
        [],
        *[Slow(a, RAW) for a in arrays],
        adds=adds,
        scratch=[pltpu.SemaphoreType.DMA((len(sources),))],
    )


def attention_forward_body(layer, v, *refs):
    nm_ref, q_ref, k_ref, v_ref = v["nm", layer], v["q", layer], v["k", layer], v["v", layer]
    p_ref, linv_ref, mt_ref = v["p", layer], v["linv", layer], v["mt", layer]
    mem_ref = v["memory", layer]
    wq_ref, wk_ref, wv_ref, wo_ref = (v[n, layer] for n in ("query", "key", "value", "out"))
    if layer == 0:
        lens, gain_ref, part_ref, s_ref = refs
        hidden = v["x"][...].astype(F32)
    else:
        lens, own_ref, other_ref, gain_ref, part_ref, s_ref = refs
        hidden = v["middle", layer - 1][...] + (own_ref[...].astype(F32) + other_ref[...].astype(F32))
        v["hidden", layer][...] = hidden
    gain = gain_ref[layer : layer + 1]
    nm_ref[MEM:] = (norm_parts(hidden)[0] * gain).astype(BF16)
    nm_ref[:MEM] = (norm_parts(mem_ref[...].astype(F32))[0] * gain).astype(BF16)
    q_ref[...] = (dot(nm_ref[MEM:], wq_ref[...]).astype(BF16).astype(F32) * (1.0 / math.sqrt(HD))).astype(BF16)
    k_ref[...] = dot(nm_ref[...], wk_ref[...]).astype(BF16)
    value_rows = dot(nm_ref[...], wv_ref[...])
    v_ref[...] = value_rows.astype(BF16)
    value_turned = jnp.transpose(value_rows).astype(BF16)
    heads = q_ref.shape[1] // HD
    queries = q_ref[...]
    for block in range(2):
        places, starts = document_starts(lens, block * HALF, heads)
        stacked = heads_stacked(queries, block * HALF)
        first_key = 0 if block == 0 else MEM
        rows = KEYS_LOW if block == 0 else SEG
        top = None
        for chunk in range(rows // HALF):
            key = first_key + chunk * HALF
            scores = dot_nt(k_ref[key : key + HALF], stacked)
            if key < MEM:
                scores = scores + jnp.where(starts == 0, 0.0, MASKED)
            else:
                spots = key - MEM + lax.broadcasted_iota(jnp.int32, scores.shape, 0)
                seen = spots >= starts
                if key - MEM == block * HALF:
                    seen = seen & (spots <= places)
                scores = jnp.where(seen, scores, MASKED)
            s_ref[chunk * HALF : (chunk + 1) * HALF] = scores
            peak = jnp.max(scores, axis=0, keepdims=True)
            top = peak if top is None else jnp.maximum(top, peak)
        total = None
        first_row = 0 if block == 0 else KEYS_LOW
        for chunk in range(rows // HALF):
            weight = jnp.exp(s_ref[chunk * HALF : (chunk + 1) * HALF] - top)
            part = jnp.sum(weight, axis=0, keepdims=True)
            total = part if total is None else total + part
            p_ref[first_row + chunk * HALF : first_row + (chunk + 1) * HALF] = weight.astype(BF16)
        inverse = 1.0 / total
        linv_ref[block : block + 1] = inverse
        for h in range(heads):
            mixed = dot(
                value_turned[h * HD : (h + 1) * HD, first_key : first_key + rows],
                p_ref[first_row : first_row + rows, h * HALF : (h + 1) * HALF],
            )
            mt_ref[h * HD : (h + 1) * HD, block * HALF : (block + 1) * HALF] = (
                mixed * inverse[:, h * HALF : (h + 1) * HALF]
            ).astype(BF16)
    part_ref[...] = dot_tn(mt_ref[...], wo_ref[...]).astype(part_ref.dtype)


def attention_forward(vault, layer, lens, parts, gain):
    width = vault.arrays["query", layer].shape[1]
    heads = width // HD
    adds = {
        ("nm", layer): ((MEM + SEG, D), BF16),
        ("q", layer): ((SEG, width), BF16),
        ("k", layer): ((MEM + SEG, width), BF16),
        ("v", layer): ((MEM + SEG, width), BF16),
        ("p", layer): ((KEYS_LOW + SEG, heads * HALF), BF16),
        ("linv", layer): ((2, heads * HALF), F32),
        ("mt", layer): ((width, SEG), BF16),
    }
    if layer > 0:
        adds["hidden", layer] = ((SEG, D), F32)
    return chain_call(
        vault,
        functools.partial(attention_forward_body, layer),
        f"attention_forward_{layer}",
        [((SEG, D), BF16)],
        *parts,
        gain,
        adds=adds,
        scalars=(lens,),
        scratch=[pltpu.VMEM((KEYS_LOW, heads * HALF), F32)],
        vmem=5,
    )[0]


GELU_INNER = math.sqrt(2.0 / math.pi)
GELU_CUBE = 0.044715


def ffn_forward_body(layer, v, own_ref, other_ref, gain_ref, part_ref):
    x_ref = v["x"] if layer == 0 else v["hidden", layer]
    nf_ref, act_ref, slope_ref = v["nf", layer], v["act", layer], v["slope", layer]
    middle = x_ref[...].astype(F32) + (own_ref[...].astype(F32) + other_ref[...].astype(F32))
    v["middle", layer][...] = middle
    nf_ref[...] = (norm_parts(middle)[0] * gain_ref[layer : layer + 1]).astype(BF16)
    step = 128
    for row in range(0, SEG, step):
        rows = pl.ds(row, step)
        pre = dot(nf_ref[rows], v["up", layer][...])
        square = pre * pre
        bend = jnp.tanh(GELU_INNER * pre * (1.0 + GELU_CUBE * square))
        half = 0.5 * (1.0 + bend)
        act = (pre * half).astype(BF16)
        act_ref[rows] = act
        slope_ref[rows] = (
            half
            + (0.5 * GELU_INNER) * pre * (1.0 - bend * bend) * (1.0 + (3.0 * GELU_CUBE) * square)
        ).astype(BF16)
        part_ref[rows] = dot(act, v["down", layer][...]).astype(part_ref.dtype)


def ffn_forward(vault, layer, own, other, gain):
    units = vault.arrays["up", layer].shape[1]
    return chain_call(
        vault,
        functools.partial(ffn_forward_body, layer),
        f"ffn_forward_{layer}",
        [((SEG, D), BF16)],
        own,
        other,
        gain,
        adds={
            ("middle", layer): ((SEG, D), F32),
            ("nf", layer): ((SEG, D), BF16),
            ("act", layer): ((SEG, units), BF16),
            ("slope", layer): ((SEG, units), BF16),
        },
        vmem=3,
    )[0]


def requests_body(owners, turned, where_ref, owner_ref, row_ref, asked_ref, ranks_ref):
    half = owners // 2
    capacity = asked_ref.shape[2] // 2
    lanes, tokens = ranks_ref.shape[1], ranks_ref.shape[0]
    me = where_ref[0]
    names = owner_ref[...] ^ (me & half)
    spots = lax.broadcasted_iota(jnp.int32, (lanes, tokens), 0)
    hits = jnp.zeros((lanes, tokens), F32)
    for k in range(NEIGHBOURS):
        hits = hits + (names[k : k + 1] == spots).astype(F32)
    above = (
        lax.broadcasted_iota(jnp.int32, (tokens, tokens), 0)
        < lax.broadcasted_iota(jnp.int32, (tokens, tokens), 1)
    )
    ranks = dot(hits.astype(BF16), above.astype(F32).astype(BF16))
    slots = lax.broadcasted_iota(jnp.int32, (capacity, tokens), 0).astype(F32)
    high = jnp.zeros((lanes, capacity), F32)
    low = jnp.zeros((lanes, capacity), F32)
    kept = jnp.full((lanes, tokens), -1.0, F32)
    order = names ^ (me & (half - 1)) if turned else names
    for k in range(NEIGHBOURS):
        named = names[k : k + 1] == spots
        rank = jnp.sum(jnp.where(named, ranks, 0.0), axis=0, keepdims=True)
        kept = jnp.where(order[k : k + 1] == spots, rank, kept)
        taken = (slots == rank).astype(F32).astype(BF16)
        row = row_ref[k : k + 1]
        upper = row // 32
        high = high + dot_nt(jnp.where(named, upper.astype(F32), 0.0).astype(BF16), taken)
        low = low + dot_nt(jnp.where(named, (row - upper * 32).astype(F32), 0.0).astype(BF16), taken)
    ranks_ref[...] = jnp.transpose(kept).astype(BF16)
    asked = (high * 32.0 + low).astype(jnp.int32)
    asked_ref[:, 0, :capacity] = asked[:half]
    asked_ref[:, 0, capacity:] = asked[half : 2 * half]


def own_rows_body(where_ref, table_ref, out_ref, semaphore):
    rows = out_ref.shape[0]
    at = pl.ds(pl.multiple_of(where_ref[1] * rows, rows), rows)
    copy = pltpu.make_async_copy(table_ref.at[at], out_ref, semaphore)
    copy.start()
    copy.wait()


def own_rows(table):
    return kernel_call(
        own_rows_body,
        "own_rows",
        [((table.shape[0] // 2, table.shape[1]), BF16)],
        Slow(table, RAW),
        here=True,
        scratch=[pltpu.SemaphoreType.DMA],
    )[0]


def build_requests(neighbour_owner, neighbour_row, owners, turned):
    tokens = neighbour_owner.shape[1]
    capacity = 2 * NEIGHBOURS * tokens // owners
    lanes = -(-owners // 128) * 128
    return kernel_call(
        functools.partial(requests_body, owners, turned),
        "build_requests",
        [((owners // 2, 1, 2 * capacity), jnp.int32), ((tokens, lanes), BF16, HBM)],
        Slow(neighbour_owner),
        Slow(neighbour_row),
        here=True,
        vmem=4,
    )


def picked_rows(column, parts, core):
    total = None
    for i, ref in enumerate(parts):
        rows = ref.shape[0]
        base = 0 if len(parts) == 1 else (core if i == 0 else 1 - core) * rows
        spots = lax.broadcasted_iota(jnp.int32, (column.shape[0], rows), 1) + base
        found = dot((column == spots.astype(F32)).astype(F32).astype(BF16), ref[...])
        total = found if total is None else total + found
    return total.astype(BF16)


def answer_body(far, v, here, asked_ref, *parts):
    blocks, _, width = asked_ref.shape
    capacity = width // 2
    me, core = here[0], here[1]
    asked = jnp.transpose(asked_ref[:, 0, :].astype(F32))[far * capacity : (far + 1) * capacity]
    parts = parts if far else (v["table"],)
    if ("rows", 1) in v:
        columns = lax.broadcasted_iota(jnp.int32, asked.shape, 1)
        for j, masks in enumerate(MASKS):
            out = v["rows", j]
            source = (me & (blocks - 1)) ^ jnp.where(core == 0, masks[0], masks[1])
            column = jnp.sum(jnp.where(columns == source, asked, 0.0), axis=1, keepdims=True)
            out[far * capacity : (far + 1) * capacity] = picked_rows(column, parts, core)
            if far:
                out[width:] = jnp.zeros((out.shape[0] - width, out.shape[1]), BF16)
        return

    @pl.when(core == far)
    def _():
        for block in range(blocks):
            v["rows", 0][block] = picked_rows(asked[:, block : block + 1], parts, core)


def answer_requests(vault, far, asked, parts, turned):
    blocks, _, width = asked.shape
    cols = vault.arrays["table"].shape[1]
    adds = {}
    if not far:
        shapes = [(width + SPARE, cols)] * len(MASKS) if turned else [(blocks, width // 2, cols)]
        adds = {("rows", j): (shape, BF16) for j, shape in enumerate(shapes)}
    chain_call(
        vault,
        functools.partial(answer_body, far),
        "answer_far" if far else "answer_near",
        [],
        asked,
        *parts,
        adds=adds,
        here=True,
        vmem=6,
    )


def retrieval_body(capacity, owners, v, where_ref, own_ref, other_ref, gate_ref, ranks_ref, *refs):
    count = len(refs) - 5
    near = refs[:count]
    final_ref, grad_ref, gate_grad_ref, s_ref, g_ref = refs[count:]
    core = where_ref[1]
    mid_ref, cot_ref = v["middle", LAYERS - 1], v["cot"]
    rows = pl.ds(pl.multiple_of(core * HALF, HALF), HALF)
    hidden = mid_ref[rows, :] + (own_ref[rows, :].astype(F32) + other_ref[rows, :].astype(F32))
    low = hidden.astype(BF16)
    cot = cot_ref[rows, :]
    ranks = ranks_ref[rows, :]
    step = 512
    scale = 1.0 / math.sqrt(D)
    owner_lane = lax.broadcasted_iota(jnp.int32, (ranks.shape[1], step), 0)
    slot_lane = lax.broadcasted_iota(jnp.int32, (ranks.shape[1], step), 1)
    slot_rank = (lax.broadcasted_iota(jnp.int32, (HALF, step), 1) % capacity).astype(F32)
    blocks = [(i, first) for i in range(count) for first in range(0, near[i].shape[0] // step * step, step)]

    def named(i, first):
        here = i < count // 2
        if count > 2:
            masks = MASKS[i % (count // 2)]
            mask = jnp.where(core == 0, masks[0 if here else 1], masks[1 if here else 0])
            return mask + slot_lane // capacity * (owners // 2)
        return (slot_lane + first) // capacity + (core if here else 1 - core) * (owners // 2)

    pair = jnp.concatenate([low, cot], axis=0)
    top = jnp.full((HALF, 1), MASKED, F32)
    for number, (i, first) in enumerate(blocks):
        at = pl.ds(number * step, step)
        spread = (named(i, first) == owner_lane).astype(F32).astype(BF16)
        taken = dot(ranks, spread) == slot_rank
        both = dot_nt(pair, near[i][pl.ds(first, step)])
        scores = jnp.where(taken, both[:HALF] * scale, MASKED)
        top = jnp.maximum(top, jnp.max(scores, axis=1, keepdims=True))
        s_ref[:, at] = scores
        g_ref[:, at] = both[HALF:]
    total = jnp.zeros((HALF, 1), F32)
    inner = jnp.zeros((HALF, 1), F32)
    for number in range(len(blocks)):
        at = pl.ds(number * step, step)
        weight = jnp.exp(s_ref[:, at] - top)
        s_ref[:, at] = weight
        total = total + jnp.sum(weight, axis=1, keepdims=True)
        inner = inner + jnp.sum(weight * g_ref[:, at], axis=1, keepdims=True)
    inverse = 1.0 / total
    inner = inner * inverse
    gate = jax.nn.sigmoid(jnp.sum(hidden * gate_ref[...], axis=1, keepdims=True))
    slope_scale = gate * scale
    found = jnp.zeros((2 * HALF, D), F32)
    for number, (i, first) in enumerate(blocks):
        at = pl.ds(number * step, step)
        weight = s_ref[:, at] * inverse
        slope = weight * ((g_ref[:, at] - inner) * slope_scale)
        found += dot(jnp.concatenate([weight.astype(BF16), slope.astype(BF16)], axis=0), near[i][pl.ds(first, step)])
    pooled, back = found[:HALF], found[HALF:]
    cot = cot.astype(F32)
    away = pooled - hidden
    final_ref[...] = hidden + gate * away
    gate_grad = gate * (1.0 - gate) * jnp.sum(cot * away, axis=1, keepdims=True)
    gate_grad_ref[...] = jnp.sum(gate_grad * hidden, axis=0, keepdims=True)
    grad_ref[...] = (1.0 - gate) * cot + gate_grad * gate_ref[...] + back


def retrieval(vault, own, other, w_gate, ranks, near, capacity, owners):
    slots = sum(a.shape[0] // 512 * 512 for a in near)
    return chain_call(
        vault,
        functools.partial(retrieval_body, capacity, owners),
        "retrieval",
        [((HALF, D), F32), ((HALF, D), F32), ((1, D), F32)],
        own,
        other,
        w_gate,
        ranks,
        *near,
        here=True,
        scratch=[pltpu.VMEM((HALF, slots), F32), pltpu.VMEM((HALF, slots), F32)],
        vmem=13,
    )


def ffn_backward_body(layer, v, *refs):
    grad_ref, low_ref, dpre_ref = v["grad", layer], v["low", layer], v["dpre", layer]
    if layer == LAYERS - 1:
        where_ref, own_ref, other_ref = refs[:3]
        parts = refs[3:]
        core = where_ref[1]
        grad_ref[pl.ds(pl.multiple_of(core * HALF, HALF), HALF), :] = own_ref[...]
        grad_ref[pl.ds(pl.multiple_of((1 - core) * HALF, HALF), HALF), :] = other_ref[...]
        grad = grad_ref[...]
    else:
        own_ref, other_ref, gain_ref, gain_grad_ref = refs[:4]
        parts = refs[4:]
        incoming = own_ref[...].astype(F32) + other_ref[...].astype(F32)
        moved, gain_grad_ref[...] = norm_backward(v["hidden", layer + 1][...], gain_ref[layer + 1 : layer + 2], incoming)
        grad = v["mid_grad", layer + 1][...] + moved
        grad_ref[...] = grad
    low_ref[...] = grad.astype(BF16)
    step = SEG // PARTS
    for part_ref, row in zip(parts, range(0, SEG, step)):
        rows = pl.ds(row, step)
        dact = dot_nt(low_ref[rows], v["down", layer][...])
        dpre = (v["slope", layer][rows].astype(F32) * dact).astype(BF16)
        dpre_ref[rows] = dpre
        part_ref[...] = dot_nt(dpre, v["up", layer][...]).astype(part_ref.dtype)


def ffn_backward(vault, layer, incoming):
    units = vault.arrays["up", layer].shape[1]
    outs = [((SEG // PARTS, D), BF16)] * PARTS
    if layer < LAYERS - 1:
        outs = [((1, D), F32)] + outs
    return chain_call(
        vault,
        functools.partial(ffn_backward_body, layer),
        f"ffn_backward_{layer}",
        outs,
        *incoming,
        adds={
            ("grad", layer): ((SEG, D), F32),
            ("low", layer): ((SEG, D), BF16),
            ("dpre", layer): ((SEG, units), BF16),
        },
        here=layer == LAYERS - 1,
        vmem=3,
    )


def side_of(where_ref, bits):
    return (where_ref[0] >> jnp.where(where_ref[1] == 0, bits[0], bits[1])) & 1


def halves_of(v, layer, place, orders, where_ref):
    mine = side_of(where_ref, orders[place][0])
    return ((v[f"sent{place}", layer], 1 - mine), (v[f"kept{place}", layer], mine))


def ffn_weights_body(layer, orders, v, where_ref):
    nf_ref, dpre_ref, act_ref, low_ref = (v[n, layer] for n in ("nf", "dpre", "act", "low"))
    rows = D // 2
    for place in range(2):
        for out, half in halves_of(v, layer, place, orders, where_ref):
            if place == 0:
                left = nf_ref[:, pl.ds(pl.multiple_of(half * rows, rows), rows)]
                grads = dot_tn(left, dpre_ref[...]).astype(BF16)
                for j in range(2):
                    out[j] = grads[:, j * D : (j + 1) * D]
            else:
                for j in range(2):
                    left = act_ref[:, pl.ds(pl.multiple_of(j * D + half * rows, rows), rows)]
                    out[j] = dot_tn(left, low_ref[...]).astype(BF16)


def ffn_weights(vault, layer, orders):
    assert vault.arrays["act", layer].shape[1] == 2 * D
    shape = ((3, D // 2, D), BF16)
    chain_call(
        vault,
        functools.partial(ffn_weights_body, layer, orders),
        f"ffn_weights_{layer}",
        [],
        adds={(f"{n}{i}", layer): shape for i in range(2) for n in ("sent", "kept")},
        here=True,
        vmem=3,
    )


def attention_backward_body(
    layer, v, own_ref, other_ref, gain_ref, gain_grad_ref, *refs
):
    parts, (ds_ref, dkey_ref, dval_ref, dqt_ref) = refs[:PARTS], refs[PARTS:]
    grad_ref, mid_ref = v["grad", layer], v["middle", layer]
    wo_ref, wq_ref, wk_ref, wv_ref = (v[n, layer] for n in ("out", "query", "key", "value"))
    q_ref, k_ref, v_ref, p_ref, linv_ref = (v[n, layer] for n in ("q", "k", "v", "p", "linv"))
    mid_grad_ref, low_ref = v["mid_grad", layer], v["low_attn", layer]
    dq_ref, dk_ref, dv_ref = (v[n, layer] for n in ("dq", "dk", "dv"))
    incoming = own_ref[...].astype(F32) + other_ref[...].astype(F32)
    moved, gain_grad_ref[...] = norm_backward(mid_ref[...], gain_ref[layer : layer + 1], incoming)
    mid_grad = grad_ref[...] + moved
    mid_grad_ref[...] = mid_grad
    low_ref[...] = mid_grad.astype(BF16)
    heads = q_ref.shape[1] // HD
    mixed_turned = dot_nt(wo_ref[...], low_ref[...])
    spread = []
    for h in range(heads):
        spread.append(
            mixed_turned[h * HD : (h + 1) * HD]
            * jnp.concatenate(
                [linv_ref[b : b + 1, h * HALF : (h + 1) * HALF] for b in range(2)], axis=1
            )
        )
    dmixed = jnp.transpose(jnp.concatenate(spread, axis=0)).astype(BF16)
    queries = q_ref[...]
    key_turned = jnp.transpose(k_ref[...].astype(F32)).astype(BF16)
    for block in range(2):
        grads = heads_stacked(dmixed, block * HALF)
        stacked = heads_stacked(queries, block * HALF)
        first_key = 0 if block == 0 else MEM
        rows = KEYS_LOW if block == 0 else SEG
        first_row = 0 if block == 0 else KEYS_LOW
        inner = None
        dprobs = []
        for chunk in range(rows // HALF):
            key = first_key + chunk * HALF
            row = first_row + chunk * HALF
            dprob = dot_nt(v_ref[key : key + HALF], grads)
            dprobs.append(dprob)
            part = jnp.sum(p_ref[row : row + HALF].astype(F32) * dprob, axis=0, keepdims=True)
            inner = part if inner is None else inner + part
        inner = inner * linv_ref[block : block + 1]
        for chunk in range(rows // HALF):
            key = first_key + chunk * HALF
            row = first_row + chunk * HALF
            prob = p_ref[row : row + HALF]
            dscore = (prob.astype(F32) * (dprobs[chunk] - inner)).astype(BF16)
            ds_ref[chunk * HALF : (chunk + 1) * HALF] = dscore
            dkey = dot(dscore, stacked)
            dval = dot(prob, grads)
            if block == 1 and key < MEM + HALF:
                dkey = dkey + dkey_ref[key : key + HALF]
                dval = dval + dval_ref[key : key + HALF]
            dkey_ref[key : key + HALF] = dkey
            dval_ref[key : key + HALF] = dval
        for h in range(heads):
            dqt_ref[h * HD : (h + 1) * HD, block * HALF : (block + 1) * HALF] = dot(
                key_turned[h * HD : (h + 1) * HD, first_key : first_key + rows],
                ds_ref[:rows, h * HALF : (h + 1) * HALF],
            )
    dq_ref[...] = (jnp.transpose(dqt_ref[...]) * (1.0 / math.sqrt(HD))).astype(BF16)
    dk_ref[...] = dkey_ref[...].astype(BF16)
    dv_ref[...] = dval_ref[...].astype(BF16)
    step = SEG // PARTS
    for part_ref, row in zip(parts, range(0, SEG, step)):
        rows, seg_rows = pl.ds(row, step), pl.ds(MEM + row, step)
        part_ref[...] = (
            dot_nt(dk_ref[seg_rows], wk_ref[...])
            + dot_nt(dv_ref[seg_rows], wv_ref[...])
            + dot_nt(dq_ref[rows], wq_ref[...])
        ).astype(part_ref.dtype)


def attention_backward(vault, layer, own, other, gain):
    kept = vault.arrays
    q, k, val = kept["q", layer].shape, kept["k", layer].shape, kept["v", layer].shape
    width = q[1]
    heads = width // HD
    return chain_call(
        vault,
        functools.partial(attention_backward_body, layer),
        f"attention_backward_{layer}",
        [((1, D), F32)] + [((SEG // PARTS, D), BF16)] * PARTS,
        own,
        other,
        gain,
        adds={
            ("mid_grad", layer): ((SEG, D), F32),
            ("low_attn", layer): ((SEG, D), BF16),
            ("dq", layer): (q, BF16),
            ("dk", layer): (k, BF16),
            ("dv", layer): (val, BF16),
        },
        scratch=[
            pltpu.VMEM((KEYS_LOW, heads * HALF), BF16),
            pltpu.VMEM(k, F32),
            pltpu.VMEM(val, F32),
            pltpu.VMEM((width, SEG), F32),
        ],
        vmem=7,
    )


def attention_weights_body(layer, orders, v, where_ref, part_ref):
    nm_ref, dq_ref, dk_ref, dv_ref, mt_ref, low_ref = (
        v[n, layer] for n in ("nm", "dq", "dk", "dv", "mt", "low_attn")
    )
    width = dq_ref.shape[1]
    rows = D // 2
    for out, half in halves_of(v, layer, 0, orders, where_ref):
        cols = pl.ds(pl.multiple_of(half * rows, rows), rows)
        out[2, :, :width] = dot_tn(nm_ref[MEM:, cols], dq_ref[...]).astype(BF16)
        out[2, :, width:] = dot_tn(nm_ref[:, cols], dk_ref[...]).astype(BF16)
    for out, half in halves_of(v, layer, 1, orders, where_ref):

        @pl.when(half == 0)
        def _():
            for part in range(2):
                out[2, :, part * width : (part + 1) * width] = dot_tn(
                    nm_ref[:, part * rows : (part + 1) * rows], dv_ref[...]
                ).astype(BF16)

        @pl.when(half == 1)
        def _():
            out[2] = dot(mt_ref[...], low_ref[...]).astype(BF16)

    part_ref[...] = (dot_nt(dk_ref[:MEM], v["key", layer][...]) + dot_nt(dv_ref[:MEM], v["value", layer][...])).astype(
        part_ref.dtype
    )


def attention_weights(vault, layer, orders):
    width = vault.arrays["dq", layer].shape[1]
    assert D == 2 * width
    return chain_call(
        vault,
        functools.partial(attention_weights_body, layer, orders),
        f"attention_weights_{layer}",
        [((MEM, D), BF16)],
        here=True,
        vmem=4,
    )[0]


def finish_body(v, where_ref, *refs):
    own_ref, other_ref, part_ref, part_other, gain_ref, gain_attn_1, gain_ffn_0, gain_ffn_1, gate_own, gate_other = refs[:10]
    rest = refs[10 : 10 + 2 * LAYERS]
    out_ref, grad_ref, mem_grad_out, small_ref, mem_grad_ref, semaphores = refs[10 + 2 * LAYERS :]
    copies = []
    core = where_ref[1]
    out_ref[pl.ds(pl.multiple_of(core * HALF, HALF), HALF), :] = own_ref[...]
    out_ref[pl.ds(pl.multiple_of((1 - core) * HALF, HALF), HALF), :] = other_ref[...]
    send(out_ref)
    incoming = part_ref[...].astype(F32) + part_other[...].astype(F32)
    moved, gain_part = norm_backward(v["x"][...].astype(F32), gain_ref[:1], incoming)
    grad_ref[...] = v["mid_grad", 0][...] + moved
    send(grad_ref)
    small_ref[...] = jnp.zeros_like(small_ref)
    for i, row in enumerate((gain_ffn_0[...], gain_ffn_1[...], gate_own[...] + gate_other[...])):
        small_ref[LAYERS + i : LAYERS + i + 1] = row
    for l in range(LAYERS):
        own, other = rest[2 * l : 2 * l + 2]
        incoming = own[...].astype(F32) + other[...].astype(F32)
        mem_grad_ref[l], gain_mem = norm_backward(v["memory", l][...].astype(F32), gain_ref[l : l + 1], incoming)
        small_ref[l : l + 1] = gain_mem + (gain_part if l == 0 else gain_attn_1[...])
        copies.append(pltpu.make_async_copy(mem_grad_ref.at[l], mem_grad_out.at[l], semaphores.at[l]))
        copies[-1].start()
    for copy in copies:
        copy.wait()


def finish_rows(vault, *operands):
    return chain_call(
        vault,
        finish_body,
        "finish_rows",
        [((SEG, D), F32, HBM), ((SEG, D), F32, HBM), ((LAYERS, MEM, D), F32, RAW), ((8, D), F32)],
        *operands,
        scratch=[pltpu.VMEM((LAYERS, MEM, D), F32), pltpu.SemaphoreType.DMA((LAYERS,))],
        here=True,
        vmem=8,
    )


def other_core(values):
    return lax.ppermute(values, "mp", [(0, 1), (1, 0)])


def other_core_split(parts):
    return Split([other_core(part) for part in parts])


def tie_split(split, *values):
    held = tie(*split.parts, *values)
    return (Split(list(held[: len(split.parts)])),) + tuple(held[len(split.parts) :])


def partner(values, bits):
    size = lax.axis_size("dp")
    pairs = [(2 * i + core, 2 * (i ^ (1 << bits[core])) + core) for i in range(size) for core in range(2)]
    return lax.ppermute(values, ("dp", "mp"), pairs)


def add_low(left, right):
    return (left.astype(F32) + right.astype(F32)).astype(BF16)


def fold_body(kept_name, bit, v, where_ref, *refs):
    come, out = refs[0], refs[-1]
    kept = v[kept_name]
    if bit is not None:
        half = come.shape[1] // 2
        mine = side_of(where_ref, bit)
        other, own = pl.ds((1 - mine) * half, half), pl.ds(mine * half, half)
        out[...] = add_low(kept[:, other], come[:, other])
        kept[:, :half] = add_low(kept[:, own], come[:, own])
        return
    total = add_low(kept[:, :1], come[...])
    if len(refs) == 2:
        out[...] = total
        return
    small = refs[1]
    rows, cols = kept.shape[2:]
    out[...] = jnp.zeros(out.shape, BF16)
    out[:, :, :, :cols] = total
    wide = D // 128
    for j in range(SMALL * wide):
        lane = cols + j // rows * 128
        out[0, 0, j % rows : j % rows + 1, lane : lane + 128] = small[
            j // wide : j // wide + 1, j % wide * 128 : (j % wide + 1) * 128
        ].astype(BF16)


def small_lanes(rows):
    return -(-SMALL * (D // 128) // rows) * 128


def fold(vault, name, kept_name, bit, come, small):
    kinds, pieces, rows, cols = come.shape
    if small is not None:
        cols += small_lanes(rows)
    return chain_call(
        vault,
        functools.partial(fold_body, kept_name, bit),
        name,
        [((kinds, 1 if bit is None else pieces // 2, rows, cols), BF16)],
        come,
        *([] if small is None else [small]),
        here=True,
        vmem=4,
        flops=SUM_FLOPS,
    )[0]


def join_body(bit, where_ref, mine_ref, other_ref, out_ref):
    pieces = mine_ref.shape[1]
    mine = side_of(where_ref, bit)
    out_ref[:, pl.ds(mine * pieces, pieces)] = mine_ref[...]
    out_ref[:, pl.ds((1 - mine) * pieces, pieces)] = other_ref[...]


def join(name, bit, mine, other):
    kinds, pieces, rows, cols = mine.shape
    return kernel_call(
        functools.partial(join_body, bit),
        name,
        [((kinds, 2 * pieces, rows, cols), BF16)],
        mine,
        other,
        here=True,
        vmem=4,
        flops=SUM_FLOPS,
    )[0]


def place_body(place, layer, bit, turned, fresh, small, where_ref, ref, *refs):
    if small:
        mine_ref, refs = refs[0], refs[1:]
    refs = refs if fresh else refs[3:]
    outs, refs = refs[:3], refs[3:]
    if small:
        small_ref, refs = refs[0], refs[1:]
    buffers, semaphores = refs[:3], refs[3]
    side = side_of(where_ref, bit) ^ turned
    pieces = ref.shape[1]
    width = D // 2
    at = pl.ds(side * pieces, pieces)
    copies = []

    def put(buffer, target, number):
        copy = pltpu.make_async_copy(buffer, target, semaphores.at[number])
        copy.start()
        return copy

    if place == 0:
        up, q, k = buffers
        for j in range(2):
            up[:, :, j * D : (j + 1) * D] = ref[j, :, :, :D].astype(F32)
        copies.append(put(up, outs[0].at[layer, at], 0))
        q[...] = ref[2, :, :, :width].astype(F32)
        copies.append(put(q, outs[1].at[layer, at], 1))
        k[...] = ref[2, :, :, width:D].astype(F32)
        copies.append(put(k, outs[2].at[layer, at], 2))
    else:
        down, val, out = buffers
        for j in range(2):
            down[j] = ref[j, :, :, :D].astype(F32)
            copies.append(put(down.at[j], outs[0].at[layer, j, at], j))

        @pl.when(side == 0)
        def _():
            for j in range(2):
                val[j] = ref[2, :, :, j * width : (j + 1) * width].astype(F32)
            put(val, outs[1].at[layer], 2).wait()

        @pl.when(side == 1)
        def _():
            out[...] = ref[2, :, :, :D].astype(F32)
            put(out, outs[2].at[layer], 2).wait()

    if small:
        rows, wide = ref.shape[2], D // 128
        total = jnp.sum(ref[0, :, :, D:].astype(F32), axis=0) + jnp.sum(mine_ref[0, :, :, D:].astype(F32), axis=0)
        for j in range(SMALL * wide):
            lane = j // rows * 128
            small_ref[j // wide : j // wide + 1, j % wide * 128 : (j % wide + 1) * 128] = total[
                j % rows : j % rows + 1, lane : lane + 128
            ]
    for copy in copies:
        copy.wait()


def place(place_index, layer, bit, turned, values, mine, totals):
    kinds, pieces, rows, cols = values.shape
    small = turned == 1 and cols > D
    if place_index == 0:
        shapes = [(2 * pieces, rows, 2 * D), (2 * pieces, rows, D // 2), (2 * pieces, rows, D // 2)]
        held = [(pieces, rows, 2 * D), (pieces, rows, D // 2), (pieces, rows, D // 2)]
    else:
        shapes = [(2, 2 * pieces, rows, D), (2, pieces, rows, D // 2), (pieces, rows, D)]
        held = [(2, pieces, rows, D), (2, pieces, rows, D // 2), (pieces, rows, D)]
    first = 2 if small else 1
    return kernel_call(
        functools.partial(place_body, place_index, layer, bit, turned, totals is None, small),
        f"place{place_index}_{layer}_{'other' if turned else 'mine'}",
        [((LAYERS,) + shape, F32, RAW) for shape in shapes] + ([((8, D), F32)] if small else []),
        values,
        *([mine] if small else []),
        *([] if totals is None else [Slow(t, RAW) for t in totals]),
        here=True,
        scratch=[pltpu.VMEM(shape, F32) for shape in held] + [pltpu.SemaphoreType.DMA((3,))],
        aliases=None if totals is None else {first + i: i for i in range(3)},
        vmem=6,
        flops=SUM_FLOPS,
    )


def in_pieces(values, size):
    kinds, rows, cols = values.shape
    return values.reshape(kinds, size // 2, 2 * rows // size, cols)


def tie(*values):
    return lax.optimization_barrier(values)


class Stream:
    def __init__(self, vault, layer, place_index, order, sent):
        self.vault, self.layer, self.place, self.order = vault, layer, place_index, order
        self.come = partner(sent, order[0])
        self.pieces = None
        self.step = 0

    def advance(self, after, small=None):
        steps = len(self.order)
        self.step += 1
        s = self.step
        name = f"sum{self.place}_{self.layer}_step{s}"
        kept_name = (f"kept{self.place}", self.layer)
        if s <= steps:
            come, after = tie(self.come, after)
            bit = None if s == steps else self.order[s]
            out = fold(self.vault, name, kept_name, bit, come, small if s == steps else None)
            at = min(s, steps - 1)
            if s == steps:
                self.vault.drop(kept_name)
        else:
            at = 2 * steps - s - 1
            come, after = tie(self.come, after)
            out = join(name, self.order[at + 1], self.pieces, come)
        if s >= steps:
            self.pieces = out
        self.come = partner(out, self.order[at])
        return out

    def settle(self, turned, totals, after):
        values, after = tie(self.come if turned else self.pieces, after)
        return place(self.place, self.layer, self.order[0], turned, values, self.pieces, totals)


def local(
    layer_input, memory, doc_lengths, neighbour_owner, neighbour_row, table, gain_attn, w_query, w_key, w_value,
    w_out, gain_ffn, w_up, w_down, w_gate, cotangent,
):
    size = lax.axis_size("dp")
    bits_count = size.bit_length() - 1
    rest = list(range(3, bits_count))
    plans = (
        (((2, 0, 1), (0, 1, 2)), ((2, 0, 1), (1, 2, 0))),
        (((0, 1, 2), (2, 0, 1)), ((2, 1, 0), (1, 0, 2))),
    )
    orders = tuple(tuple(list(zip(*plan)) + [(bit, bit) for bit in rest] for plan in pair) for pair in plans)
    x = layer_input[0]

    half = size // 2
    turned = half == 8
    far_own = partner(own_rows(table), (bits_count - 1, bits_count - 1))
    wanted, ranks = build_requests(neighbour_owner[0].T, neighbour_row[0].T, size, turned)
    capacity = wanted.shape[2] // 2
    halves = [list(range(half)), list(range(half, size))]

    def exchange(values):
        return lax.all_to_all(values, "dp", split_axis=0, concat_axis=0, tiled=True, axis_index_groups=halves)

    asked, x = tie(exchange(wanted), x)
    vault = Vault()
    stacks = (w_query, w_key, w_value, w_out, w_up, w_down, memory[:, 0], x, cotangent[0], table)
    names = ("query", "key", "value", "out", "up", "down", "memory")
    sources = [("x", 7, None)] + [((n, l), i, l) for l in range(LAYERS) for i, n in enumerate(names)] + [("cot", 8, None), ("table", 9, None)]
    load(vault, stacks, sources)
    parts = ()
    for l in range(LAYERS):
        part = attention_forward(vault, l, doc_lengths, parts, gain_attn)
        if l == 0:
            part, asked, far_own = tie(part, asked, far_own)
            answer_requests(vault, 0, asked, (), turned)
            answer_requests(vault, 1, asked, (far_own, other_core(far_own)), turned)
            vault.drop("table")
            answers = [vault.arrays.pop(("rows", j)) for j in range(len(MASKS) if turned else 1)]
            part, *answers = tie(part, *answers)
            if turned:
                near = [
                    lax.ppermute(a, ("dp", "mp"), [(2 * i + c, 2 * (i ^ m[c]) + c) for i in range(size) for c in range(2)])
                    for a, m in zip(answers, MASKS)
                ]
        if l == 1 and turned:
            part, *near[:3] = tie(part, *near[:3])
        ffn_part = ffn_forward(vault, l, part, other_core(part), gain_ffn)
        if l == 1 and turned:
            ffn_part, near[3] = tie(ffn_part, near[3])
        parts = (ffn_part, other_core(ffn_part))
    if not turned:
        near = [exchange(answers[0]).reshape(-1, D)]
    near = near + [other_core(a) for a in near]

    final, grad, gate_part = retrieval(vault, *parts, w_gate[None], Slow(ranks), near, capacity, size)
    vault.drop("cot")
    incoming = (grad, other_core(grad))
    memory_parts = []
    gain_attn_1 = None
    gains_ffn = [None] * LAYERS
    streams = {}
    for l in range(LAYERS - 1, -1, -1):
        part = ffn_backward(vault, l, incoming)
        if l < LAYERS - 1:
            gain_attn_1, *part = part
            vault.drop(("hidden", l + 1), ("mid_grad", l + 1))
        vault.drop(("slope", l))
        part_other = other_core_split(part)
        ffn_weights(vault, l, orders[l])
        vault.drop(*((n, l) for n in ("nf", "dpre", "act", "low", "up", "down")))
        gains_ffn[l], *part = attention_backward(vault, l, Split(part), part_other, gain_ffn)
        vault.drop(*((n, l) for n in ("q", "k", "v", "p", "linv", "grad", "middle", "out", "query")))
        part_other = other_core_split(part)
        mem_part = attention_weights(vault, l, orders[l])
        vault.drop(*((n, l) for n in ("nm", "dq", "dk", "dv", "mt", "low_attn", "key", "value")))
        for i in range(2):
            vault.arrays[f"kept{i}", l] = in_pieces(vault.arrays[f"kept{i}", l], size)
            sent = in_pieces(vault.arrays.pop((f"sent{i}", l)), size)
            streams[l, i] = Stream(vault, l, i, orders[l][i], sent)
        part_other, mem_part = tie_split(part_other, mem_part)
        memory_parts = [mem_part, other_core(mem_part)] + memory_parts
        incoming = (Split(part), part_other, gain_attn)
    last = 2 * bits_count - 1
    lag = {(1, 1): 0.29, (1, 0): 0.11, (0, 0): 2.33, (0, 1): 2.18}
    events = sorted((s + lag[key], key) for key in streams for s in range(1, last + 1))
    after, small = mem_part, None
    totals = [None, None]

    def settle(key, turned, after):
        result = streams[key].settle(turned, totals[key[1]], after)
        totals[key[1]] = result[:3]
        return result

    ended = []
    for count, (_, key) in enumerate(events):
        if count == 2:
            gate_part, final, after = tie(gate_part, final, after)
            layer_output, input_grad, memory_grad, small = finish_rows(
                vault, final, other_core(final), *incoming[:2], gain_attn, gain_attn_1, *gains_ffn,
                gate_part, other_core(gate_part), *memory_parts,
            )
            vault.drop("x", ("mid_grad", 0), *(("memory", l) for l in range(LAYERS)))
            after = small
        stream = streams[key]
        after = stream.advance(after, small if key == (1, 1) else None)
        if stream.step == last:
            after = settle(key, 0, after)[0]
            ended.append(key)
    for key in ended:
        result = settle(key, 1, after)
        after = result[0]
        if len(result) > 3:
            small = result[3]
    (up, wq, wk), (down, wv, wo) = totals
    up = up.reshape(LAYERS, D, -1)
    down = down.reshape(LAYERS, -1, D)
    width = wq.shape[-1]
    return (
        layer_output[None],
        input_grad[None],
        memory_grad[:, None],
        small[:LAYERS],
        wq.reshape(LAYERS, D, width),
        wk.reshape(LAYERS, D, width),
        wv.reshape(LAYERS, D, width),
        wo.reshape(LAYERS, width, D),
        small[LAYERS : 2 * LAYERS],
        up,
        down,
        small[2 * LAYERS],
    )


def solution(mesh):
    return jax.shard_map(
        local,
        mesh=mesh,
        in_specs=(
            P("dp", None, None),
            P(None, "dp", None, None),
            P("dp", None),
            P("dp", None, None),
            P("dp", None, None),
            P("dp", None),
            P(),
            P(None, None, "mp"),
            P(None, None, "mp"),
            P(None, None, "mp"),
            P(None, "mp", None),
            P(),
            P(None, None, "mp"),
            P(None, "mp", None),
            P(),
            P("dp", None, None),
        ),
        out_specs=(
            P("dp", None, None),
            P("dp", None, None),
            P(None, "dp", None, None),
            P(),
            P(None, None, "mp"),
            P(None, None, "mp"),
            P(None, None, "mp"),
            P(None, "mp", None),
            P(),
            P(None, None, "mp"),
            P(None, "mp", None),
            P(),
        ),
        check_vma=False,
    )
```
